32 devices in a mesh: fsdp: 8 (over y, x, core), ctx: 2 (over z_hi), tp: 2 (over z_lo).
Axes of the slice: x: 2, y: 2, z: 4 (z_hi: 2, z_lo: 2; z = z_hi * 2 + z_lo), core: 2. Of those that a mesh axis runs over, the one named last changes fastest.
Arguments:
- tokens: bfloat16 [8, 320, 1024], P('fsdp', 'ctx'), may hold values from -6 to 6
- lengths: int32 [8], P('fsdp'), may hold values from 0 to 320, as said below
- cotangent: bfloat16 [8, 320, 1024], P('fsdp', 'ctx'), may hold values from -6 to 6
- attn_gain: bfloat16 [3, 1024], P(None, ('fsdp', 'ctx')), may hold values from 0.5 to 1.5
- attn_shift: bfloat16 [3, 1024], P(None, ('fsdp', 'ctx')), may hold values from -1.75 to 1.75
- qkv_weight: bfloat16 [3, 1024, 3, 1024], P(None, ('fsdp', 'ctx'), None, 'tp'), may hold values from -0.1875 to 0.1875
- qv_bias: bfloat16 [3, 2, 1024], P(None, None, 'tp'), may hold values from -3 to 3
- out_weight: bfloat16 [3, 1024, 1024], P(None, 'tp', ('fsdp', 'ctx')), may hold values from -0.1875 to 0.1875
- out_bias: bfloat16 [3, 1024], P(None, ('fsdp', 'ctx')), may hold values from -1.75 to 1.75
- mlp_gain: bfloat16 [3, 1024], P(None, ('fsdp', 'ctx')), may hold values from 0.5 to 1.5
- mlp_shift: bfloat16 [3, 1024], P(None, ('fsdp', 'ctx')), may hold values from -1.75 to 1.75
- up_weight: bfloat16 [3, 1024, 4096], P(None, ('fsdp', 'ctx'), 'tp'), may hold values from -0.1875 to 0.1875
- up_bias: bfloat16 [3, 4096], P(None, 'tp'), may hold values from -3 to 3
- down_weight: bfloat16 [3, 4096, 1024], P(None, 'tp', ('fsdp', 'ctx')), may hold values from -0.09375 to 0.09375
- down_bias: bfloat16 [3, 1024], P(None, ('fsdp', 'ctx')), may hold values from -1.75 to 1.75
Outputs:
- output: bfloat16 [8, 320, 1024], P('fsdp', 'ctx')
- input_grad: float32 [8, 320, 1024], P('fsdp', 'ctx')
- grad_attn_gain: float32 [3, 1024], P(None, ('fsdp', 'ctx'))
- grad_attn_shift: float32 [3, 1024], P(None, ('fsdp', 'ctx'))
- grad_qkv_weight: float32 [3, 1024, 3, 1024], P(None, ('fsdp', 'ctx'), None, 'tp')
- grad_qv_bias: float32 [3, 2, 1024], P(None, None, 'tp')
- grad_out_weight: float32 [3, 1024, 1024], P(None, 'tp', ('fsdp', 'ctx'))
- grad_out_bias: float32 [3, 1024], P(None, ('fsdp', 'ctx'))
- grad_mlp_gain: float32 [3, 1024], P(None, ('fsdp', 'ctx'))
- grad_mlp_shift: float32 [3, 1024], P(None, ('fsdp', 'ctx'))
- grad_up_weight: float32 [3, 1024, 4096], P(None, ('fsdp', 'ctx'), 'tp')
- grad_up_bias: float32 [3, 4096], P(None, 'tp')
- grad_down_weight: float32 [3, 4096, 1024], P(None, 'tp', ('fsdp', 'ctx'))
- grad_down_bias: float32 [3, 1024], P(None, ('fsdp', 'ctx'))
The draws below stay inside these ranges and needn't reach their ends.
Inputs may be any that keep to these rules, and one draw needn't show every extreme that they name: `lengths`: image places 1 * g to 1 * g + 1 - 1 form group g; in each group the first 1 to 1 places hold live images of length 224 to 320, the others have length 0; some image has length 320 and some group is full.
All inputs are finite; a program needn't handle non-finite values.
Results may differ from the reference program's by a relative error of at most 0.012.
Values may be sent and summed in bfloat16 or wider, within the bound.
A program may use at most 256 MiB of HBM per device.

```python
import jax
import jax.numpy as jnp
from jax import lax

D = 1024
HEADS = 16
HEAD_DIM = 64
FF = 4096
LAYERS = 3
SLOTS = 320
LEN_MIN = 224
CAP = 1
IMG_SLOTS = 8


def draw_lengths(key, part):
    groups = IMG_SLOTS // CAP
    count_key, group_key, size_key = jax.random.split(jax.random.fold_in(key, 11), 3)
    counts = jax.random.randint(count_key, (groups,), 1, CAP + 1)
    fullest = jax.random.randint(group_key, (), 0, groups)
    group_ids = jnp.arange(groups)
    counts = jnp.where(group_ids == fullest, CAP, counts)
    drawn_sizes = jax.random.randint(size_key, (groups, CAP), LEN_MIN, SLOTS + 1)
    place_ids = jnp.arange(CAP)
    longest = (group_ids[:, None] == fullest) & (place_ids[None, :] == 0)
    drawn_sizes = jnp.where(longest, SLOTS, drawn_sizes)
    live_slots = place_ids[None, :] < counts[:, None]
    return jnp.where(live_slots, drawn_sizes, 0).reshape(IMG_SLOTS).astype(jnp.int32)


def steps_of(own_key, extent, shards, least, largest):
    gain, own = 1.0, jax.random.fold_in(own_key, 6)
    for axis_at, shards_of in shards:
        heights = jnp.exp(jax.random.uniform(jax.random.fold_in(own, axis_at), (shards_of,), jnp.float32, least / len(shards), largest / len(shards)))
        gain = gain * jnp.repeat(heights, extent[axis_at] // shards_of).reshape([-1 if axis == axis_at else 1 for axis in range(len(extent))])
    return gain


def centred(stream_key, shape, scale, most, shards=(), held_as=jnp.bfloat16):
    entries = jax.random.normal(stream_key, shape, jnp.float32) * scale
    if len(shards) > 0:
        entries = steps_of(stream_key, shape, shards, -0.22, 0.18) * entries
    return jnp.clip(entries, min=-most, max=most).astype(held_as)


def setup_inputs(seed: int = 0) -> dict:
    streams_of = jax.random.split(jax.random.key(seed), 16)
    return {
        "tokens": centred(streams_of[0], (IMG_SLOTS, SLOTS, D), 1.0, 6.0, ((0, 8), (1, 2))),
        "lengths": draw_lengths(jax.random.fold_in(streams_of[15], 71), 0),
        "cotangent": centred(streams_of[2], (IMG_SLOTS, SLOTS, D), 1.0, 6.0, ((0, 8), (1, 2))),
        "attn_gain": jnp.clip(1.0 + 0.1 * jax.random.normal(streams_of[3], (LAYERS, D), jnp.float32), 0.5, 1.5).astype(jnp.bfloat16),
        "attn_shift": centred(streams_of[4], (LAYERS, D), 0.3, 1.75, ((1, 16),)),
        "qkv_weight": centred(streams_of[5], (LAYERS, D, 3, D), D ** -0.5, 0.1875, ((1, 16), (3, 2))),
        "qv_bias": centred(streams_of[6], (LAYERS, 2, D), 0.5, 3.0, ((2, 2),)),
        "out_weight": centred(streams_of[7], (LAYERS, D, D), D ** -0.5, 0.1875, ((1, 2), (2, 16))),
        "out_bias": centred(streams_of[8], (LAYERS, D), 0.3, 1.75, ((1, 16),)),
        "mlp_gain": jnp.clip(1.0 + 0.1 * jax.random.normal(streams_of[9], (LAYERS, D), jnp.float32), 0.5, 1.5).astype(jnp.bfloat16),
        "mlp_shift": centred(streams_of[10], (LAYERS, D), 0.3, 1.75, ((1, 16),)),
        "up_weight": centred(streams_of[11], (LAYERS, D, FF), D ** -0.5, 0.1875, ((1, 16), (2, 2))),
        "up_bias": centred(streams_of[12], (LAYERS, FF), 0.5, 3.0, ((1, 2),)),
        "down_weight": centred(streams_of[13], (LAYERS, FF, D), FF ** -0.5, 0.09375, ((1, 2), (2, 16))),
        "down_bias": centred(streams_of[14], (LAYERS, D), 0.3, 1.75, ((1, 16),)),
    }


EPS = 1e-05
NEG = -30000.0
HIGH = lax.Precision.HIGHEST

@jax.custom_vjp
def low(v):
    return lax.optimization_barrier(v.astype(jnp.bfloat16)).astype(jnp.float32)

@jax.custom_vjp
def low_back(v):
    return v

def low_keep(v):
    return (low(v), None)

def low_pass(kept, grad):
    return (grad,)

def back_keep(v):
    return (v, None)

def back_low(kept, grad):
    return (low(grad),)
low.defvjp(low_keep, low_pass)
low_back.defvjp(back_keep, back_low)

def rounded_both(value):
    return low(low_back(value))

def layer_norm(values, norm_gain, norm_shift):
    row_mean = lax.optimization_barrier(jnp.mean(values, axis=-1, keepdims=True))
    centered = values - row_mean
    row_var = lax.optimization_barrier(jnp.mean(centered * centered, axis=-1, keepdims=True))
    return centered * lax.rsqrt(row_var + EPS) * norm_gain + norm_shift

def attend(image_item):
    queries, key_heads, values, length = image_item
    raw_scores = jnp.einsum('qhd,khd->hqk', queries, key_heads, precision=HIGH) * HEAD_DIM ** (-0.5)
    raw_scores = low_back(raw_scores)
    key_live = jnp.arange(SLOTS)[None, None, :] < length
    scores = jnp.where(key_live, raw_scores, NEG)
    row_top = lax.optimization_barrier(jnp.max(scores, axis=-1, keepdims=True))
    exp_scores = jnp.exp(scores - row_top)
    attn_probs = low(exp_scores / lax.optimization_barrier(jnp.sum(exp_scores, axis=-1, keepdims=True)))
    return jnp.einsum('hqk,khd->qhd', attn_probs, values, precision=HIGH)

def layer(stream, row_mask, lengths, gain_a, shift_a, qkv_w, qv_b, out_w, out_b, gain_b, shift_b, up_w, up_b, down_w, down_b):
    images = stream.shape[0]
    normed_a = low(layer_norm(stream, gain_a, shift_a))
    projected = jnp.einsum('nsd,dtf->nstf', normed_a, qkv_w, precision=HIGH)
    queries = rounded_both(projected[:, :, 0] + qv_b[0])
    key_rows = rounded_both(projected[:, :, 1])
    values = rounded_both(projected[:, :, 2] + qv_b[1])
    head_shape = (images, SLOTS, HEADS, HEAD_DIM)
    attended = lax.map(jax.checkpoint(attend), (queries.reshape(head_shape), key_rows.reshape(head_shape), values.reshape(head_shape), lengths))
    attended = rounded_both(attended.reshape(images, SLOTS, D))
    branch_a = low_back(jnp.einsum('nsf,fd->nsd', attended, out_w, precision=HIGH))
    mid = stream + row_mask * (branch_a + out_b)
    normed_b = low(layer_norm(mid, gain_b, shift_b))
    hidden_pre = low_back(jnp.einsum('nsd,df->nsf', normed_b, up_w, precision=HIGH)) + up_b
    hidden = low(jax.nn.gelu(hidden_pre, approximate=False))
    branch_b = low_back(jnp.einsum('nsf,fd->nsd', hidden, down_w, precision=HIGH))
    return mid + row_mask * (branch_b + down_b)

def reference(tokens, lengths, cotangent, attn_gain, attn_shift, qkv_weight, qv_bias, out_weight, out_bias, mlp_gain, mlp_shift, up_weight, up_bias, down_weight, down_bias):
    row_mask = (jnp.arange(SLOTS)[None, :] < lengths[:, None]).astype(jnp.float32)[:, :, None]
    params = tuple((p.astype(jnp.float32) for p in (attn_gain, attn_shift, qkv_weight, qv_bias, out_weight, out_bias, mlp_gain, mlp_shift, up_weight, up_bias, down_weight, down_bias)))

    def forward(start, weights):
        stream = row_mask * start
        for layer_index in range(LAYERS):
            stream = layer(stream, row_mask, lengths, *[w[layer_index] for w in weights])
        return stream
    result, pull_back = jax.vjp(forward, tokens.astype(jnp.float32), params)
    grad_input, grad_params = pull_back(cotangent.astype(jnp.float32))
    return (result.astype(jnp.bfloat16), grad_input, grad_params[0], grad_params[1], grad_params[2], grad_params[3], grad_params[4], grad_params[5], grad_params[6], grad_params[7], grad_params[8], grad_params[9], grad_params[10], grad_params[11])
```

```python
import functools

import jax
import jax.numpy as jnp
from jax import lax
from jax.experimental import pallas as pl
from jax.experimental.pallas import tpu as pltpu
from jax.sharding import PartitionSpec as P

HEAD_DIM = 64
EPS = 1e-05
NEG = -30000.0
MESH = pl.DeviceIdType.MESH
PARTS = 6
BF16 = jnp.bfloat16
F32 = jnp.float32


def flip(index, bit):
    size = 2**bit
    return index + size - 2 * size * ((index // size) % 2)


def flip_all(index, bits):
    for bit in bits:
        index = flip(index, bit)
    return index


def subsets(bits):
    found = [()]
    for bit in bits:
        found = found + [entry + (bit,) for entry in found]
    return found


def orders(fsdp_size):
    top = fsdp_size.bit_length() - 1
    bits = list(range(1, top))
    half = len(bits) // 2
    return bits, bits[half:] + bits[:half]


class Link:
    def __init__(self, send_sem, recv_sem):
        self.send_sem, self.recv_sem, self.used, self.sent = send_sem, recv_sem, 0, []

    def push(self, src, dst, device):
        at = self.used
        self.used += 1
        copy = pltpu.make_async_remote_copy(
            src_ref=src,
            dst_ref=dst,
            send_sem=self.send_sem.at[at],
            recv_sem=self.recv_sem.at[at],
            device_id=device,
            device_id_type=MESH,
        )
        copy.start()
        self.sent.append(copy)
        return copy

    def drain(self):
        for copy in self.sent:
            copy.wait_send()
        self.sent = []


def greet(fsdp_size, ctx_size, with_tp):
    me, ctx, tp = lax.axis_index("fsdp"), lax.axis_index("ctx"), lax.axis_index("tp")
    barrier = pltpu.get_barrier_semaphore()
    count = 0
    for bit in range(fsdp_size.bit_length() - 1):
        pl.semaphore_signal(
            barrier, inc=1, device_id={"fsdp": flip(me, bit)}, device_id_type=MESH
        )
        count += 1
    if ctx_size > 1:
        pl.semaphore_signal(barrier, inc=1, device_id={"ctx": 1 - ctx}, device_id_type=MESH)
        count += 1
    if with_tp:
        pl.semaphore_signal(barrier, inc=1, device_id={"tp": 1 - tp}, device_id_type=MESH)
        count += 1
    pl.semaphore_wait(barrier, count)


def rows_of(start, rows):
    return pl.ds(pl.multiple_of(start * rows, rows), rows)


def gather_pushes(fsdp_size, ctx_size):
    steps = fsdp_size.bit_length() - 2
    return (ctx_size - 1) + ctx_size * (2**steps - 1) + 2**steps


class Gather:
    def __init__(self, link, ctx_size, own, whole, block, order, local_sem):
        self.link, self.own, self.whole, self.block, self.order = link, own, whole, block, order
        self.ctx_size = ctx_size
        self.me, self.ctx = lax.axis_index("fsdp"), lax.axis_index("ctx")
        self.waits = {}
        self.stay = pltpu.make_async_copy(own, self.rows(self.me, self.ctx), local_sem)

    def rows(self, fsdp, ctx):
        return self.whole.at[rows_of(fsdp * self.ctx_size + ctx, self.block)]

    def spread(self, stream, step):
        ctx = self.ctx if stream == 0 else 1 - self.ctx
        bit = self.order[step]
        to = {"fsdp": flip(self.me, bit)}
        copies = []
        for entry in subsets(self.order[:step]):
            place = self.rows(flip_all(self.me, entry), ctx)
            source = self.own if (stream == 0 and not entry) else place
            copies.append(self.link.push(source, place, to))
        self.waits[stream, step] = copies

    def arrive(self, *key):
        for copy in self.waits.pop(key):
            copy.wait_recv()

    def start(self):
        self.stay.start()
        if self.ctx_size > 1:
            self.waits["ctx",] = [
                self.link.push(self.own, self.rows(self.me, self.ctx), {"ctx": 1 - self.ctx})
            ]
        self.spread(0, 0)

    def next_step(self, stream, step):
        self.arrive(stream, step - 1)
        self.spread(stream, step)

    def other(self):
        self.arrive("ctx")
        self.spread(1, 0)

    def core(self):
        last = len(self.order) - 1
        for stream in range(self.ctx_size):
            self.arrive(stream, last)
        self.stay.wait()
        both = self.block * self.ctx_size
        copies = []
        for entry in subsets(self.order):
            place = self.whole.at[rows_of(flip_all(self.me, entry), both)]
            copies.append(self.link.push(place, place, {"fsdp": flip(self.me, 0)}))
        self.waits["core",] = copies

    def finish(self):
        self.arrive("core")

    def events(self):
        found = [self.start]
        for step in range(1, len(self.order)):
            found.append(functools.partial(self.next_step, 0, step))
        if self.ctx_size > 1:
            found.append(self.other)
            for step in range(1, len(self.order)):
                found.append(functools.partial(self.next_step, 1, step))
        return found + [self.core, self.finish]


def skewed(groups, skew):
    timed = []
    for at, events in enumerate(groups):
        for place, event in enumerate(events):
            timed.append((0 if place == 0 else place + at * skew, at, place, event))
    return [entry[3] for entry in sorted(timed, key=lambda entry: entry[:3])]


def in_step(first, second):
    def run(one, two):
        one()
        two()

    return [functools.partial(run, one, two) for one, two in zip(first, second)]


def gather_kernel(ctx_size, fsdp_size, with_small, *refs):
    if with_small:
        own_ref, small_ref, whole_ref, small_whole, send_sem, recv_sem, local_sem = refs
    else:
        own_ref, whole_ref, send_sem, recv_sem, local_sem = refs
    greet(fsdp_size, ctx_size, False)
    link = Link(send_sem, recv_sem)
    both = orders(fsdp_size)
    groups = []
    if with_small:
        groups.append(
            Gather(
                link, ctx_size, small_ref, small_whole, small_ref.shape[0], both[0], local_sem.at[PARTS]
            ).events()
        )
    for pair in range(PARTS // 2):
        groups.append(
            in_step(
                *[
                    Gather(
                        link,
                        ctx_size,
                        own_ref.at[part],
                        whole_ref.at[part],
                        own_ref.shape[1],
                        both[part % 2],
                        local_sem.at[part],
                    ).events()
                    for part in (2 * pair, 2 * pair + 1)
                ]
            )
        )
    for event in skewed(groups, 1):
        event()
    link.drain()


def gather_layer(mesh, own, small=None):
    fsdp_size, ctx_size = mesh.shape["fsdp"], mesh.shape["ctx"]
    parts, block, columns = own.shape
    everyone = fsdp_size * ctx_size
    out_shape = [jax.ShapeDtypeStruct((parts, everyone * block, columns), own.dtype)]
    operands = [own]
    if small is not None:
        operands.append(small)
        out_shape.append(jax.ShapeDtypeStruct((everyone * small.shape[0], small.shape[1]), small.dtype))
    pushes = gather_pushes(fsdp_size, ctx_size) * (parts + len(operands) - 1)
    any_space = pl.BlockSpec(memory_space=pl.ANY)
    return pl.pallas_call(
        functools.partial(gather_kernel, ctx_size, fsdp_size, small is not None),
        out_shape=out_shape,
        in_specs=[any_space] * len(operands),
        out_specs=[any_space] * len(out_shape),
        scratch_shapes=[
            pltpu.SemaphoreType.DMA((pushes,)),
            pltpu.SemaphoreType.DMA((pushes,)),
            pltpu.SemaphoreType.DMA((parts + 1,)),
        ],
        compiler_params=pltpu.CompilerParams(
            collective_id=0 if small is None else 1, has_side_effects=True
        ),
        name="gather_layer",
    )(*operands)


class Scatter:
    def __init__(self, link, ctx_size, terms, held, arrived, last, order, load_sem, write):
        self.link, self.terms, self.held, self.arrived, self.last = link, terms, held, arrived, last
        self.ctx_size, self.order, self.load_sem, self.write = ctx_size, order, load_sem, write
        self.me, self.ctx = lax.axis_index("fsdp"), lax.axis_index("ctx")
        self.both = held.shape[1]
        self.slots = held.shape[0]
        self.flips = []
        for slot in range(self.slots):
            chosen = [
                bit for at, bit in enumerate(order) if (slot >> (len(order) - 1 - at)) % 2 == 1
            ]
            self.flips.append(chosen)
        self.base = 0

    def start(self):
        other = flip(self.me, 0)
        self.copies, self.loads = [], []
        for slot, chosen in enumerate(self.flips):
            theirs = self.terms.at[rows_of(flip_all(other, chosen), self.both)]
            ours = self.terms.at[rows_of(flip_all(self.me, chosen), self.both)]
            self.copies.append(self.link.push(theirs, self.arrived.at[slot], {"fsdp": other}))
            load = pltpu.make_async_copy(ours, self.held.at[slot], self.load_sem.at[slot])
            load.start()
            self.loads.append(load)

    def take(self, count, base):
        for copy in self.copies:
            copy.wait_recv()
        for slot in range(count):
            self.held[slot] = self.held[slot] + self.arrived[base + slot]

    def step(self, at):
        count = self.slots >> at
        if at == 0:
            for load in self.loads:
                load.wait()
        self.take(count, self.base)
        self.base += count
        half = count // 2
        self.copies = [
            self.link.push(
                self.held.at[pl.ds(half, half)],
                self.arrived.at[pl.ds(self.base, half)],
                {"fsdp": flip(self.me, self.order[at])},
            )
        ]

    def across(self):
        self.take(1, self.base)
        if self.ctx_size > 1:
            block = self.both // self.ctx_size
            self.copies = [
                self.link.push(
                    self.held.at[0, rows_of(1 - self.ctx, block)],
                    self.last,
                    {"ctx": 1 - self.ctx},
                )
            ]

    def finish(self):
        block = self.both // self.ctx_size
        total = self.held[0, rows_of(self.ctx, block)].astype(F32)
        if self.ctx_size > 1:
            for copy in self.copies:
                copy.wait_recv()
            total = total + self.last[...].astype(F32)
        self.write(total)

    def events(self):
        found = [self.start]
        for at in range(len(self.order)):
            found.append(functools.partial(self.step, at))
        return found + [self.across, self.finish]


class Total:
    def __init__(self, link, fsdp_size, ctx_size, held, arrived):
        self.link, self.held, self.arrived = link, held, arrived
        me, ctx = lax.axis_index("fsdp"), lax.axis_index("ctx")
        self.partners = [{"fsdp": flip(me, bit)} for bit in range(fsdp_size.bit_length() - 1)]
        if ctx_size > 1:
            self.partners.append({"ctx": 1 - ctx})

    def step(self, at):
        if at > 0:
            self.copy.wait_recv()
            self.held[at] = self.held[at - 1] + self.arrived[at - 1]
        if at < len(self.partners):
            self.copy = self.link.push(self.held.at[at], self.arrived.at[at], self.partners[at])

    def events(self):
        return [functools.partial(self.step, at) for at in range(len(self.partners) + 1)]


def scatter_pushes(fsdp_size):
    steps = fsdp_size.bit_length() - 2
    return 2**steps + steps + 1


def scatter_kernel(
    ctx_size,
    fsdp_size,
    terms_ref,
    small_ref,
    out_ref,
    small_out,
    held,
    arrived,
    last,
    small_held,
    small_arrived,
    send_sem,
    recv_sem,
    load_sem,
):
    small_held[0] = small_ref[...]
    greet(fsdp_size, ctx_size, False)
    link = Link(send_sem, recv_sem)
    both = [order[::-1] for order in orders(fsdp_size)]
    total = Total(link, fsdp_size, ctx_size, small_held, small_arrived)
    groups = [total.events()]

    def writer(part):
        def write(value):
            out_ref[part] = value

        return write

    for pair in range(PARTS // 2):
        groups.append(
            in_step(
                *[
                    Scatter(
                        link,
                        ctx_size,
                        terms_ref.at[part],
                        held.at[part],
                        arrived.at[part],
                        last.at[part],
                        both[part % 2],
                        load_sem.at[part],
                        writer(part),
                    ).events()
                    for part in (2 * pair, 2 * pair + 1)
                ]
            )
        )
    for event in skewed(groups, 1):
        event()
    small_out[...] = small_held[len(total.partners)]
    link.drain()


def scatter_layer(mesh, terms, small):
    fsdp_size, ctx_size = mesh.shape["fsdp"], mesh.shape["ctx"]
    parts, depth, columns = terms.shape
    both = depth // fsdp_size
    block = both // ctx_size
    slots = fsdp_size // 2
    steps = fsdp_size.bit_length() - 1 + (ctx_size > 1)
    pushes = scatter_pushes(fsdp_size) * parts + steps
    vmem = pl.BlockSpec(memory_space=pltpu.VMEM)
    return pl.pallas_call(
        functools.partial(scatter_kernel, ctx_size, fsdp_size),
        out_shape=[
            jax.ShapeDtypeStruct((parts, block, columns), F32),
            jax.ShapeDtypeStruct(small.shape, F32),
        ],
        in_specs=[pl.BlockSpec(memory_space=pl.ANY), vmem],
        out_specs=[vmem, vmem],
        scratch_shapes=[
            pltpu.VMEM((parts, slots, both, columns), BF16),
            pltpu.VMEM((parts, 2 * slots - 1, both, columns), BF16),
            pltpu.VMEM((parts, block, columns), BF16),
            pltpu.VMEM((steps + 1,) + small.shape, F32),
            pltpu.VMEM((steps,) + small.shape, F32),
            pltpu.SemaphoreType.DMA((pushes,)),
            pltpu.SemaphoreType.DMA((pushes,)),
            pltpu.SemaphoreType.DMA((parts, slots)),
        ],
        compiler_params=pltpu.CompilerParams(
            collective_id=2, has_side_effects=True, vmem_limit_bytes=48 * 2**20
        ),
        name="scatter_layer",
    )(terms, small)


def layer_norm(values, norm_gain, norm_shift):
    row_mean = jnp.mean(values, axis=-1, keepdims=True)
    centered = values - row_mean
    row_var = jnp.mean(centered * centered, axis=-1, keepdims=True)
    return centered * lax.rsqrt(row_var + EPS) * norm_gain + norm_shift


def gelu_exact(values):
    return jax.nn.gelu(values, approximate=False)


def head_sum(partial_rows):
    return lax.psum(partial_rows, "tp")


def dot(spec, left, right):
    return jnp.einsum(spec, left, right, preferred_element_type=F32)


def masked_scores(query_heads, key_heads, key_live, score_scale):
    raw_scores = dot("nqhd,nkhd->nhqk", query_heads, key_heads) * score_scale
    return jnp.where(key_live, raw_scores, NEG)


def body(
    mesh,
    tokens,
    lengths,
    cotangent,
    attn_gain,
    attn_shift,
    qkv_weight,
    qv_bias,
    out_weight,
    out_bias,
    mlp_gain,
    mlp_shift,
    up_weight,
    up_bias,
    down_weight,
    down_bias,
):
    images, local_slots, width = tokens.shape
    fsdp_size, ctx_size = mesh.shape["fsdp"], mesh.shape["ctx"]
    everyone = fsdp_size * ctx_size
    slots_all = local_slots * ctx_size
    layers, block, _, cols = qkv_weight.shape
    heads_here = cols // HEAD_DIM
    units = up_weight.shape[2]
    score_scale = HEAD_DIM ** (-0.5)
    slot_ids = lax.axis_index("ctx") * local_slots + jnp.arange(local_slots, dtype=jnp.int32)
    row_mask = (slot_ids[None, :] < lengths[:, None]).astype(F32)[:, :, None]
    key_live = (jnp.arange(slots_all, dtype=jnp.int32)[None, :] < lengths[:, None])[
        :, None, None, :
    ]
    vectors = jnp.stack((attn_gain, attn_shift, out_bias, mlp_gain, mlp_shift, down_bias), axis=1)
    flat = vectors.reshape(-1)
    small_rows = 16 * -(-flat.size // (16 * 2 * cols))
    small = jnp.pad(flat, (0, small_rows * 2 * cols - flat.size)).reshape(small_rows, 2 * cols)
    out_t = jnp.swapaxes(out_weight, 1, 2)
    down_t = jnp.swapaxes(down_weight, 1, 2)

    def own_parts(at):
        return jnp.stack(
            (
                qkv_weight[at, :, 0:2].reshape(block, 2 * cols),
                jnp.concatenate((qkv_weight[at, :, 2], out_t[at]), axis=1),
                up_weight[at, :, : units // 2],
                up_weight[at, :, units // 2 :],
                down_t[at, :, : units // 2],
                down_t[at, :, units // 2 :],
            )
        )

    weights = []
    for at in range(layers):
        if at == 0:
            whole, small_whole = gather_layer(mesh, own_parts(at), small)
        else:
            (whole,) = gather_layer(mesh, own_parts(at))
        weights.append(whole)
    gathered = small_whole.reshape(everyone, small_rows * 2 * cols)[:, : flat.size]
    vectors = jnp.swapaxes(gathered.reshape(everyone, layers * 6, block), 0, 1)
    vectors = vectors.reshape(layers, 6, width).astype(F32)

    stream = tokens.astype(F32) * row_mask
    kept = []
    for at in range(layers):
        whole = weights[at]
        gain_a, shift_a, out_b, gain_b, shift_b, down_b = [vectors[at, i] for i in range(6)]
        bias_qv = qv_bias[at].astype(F32)
        normed_a = layer_norm(stream, gain_a, shift_a).astype(BF16)
        queries = (dot("nsd,df->nsf", normed_a, whole[0, :, :cols]) + bias_qv[0]).astype(BF16)
        keys_own = dot("nsd,df->nsf", normed_a, whole[0, :, cols:]).astype(BF16)
        values_own = (dot("nsd,df->nsf", normed_a, whole[1, :, :cols]) + bias_qv[1]).astype(BF16)
        both = lax.all_gather(jnp.concatenate((keys_own, values_own), -1), "ctx", axis=1, tiled=True)
        query_heads = queries.reshape(images, local_slots, heads_here, HEAD_DIM)
        key_heads = both[:, :, :cols].reshape(images, slots_all, heads_here, HEAD_DIM)
        value_heads = both[:, :, cols:].reshape(images, slots_all, heads_here, HEAD_DIM)
        scores = masked_scores(query_heads, key_heads, key_live, score_scale)
        row_top = jnp.max(scores, axis=-1, keepdims=True)
        exp_scores = jnp.exp(scores - row_top)
        row_total = jnp.sum(exp_scores, axis=-1, keepdims=True)
        attn_probs = (exp_scores / row_total).astype(BF16)
        log_total = row_top + jnp.log(row_total)
        attended = dot("nhqk,nkhd->nqhd", attn_probs, value_heads)
        attended = attended.reshape(images, local_slots, cols).astype(BF16)
        branch_a = head_sum(dot("nsf,df->nsd", attended, whole[1, :, cols:]))
        mid = stream + row_mask * (branch_a + out_b)
        normed_b = layer_norm(mid, gain_b, shift_b).astype(BF16)
        hidden_pre = jnp.concatenate(
            [dot("nsd,df->nsf", normed_b, whole[part]) for part in (2, 3)], axis=-1
        ) + up_bias[at].astype(F32)
        hidden = gelu_exact(hidden_pre).astype(BF16)
        halves = (hidden[:, :, : units // 2], hidden[:, :, units // 2 :])
        branch_b = head_sum(
            dot("nsf,df->nsd", halves[0], whole[4]) + dot("nsf,df->nsd", halves[1], whole[5])
        )
        kept.append(
            (
                stream,
                normed_a,
                query_heads,
                key_heads,
                value_heads,
                log_total,
                attended,
                mid,
                normed_b,
                hidden_pre,
                halves,
            )
        )
        stream = mid + row_mask * (branch_b + down_b)
    output = stream.astype(BF16)
    grad_stream = cotangent.astype(F32)
    big, little = [None] * layers, [None] * layers
    for at in reversed(range(layers)):
        (
            layer_in,
            normed_a,
            query_heads,
            key_heads,
            value_heads,
            log_total,
            attended,
            mid,
            normed_b,
            hidden_pre,
            halves,
        ) = kept[at]
        whole = weights[at]
        gain_a, shift_a, out_b, gain_b, shift_b, down_b = [vectors[at, i] for i in range(6)]
        grad_branch_b = row_mask * grad_stream
        grad_down_b = jnp.sum(grad_branch_b, axis=(0, 1))
        low_b = grad_branch_b.astype(BF16)
        grad_down = [dot("nsd,nsf->df", low_b, half) for half in halves]
        grad_hidden = jnp.concatenate(
            [dot("nsd,df->nsf", low_b, whole[part]) for part in (4, 5)], axis=-1
        )
        grad_pre = jax.vjp(gelu_exact, hidden_pre)[1](grad_hidden)[0]
        grad_up_b = jnp.sum(grad_pre, axis=(0, 1))
        low_pre = grad_pre.astype(BF16)
        pre_halves = (low_pre[:, :, : units // 2], low_pre[:, :, units // 2 :])
        grad_up = [dot("nsd,nsf->df", normed_b, half) for half in pre_halves]
        grad_normed_b = head_sum(
            dot("nsf,df->nsd", pre_halves[0], whole[2])
            + dot("nsf,df->nsd", pre_halves[1], whole[3])
        )
        grad_mid_norm, grad_gain_b, grad_shift_b = jax.vjp(layer_norm, mid, gain_b, shift_b)[1](
            grad_normed_b
        )
        grad_mid = grad_stream + grad_mid_norm
        grad_branch_a = row_mask * grad_mid
        grad_out_b = jnp.sum(grad_branch_a, axis=(0, 1))
        low_a = grad_branch_a.astype(BF16)
        grad_out = dot("nsd,nsf->df", low_a, attended)
        grad_att = dot("nsd,df->nsf", low_a, whole[1, :, cols:]).astype(BF16)
        grad_att = grad_att.reshape(images, local_slots, heads_here, HEAD_DIM)
        scores = masked_scores(query_heads, key_heads, key_live, score_scale)
        attn_p = jnp.exp(scores - log_total)
        grad_probs = dot("nqhd,nkhd->nhqk", grad_att, value_heads)
        row_dot = jnp.sum(attn_p * grad_probs, axis=-1, keepdims=True)
        grad_scores = (attn_p * (grad_probs - row_dot)).astype(BF16)
        grad_q = (dot("nhqk,nkhd->nqhd", grad_scores, key_heads) * score_scale).astype(BF16)
        grad_q = grad_q.reshape(images, local_slots, cols)
        grad_k = dot("nhqk,nqhd->nkhd", grad_scores, query_heads) * score_scale
        grad_v = dot("nhqk,nqhd->nkhd", attn_p.astype(BF16), grad_att)
        grad_kv = jnp.concatenate(
            (
                grad_k.reshape(images, slots_all, cols),
                grad_v.reshape(images, slots_all, cols),
            ),
            axis=-1,
        )
        grad_kv = lax.psum_scatter(grad_kv, "ctx", scatter_dimension=1, tiled=True).astype(BF16)
        grad_v = grad_kv[:, :, cols:]
        grad_qv_b = jnp.concatenate(
            (jnp.sum(grad_q.astype(F32), axis=(0, 1)), jnp.sum(grad_v.astype(F32), axis=(0, 1)))
        )
        grad_qk = jnp.concatenate((grad_q, grad_kv[:, :, :cols]), axis=-1)
        terms = [
            dot("nsd,nsf->df", normed_a, grad_qk),
            jnp.concatenate((dot("nsd,nsf->df", normed_a, grad_v), grad_out), axis=1),
            *grad_up,
            *grad_down,
        ]
        grad_normed_a = head_sum(
            dot("nsf,df->nsd", grad_qk, whole[0]) + dot("nsf,df->nsd", grad_v, whole[1, :, :cols])
        )
        grad_in_norm, grad_gain_a, grad_shift_a = jax.vjp(layer_norm, layer_in, gain_a, shift_a)[1](
            grad_normed_a
        )
        grad_stream = grad_mid + grad_in_norm
        rows = [grad_gain_a, grad_shift_a, grad_out_b, grad_gain_b, grad_shift_b, grad_down_b]
        rows.append(grad_qv_b)
        rows.extend(jnp.split(grad_up_b, units // width))
        rows = jnp.pad(jnp.stack(rows), ((0, -len(rows) % 8), (0, 0)))
        big[at], little[at] = scatter_layer(
            mesh, jnp.stack([term.astype(BF16) for term in terms]), rows
        )
    input_grad = grad_stream * row_mask
    big, little = jnp.stack(big), jnp.stack(little)
    here = (lax.axis_index("fsdp") * ctx_size + lax.axis_index("ctx")) * block
    own_vectors = lax.dynamic_slice_in_dim(little[:, :6], here, block, axis=2)
    grad_qkv = jnp.concatenate((big[:, 0], big[:, 1, :, :cols]), axis=2)
    return (
        output,
        input_grad,
        own_vectors[:, 0],
        own_vectors[:, 1],
        grad_qkv.reshape(layers, block, 3, cols),
        little[:, 6].reshape(layers, 2, cols),
        jnp.swapaxes(big[:, 1, :, cols:], 1, 2),
        own_vectors[:, 2],
        own_vectors[:, 3],
        own_vectors[:, 4],
        jnp.concatenate((big[:, 2], big[:, 3]), axis=2),
        little[:, 7 : 7 + units // width].reshape(layers, units),
        jnp.swapaxes(jnp.concatenate((big[:, 4], big[:, 5]), axis=2), 1, 2),
        own_vectors[:, 5],
    )


def solution(mesh):
    place = P(None, ("fsdp", "ctx"))
    rows = P("fsdp", "ctx", None)
    return jax.shard_map(
        functools.partial(body, mesh),
        mesh=mesh,
        in_specs=(
            rows,
            P("fsdp"),
            rows,
            place,
            place,
            P(None, ("fsdp", "ctx"), None, "tp"),
            P(None, None, "tp"),
            P(None, "tp", ("fsdp", "ctx")),
            place,
            place,
            place,
            P(None, ("fsdp", "ctx"), "tp"),
            P(None, "tp"),
            P(None, "tp", ("fsdp", "ctx")),
            place,
        ),
        out_specs=(
            rows,
            rows,
            place,
            place,
            P(None, ("fsdp", "ctx"), None, "tp"),
            P(None, None, "tp"),
            P(None, "tp", ("fsdp", "ctx")),
            place,
            place,
            place,
            P(None, ("fsdp", "ctx"), "tp"),
            P(None, "tp"),
            P(None, "tp", ("fsdp", "ctx")),
            place,
        ),
        check_vma=False,
    )
```

```python
import functools

import jax
import jax.numpy as jnp
from jax import lax
from jax.experimental import pallas as pl
from jax.experimental.pallas import tpu as pltpu
from jax.sharding import PartitionSpec as P

HEAD_DIM = 64
EPS = 1e-05
NEG = -30000.0
MESH = pl.DeviceIdType.MESH
PARTS = 6
BF16 = jnp.bfloat16
F32 = jnp.float32


def flip(index, bit):
    size = 2**bit
    return index + size - 2 * size * ((index // size) % 2)


def flip_all(index, bits):
    for bit in bits:
        index = flip(index, bit)
    return index


def subsets(bits):
    found = [()]
    for bit in bits:
        found = found + [entry + (bit,) for entry in found]
    return found


def orders(fsdp_size):
    top = fsdp_size.bit_length() - 1
    bits = list(range(1, top))
    half = len(bits) // 2
    return bits, bits[half:] + bits[:half]


class Link:
    def __init__(self, send_sem, recv_sem):
        self.send_sem, self.recv_sem, self.used, self.sent = send_sem, recv_sem, 0, []

    def push(self, src, dst, device):
        at = self.used
        self.used += 1
        copy = pltpu.make_async_remote_copy(
            src_ref=src,
            dst_ref=dst,
            send_sem=self.send_sem.at[at],
            recv_sem=self.recv_sem.at[at],
            device_id=device,
            device_id_type=MESH,
        )
        copy.start()
        self.sent.append(copy)
        return copy

    def drain(self):
        for copy in self.sent:
            copy.wait_send()
        self.sent = []


def greet(fsdp_size, ctx_size, with_tp):
    me, ctx, tp = lax.axis_index("fsdp"), lax.axis_index("ctx"), lax.axis_index("tp")
    barrier = pltpu.get_barrier_semaphore()
    count = 0
    for bit in range(fsdp_size.bit_length() - 1):
        pl.semaphore_signal(
            barrier, inc=1, device_id={"fsdp": flip(me, bit)}, device_id_type=MESH
        )
        count += 1
    if ctx_size > 1:
        pl.semaphore_signal(barrier, inc=1, device_id={"ctx": 1 - ctx}, device_id_type=MESH)
        count += 1
    if with_tp:
        pl.semaphore_signal(barrier, inc=1, device_id={"tp": 1 - tp}, device_id_type=MESH)
        count += 1
    pl.semaphore_wait(barrier, count)


def rows_of(start, rows):
    return pl.ds(pl.multiple_of(start * rows, rows), rows)


def gather_pushes(fsdp_size, ctx_size):
    steps = fsdp_size.bit_length() - 2
    return (ctx_size - 1) + ctx_size * (2**steps - 1) + 2**steps


class Gather:
    def __init__(self, link, ctx_size, own, whole, block, order, local_sem):
        self.link, self.own, self.whole, self.block, self.order = link, own, whole, block, order
        self.ctx_size = ctx_size
        self.me, self.ctx = lax.axis_index("fsdp"), lax.axis_index("ctx")
        self.waits = {}
        self.stay = pltpu.make_async_copy(own, self.rows(self.me, self.ctx), local_sem)

    def rows(self, fsdp, ctx):
        return self.whole.at[rows_of(fsdp * self.ctx_size + ctx, self.block)]

    def spread(self, stream, step):
        ctx = self.ctx if stream == 0 else 1 - self.ctx
        bit = self.order[step]
        to = {"fsdp": flip(self.me, bit)}
        copies = []
        for entry in subsets(self.order[:step]):
            place = self.rows(flip_all(self.me, entry), ctx)
            source = self.own if (stream == 0 and not entry) else place
            copies.append(self.link.push(source, place, to))
        self.waits[stream, step] = copies

    def arrive(self, *key):
        for copy in self.waits.pop(key):
            copy.wait_recv()

    def start(self):
        self.stay.start()
        if self.ctx_size > 1:
            self.waits["ctx",] = [
                self.link.push(self.own, self.rows(self.me, self.ctx), {"ctx": 1 - self.ctx})
            ]
        self.spread(0, 0)

    def next_step(self, stream, step):
        self.arrive(stream, step - 1)
        self.spread(stream, step)

    def other(self):
        self.arrive("ctx")
        self.spread(1, 0)

    def core(self):
        last = len(self.order) - 1
        for stream in range(self.ctx_size):
            self.arrive(stream, last)
        self.stay.wait()
        both = self.block * self.ctx_size
        copies = []
        for entry in subsets(self.order):
            place = self.whole.at[rows_of(flip_all(self.me, entry), both)]
            copies.append(self.link.push(place, place, {"fsdp": flip(self.me, 0)}))
        self.waits["core",] = copies

    def finish(self):
        self.arrive("core")

    def events(self):
        found = [self.start]
        for step in range(1, len(self.order)):
            found.append(functools.partial(self.next_step, 0, step))
        if self.ctx_size > 1:
            found.append(self.other)
            for step in range(1, len(self.order)):
                found.append(functools.partial(self.next_step, 1, step))
        return found + [self.core, self.finish]


def skewed(groups, skew):
    timed = []
    for at, events in enumerate(groups):
        for place, event in enumerate(events):
            timed.append((0 if place == 0 else place + at * skew, at, place, event))
    return [entry[3] for entry in sorted(timed, key=lambda entry: entry[:3])]


def in_step(first, second):
    def run(one, two):
        one()
        two()

    return [functools.partial(run, one, two) for one, two in zip(first, second)]


def gather_events(link, ctx_size, fsdp_size, own_ref, whole_ref, local_sem, small=None):
    both = orders(fsdp_size)
    groups = []
    if small is not None:
        small_ref, small_whole = small
        groups.append(
            Gather(
                link, ctx_size, small_ref, small_whole, small_ref.shape[0], both[0], local_sem.at[PARTS]
            ).events()
        )
    for pair in range(PARTS // 2):
        groups.append(
            in_step(
                *[
                    Gather(
                        link,
                        ctx_size,
                        own_ref.at[part],
                        whole_ref.at[part],
                        own_ref.shape[1],
                        both[part % 2],
                        local_sem.at[part],
                    ).events()
                    for part in (2 * pair, 2 * pair + 1)
                ]
            )
        )
    return skewed(groups, 1)


def gather_kernel(ctx_size, fsdp_size, own_ref, small_ref, whole_ref, small_whole, send_sem, recv_sem, local_sem):
    greet(fsdp_size, ctx_size, False)
    link = Link(send_sem, recv_sem)
    small = (small_ref, small_whole)
    for event in gather_events(link, ctx_size, fsdp_size, own_ref, whole_ref, local_sem, small):
        event()
    link.drain()


def gather_layer(mesh, own, small):
    fsdp_size, ctx_size = mesh.shape["fsdp"], mesh.shape["ctx"]
    parts, block, columns = own.shape
    everyone = fsdp_size * ctx_size
    pushes = gather_pushes(fsdp_size, ctx_size) * (parts + 1)
    any_space = pl.BlockSpec(memory_space=pl.ANY)
    return pl.pallas_call(
        functools.partial(gather_kernel, ctx_size, fsdp_size),
        out_shape=[
            jax.ShapeDtypeStruct((parts, everyone * block, columns), own.dtype),
            jax.ShapeDtypeStruct((everyone * small.shape[0], small.shape[1]), small.dtype),
        ],
        in_specs=[any_space] * 2,
        out_specs=[any_space] * 2,
        scratch_shapes=[
            pltpu.SemaphoreType.DMA((pushes,)),
            pltpu.SemaphoreType.DMA((pushes,)),
            pltpu.SemaphoreType.DMA((parts + 1,)),
        ],
        compiler_params=pltpu.CompilerParams(collective_id=1, has_side_effects=True),
        name="gather_layer",
    )(own, small)


class Scatter:
    def __init__(self, link, ctx_size, terms, held, arrived, last, order, load_sem, write):
        self.link, self.terms, self.held, self.arrived, self.last = link, terms, held, arrived, last
        self.ctx_size, self.order, self.load_sem, self.write = ctx_size, order, load_sem, write
        self.me, self.ctx = lax.axis_index("fsdp"), lax.axis_index("ctx")
        self.both = held.shape[1]
        self.slots = held.shape[0]
        self.flips = []
        for slot in range(self.slots):
            chosen = [
                bit for at, bit in enumerate(order) if (slot >> (len(order) - 1 - at)) % 2 == 1
            ]
            self.flips.append(chosen)
        self.base = 0

    def start(self):
        other = flip(self.me, 0)
        self.copies, self.loads = [], []
        for slot, chosen in enumerate(self.flips):
            theirs = self.terms.at[rows_of(flip_all(other, chosen), self.both)]
            ours = self.terms.at[rows_of(flip_all(self.me, chosen), self.both)]
            self.copies.append(self.link.push(theirs, self.arrived.at[slot], {"fsdp": other}))
            load = pltpu.make_async_copy(ours, self.held.at[slot], self.load_sem.at[slot])
            load.start()
            self.loads.append(load)

    def take(self, count, base):
        for copy in self.copies:
            copy.wait_recv()
        for slot in range(count):
            self.held[slot] = self.held[slot] + self.arrived[base + slot]

    def step(self, at):
        count = self.slots >> at
        if at == 0:
            for load in self.loads:
                load.wait()
        self.take(count, self.base)
        self.base += count
        half = count // 2
        self.copies = [
            self.link.push(
                self.held.at[pl.ds(half, half)],
                self.arrived.at[pl.ds(self.base, half)],
                {"fsdp": flip(self.me, self.order[at])},
            )
        ]

    def across(self):
        self.take(1, self.base)
        if self.ctx_size > 1:
            block = self.both // self.ctx_size
            self.copies = [
                self.link.push(
                    self.held.at[0, rows_of(1 - self.ctx, block)],
                    self.last,
                    {"ctx": 1 - self.ctx},
                )
            ]

    def finish(self):
        block = self.both // self.ctx_size
        total = self.held[0, rows_of(self.ctx, block)].astype(F32)
        if self.ctx_size > 1:
            for copy in self.copies:
                copy.wait_recv()
            total = total + self.last[...].astype(F32)
        self.write(total)

    def events(self):
        found = [self.start]
        for at in range(len(self.order)):
            found.append(functools.partial(self.step, at))
        return found + [self.across, self.finish]


class Total:
    def __init__(self, link, fsdp_size, ctx_size, held, arrived):
        self.link, self.held, self.arrived = link, held, arrived
        me, ctx = lax.axis_index("fsdp"), lax.axis_index("ctx")
        self.partners = [{"fsdp": flip(me, bit)} for bit in range(fsdp_size.bit_length() - 1)]
        if ctx_size > 1:
            self.partners.append({"ctx": 1 - ctx})

    def step(self, at):
        if at > 0:
            self.copy.wait_recv()
            self.held[at] = self.held[at - 1] + self.arrived[at - 1]
        if at < len(self.partners):
            self.copy = self.link.push(self.held.at[at], self.arrived.at[at], self.partners[at])

    def events(self):
        return [functools.partial(self.step, at) for at in range(len(self.partners) + 1)]


def scatter_count(mesh):
    steps = mesh.shape["fsdp"].bit_length() - 2
    return (2**steps + steps + 1) * PARTS + steps + 1 + (mesh.shape["ctx"] > 1)


def scatter_scratch(mesh, terms, small):
    parts, depth, columns = terms.shape
    both = depth // mesh.shape["fsdp"]
    slots = mesh.shape["fsdp"] // 2
    steps = mesh.shape["fsdp"].bit_length() - 1 + (mesh.shape["ctx"] > 1)
    return [
        pltpu.VMEM((parts, slots, both, columns), BF16),
        pltpu.VMEM((parts, 2 * slots - 1, both, columns), BF16),
        pltpu.VMEM((parts, both // mesh.shape["ctx"], columns), BF16),
        pltpu.VMEM((steps + 1,) + small.shape, F32),
        pltpu.VMEM((steps,) + small.shape, F32),
        pltpu.SemaphoreType.DMA((parts, slots)),
    ]


def scatter_shapes(mesh, terms, small):
    parts, depth, columns = terms.shape
    block = depth // (mesh.shape["fsdp"] * mesh.shape["ctx"])
    return [
        jax.ShapeDtypeStruct((parts, block, columns), F32),
        jax.ShapeDtypeStruct(small.shape, F32),
    ]


def scatter_events(
    link,
    ctx_size,
    fsdp_size,
    terms_ref,
    out_ref,
    small_out,
    held,
    arrived,
    last,
    small_held,
    small_arrived,
    load_sem,
):
    both = [order[::-1] for order in orders(fsdp_size)]
    total = Total(link, fsdp_size, ctx_size, small_held, small_arrived)
    groups = [total.events()]

    def writer(part):
        def write(value):
            out_ref[part] = value

        return write

    for pair in range(PARTS // 2):
        groups.append(
            in_step(
                *[
                    Scatter(
                        link,
                        ctx_size,
                        terms_ref.at[part],
                        held.at[part],
                        arrived.at[part],
                        last.at[part],
                        both[part % 2],
                        load_sem.at[part],
                        writer(part),
                    ).events()
                    for part in (2 * pair, 2 * pair + 1)
                ]
            )
        )

    def finish():
        small_out[...] = small_held[len(total.partners)]

    return skewed(groups, 1), finish


def scatter_kernel(ctx_size, fsdp_size, terms_ref, small_ref, out_ref, small_out, *scratch):
    *buffers, send_sem, recv_sem = scratch
    buffers[3][0] = small_ref[...]
    greet(fsdp_size, ctx_size, False)
    link = Link(send_sem, recv_sem)
    events, finish = scatter_events(
        link, ctx_size, fsdp_size, terms_ref, out_ref, small_out, *buffers
    )
    for event in events:
        event()
    finish()
    link.drain()


def scatter_layer(mesh, terms, small):
    pushes = scatter_count(mesh)
    vmem = pl.BlockSpec(memory_space=pltpu.VMEM)
    return pl.pallas_call(
        functools.partial(scatter_kernel, mesh.shape["ctx"], mesh.shape["fsdp"]),
        out_shape=scatter_shapes(mesh, terms, small),
        in_specs=[pl.BlockSpec(memory_space=pl.ANY), vmem],
        out_specs=[vmem, vmem],
        scratch_shapes=scatter_scratch(mesh, terms, small)
        + [pltpu.SemaphoreType.DMA((pushes,)), pltpu.SemaphoreType.DMA((pushes,))],
        compiler_params=pltpu.CompilerParams(
            collective_id=2, has_side_effects=True, vmem_limit_bytes=48 * 2**20
        ),
        name="scatter_layer",
    )(terms, small)


def dot_nn(left, right):
    return lax.dot_general(left, right, (((1,), (0,)), ((), ())), preferred_element_type=F32)


def dot_nt(left, right):
    return lax.dot_general(left, right, (((1,), (1,)), ((), ())), preferred_element_type=F32)


def dot_tn(left, right):
    return lax.dot_general(left, right, (((0,), (0,)), ((), ())), preferred_element_type=F32)


TILE = 256
ROOT_HALF = 0.7071067811865476
ROOT_TWO_PI = 2.5066282746310002
GAIN_A, SHIFT_A, OUT_B, GAIN_B, SHIFT_B, DOWN_B, QV_B, UP_B = range(8)


def lanes(at, count):
    return pl.ds(pl.multiple_of(at * count, count), count)


def standardized(values):
    centered = values - jnp.mean(values, axis=-1, keepdims=True)
    scale = lax.rsqrt(jnp.mean(centered * centered, axis=-1, keepdims=True) + EPS)
    return centered * scale, scale


class Pump:
    def __init__(self, events):
        self.events = list(events)

    def __call__(self, count):
        for event in self.events[:count]:
            event()
        self.events = self.events[count:]

    def rest(self):
        self(len(self.events))


def send_pieces(link, partial, sent, got, pieces, partner):
    copies = []
    for at in range(pieces):
        sent[at] = partial(at).astype(BF16)
        copies.append(link.push(sent.at[at], got.at[at], partner))
    return copies


def both_halves(copies, sent, got):
    found = []
    for at, copy in enumerate(copies):
        copy.wait_recv()
        found.append(sent[at].astype(F32) + got[at].astype(F32))
    return jnp.concatenate(found, axis=1)


def load_parts(whole_ref, held, load_sem):
    copies = [
        pltpu.make_async_copy(whole_ref.at[part], held.at[part], load_sem.at[part])
        for part in range(PARTS)
    ]
    for copy in copies:
        copy.start()
    return copies


def forward_kernel(ctx_size, fsdp_size, with_next, *refs):
    refs = list(refs)
    stream_ref, mask_ref, live_ref, vector_ref, whole_ref = refs[:5]
    del refs[:5]
    next_own = refs.pop(0) if with_next else None
    (
        out_ref,
        normed_a_ref,
        query_ref,
        kv_ref,
        log_total_ref,
        attended_ref,
        mid_ref,
        normed_b_ref,
        pre_ref,
        hidden_ref,
    ) = refs[:10]
    del refs[:10]
    next_whole = refs.pop(0) if with_next else None
    held, kv, sent, got, send_sem, recv_sem, load_sem, local_sem = refs
    rows, width = stream_ref.shape
    cols = query_ref.shape[1]
    slots_all = kv.shape[0]
    pieces = width // TILE
    ctx = lax.axis_index("ctx")
    across = {"tp": 1 - lax.axis_index("tp")}
    loads = load_parts(whole_ref, held, load_sem)
    greet(fsdp_size, ctx_size, True)
    link = Link(send_sem, recv_sem)
    pump = Pump(gather_events(link, ctx_size, fsdp_size, next_own, next_whole, local_sem) if with_next else [])
    mask = mask_ref[...]

    normal, _ = standardized(stream_ref[...])
    normed_a_ref[...] = (
        normal * vector_ref[GAIN_A : GAIN_A + 1, :] + vector_ref[SHIFT_A : SHIFT_A + 1, :]
    ).astype(BF16)
    loads[0].wait()
    loads[1].wait()
    mine = rows_of(ctx, rows)

    @pl.loop(0, cols // TILE)
    def _(at):
        normed = normed_a_ref[...]
        kv[mine, lanes(at, TILE)] = dot_nn(
            normed, held[0, :, lanes(at + cols // TILE, TILE)]
        ).astype(BF16)
        kv[mine, lanes(at + cols // TILE, TILE)] = (
            dot_nn(normed, held[1, :, lanes(at, TILE)])
            + vector_ref[QV_B : QV_B + 1, lanes(at + cols // TILE, TILE)]
        ).astype(BF16)

    kv_copy = None
    if ctx_size > 1:
        kv_copy = link.push(kv.at[mine], kv.at[mine], {"ctx": 1 - ctx})
    pump(PARTS // 2)

    @pl.loop(0, cols // TILE)
    def _(at):
        query_ref[:, lanes(at, TILE)] = (
            dot_nn(normed_a_ref[...], held[0, :, lanes(at, TILE)])
            + vector_ref[QV_B : QV_B + 1, lanes(at, TILE)]
        ).astype(BF16)

    pump(1)
    if kv_copy is not None:
        kv_copy.wait_recv()
    pair = 2 * HEAD_DIM
    first = lax.broadcasted_iota(jnp.int32, (rows, pair), 1) < HEAD_DIM
    live = live_ref[...] > 0

    @pl.loop(0, cols // pair)
    def _(at):
        queries = query_ref[:, lanes(at, pair)]
        keys = kv[:, lanes(at, pair)]
        values = kv[:, lanes(at + cols // pair, pair)]
        found = []
        for head in range(2):
            chosen = jnp.where(first if head == 0 else ~first, queries, jnp.zeros_like(queries))
            scores = jnp.where(live, dot_nt(chosen, keys) * HEAD_DIM**-0.5, NEG)
            top = jnp.max(scores, axis=-1, keepdims=True)
            weights = jnp.exp(scores - top)
            total = jnp.sum(weights, axis=-1, keepdims=True)
            log_total_ref[2 * at + head] = top + jnp.log(total)
            found.append(dot_nn((weights * (1.0 / total)).astype(BF16), values))
        attended_ref[:, lanes(at, pair)] = jnp.where(first, found[0], found[1]).astype(BF16)

    def out_partial(at):
        return dot_nt(attended_ref[...], held[1, at * TILE : (at + 1) * TILE, cols:])

    copies = send_pieces(link, out_partial, sent.at[0], got.at[0], pieces, across)
    kv_ref[...] = kv[...]
    pump(2)
    for load in loads[2:]:
        load.wait()
    branch = both_halves(copies, sent.at[0], got.at[0])
    mid = stream_ref[...] + mask * (branch + vector_ref[OUT_B : OUT_B + 1, :])
    mid_ref[...] = mid
    normal, _ = standardized(mid)
    normed_b_ref[...] = (
        normal * vector_ref[GAIN_B : GAIN_B + 1, :] + vector_ref[SHIFT_B : SHIFT_B + 1, :]
    ).astype(BF16)
    pump(2)
    for part in range(2):

        @pl.loop(0, pieces)
        def _(at):
            pre = (
                dot_nn(normed_b_ref[...], held[2 + part, :, lanes(at, TILE)])
                + vector_ref[UP_B + part : UP_B + part + 1, lanes(at, TILE)]
            )
            pre_ref[part, :, lanes(at, TILE)] = pre
            hidden_ref[part, :, lanes(at, TILE)] = (
                0.5 * pre * (1.0 + lax.erf(pre * ROOT_HALF))
            ).astype(BF16)

    pump(2)

    def down_partial(at):
        here = slice(at * TILE, (at + 1) * TILE)
        return dot_nt(hidden_ref[0], held[4, here, :]) + dot_nt(hidden_ref[1], held[5, here, :])

    copies = send_pieces(link, down_partial, sent.at[1], got.at[1], pieces, across)
    pump(2)
    branch = both_halves(copies, sent.at[1], got.at[1])
    out_ref[...] = mid_ref[...] + mask * (branch + vector_ref[DOWN_B : DOWN_B + 1, :])
    pump.rest()
    link.drain()


def forward_layer(mesh, stream, mask, live, vectors, whole, next_own):
    fsdp_size, ctx_size = mesh.shape["fsdp"], mesh.shape["ctx"]
    rows, width = stream.shape
    cols = width // mesh.shape["tp"]
    slots_all = rows * ctx_size
    pieces = width // TILE
    shape = jax.ShapeDtypeStruct
    out_shape = [
        shape((rows, width), F32),
        shape((rows, width), BF16),
        shape((rows, cols), BF16),
        shape((slots_all, 2 * cols), BF16),
        shape((cols // HEAD_DIM, rows, 1), F32),
        shape((rows, cols), BF16),
        shape((rows, width), F32),
        shape((rows, width), BF16),
        shape((2, rows, width), F32),
        shape((2, rows, width), BF16),
    ]
    vmem = pl.BlockSpec(memory_space=pltpu.VMEM)
    any_space = pl.BlockSpec(memory_space=pl.ANY)
    operands = [stream, mask, live, vectors, whole]
    in_specs = [vmem] * 4 + [any_space]
    out_specs = [vmem] * len(out_shape)
    pushes = (ctx_size > 1) + 2 * pieces
    with_next = next_own is not None
    if with_next:
        operands.append(next_own)
        in_specs.append(any_space)
        out_shape.append(shape(whole.shape, BF16))
        out_specs.append(any_space)
        pushes += gather_pushes(fsdp_size, ctx_size) * PARTS
    return pl.pallas_call(
        functools.partial(forward_kernel, ctx_size, fsdp_size, with_next),
        out_shape=out_shape,
        in_specs=in_specs,
        out_specs=out_specs,
        scratch_shapes=[
            pltpu.VMEM(whole.shape, BF16),
            pltpu.VMEM((slots_all, 2 * cols), BF16),
            pltpu.VMEM((2, pieces, rows, TILE), BF16),
            pltpu.VMEM((2, pieces, rows, TILE), BF16),
            pltpu.SemaphoreType.DMA((pushes,)),
            pltpu.SemaphoreType.DMA((pushes,)),
            pltpu.SemaphoreType.DMA((PARTS,)),
            pltpu.SemaphoreType.DMA((PARTS,)),
        ],
        compiler_params=pltpu.CompilerParams(
            collective_id=3 if with_next else 4,
            has_side_effects=True,
            vmem_limit_bytes=56 * 2**20,
        ),
        name="forward_layer",
    )(*operands)


def norm_pull(values, gain, grad):
    normal, scale = standardized(values)
    grad_gain = jnp.sum(grad * normal, axis=0, keepdims=True)
    grad_shift = jnp.sum(grad, axis=0, keepdims=True)
    inner = grad * gain
    along = jnp.mean(inner * normal, axis=-1, keepdims=True)
    grad_in = scale * (inner - jnp.mean(inner, axis=-1, keepdims=True) - normal * along)
    return grad_in, grad_gain, grad_shift


def backward_kernel(ctx_size, fsdp_size, with_last, *refs):
    refs = list(refs)
    (
        grad_ref,
        mask_ref,
        live_ref,
        vector_ref,
        stream_ref,
        normed_a_ref,
        query_ref,
        kv_ref,
        log_total_ref,
        attended_ref,
        mid_ref,
        normed_b_ref,
        pre_ref,
        hidden_ref,
        whole_ref,
    ) = refs[:15]
    del refs[:15]
    if with_last:
        last_terms, last_small = refs[:2]
        del refs[:2]
    out_ref, small_ref, terms_ref = refs[:3]
    del refs[:3]
    if with_last:
        summed_ref, small_summed = refs[:2]
        del refs[:2]
    (
        held,
        terms,
        turned,
        low,
        low_pre,
        grad_att,
        grad_qk,
        grad_kv,
        kv_sent,
        kv_got,
        sent,
        got,
        send_sem,
        recv_sem,
        load_sem,
        term_sem,
    ) = refs[:16]
    del refs[:16]
    rows, width = grad_ref.shape
    cols = query_ref.shape[1]
    pieces = width // TILE
    ctx = lax.axis_index("ctx")
    across = {"tp": 1 - lax.axis_index("tp")}
    loads = load_parts(whole_ref, held, load_sem)
    small_ref[...] = jnp.zeros_like(small_ref)
    if with_last:
        small_held = refs[3]
        small_held[0] = last_small[...]
    greet(fsdp_size, ctx_size, True)
    link = Link(send_sem, recv_sem)
    pump = Pump([])
    if with_last:
        events, finish = scatter_events(
            link, ctx_size, fsdp_size, last_terms, summed_ref, small_summed, *refs
        )
        pump = Pump(events)
    mask = mask_ref[...]
    stores = []

    def keep(part):
        copy = pltpu.make_async_copy(terms.at[part], terms_ref.at[part], term_sem.at[part])
        copy.start()
        stores.append(copy)

    def product(part, start, count, right):
        @pl.loop(0, count)
        def _(at):
            terms[part, :, lanes(at + start, TILE)] = dot_nn(turned[...], right(at)).astype(BF16)

    masked = mask * grad_ref[...]
    small_ref[DOWN_B : DOWN_B + 1, :] = jnp.sum(masked, axis=0, keepdims=True)
    low[...] = masked.astype(BF16)
    pump(PARTS // 2 + 1)
    for load in loads:
        load.wait()
    for part in range(2):

        @pl.loop(0, pieces)
        def _(at):
            pre = pre_ref[part, :, lanes(at, TILE)]
            slope = 0.5 * (1.0 + lax.erf(pre * ROOT_HALF)) + pre * (
                jnp.exp(-0.5 * pre * pre) * (1.0 / ROOT_TWO_PI)
            )
            grad_pre = dot_nn(low[...], held[4 + part, :, lanes(at, TILE)]) * slope
            small_ref[UP_B + part : UP_B + part + 1, lanes(at, TILE)] = jnp.sum(
                grad_pre, axis=0, keepdims=True
            )
            low_pre[part, :, lanes(at, TILE)] = grad_pre.astype(BF16)

    def up_partial(at):
        here = slice(at * TILE, (at + 1) * TILE)
        return dot_nt(low_pre[0], held[2, here, :]) + dot_nt(low_pre[1], held[3, here, :])

    copies = send_pieces(link, up_partial, sent.at[0], got.at[0], pieces, across)
    pump(2)
    turned[...] = jnp.transpose(low[...])
    for part in range(2):
        product(4 + part, 0, pieces, lambda at, part=part: hidden_ref[part, :, lanes(at, TILE)])
        keep(4 + part)
    turned[...] = jnp.transpose(normed_b_ref[...])
    for part in range(2):
        product(2 + part, 0, pieces, lambda at, part=part: low_pre[part, :, lanes(at, TILE)])
        keep(2 + part)
    pump(2)
    grad_normed = both_halves(copies, sent.at[0], got.at[0])
    grad_in, grad_gain, grad_shift = norm_pull(
        mid_ref[...], vector_ref[GAIN_B : GAIN_B + 1, :], grad_normed
    )
    small_ref[GAIN_B : GAIN_B + 1, :] = grad_gain
    small_ref[SHIFT_B : SHIFT_B + 1, :] = grad_shift
    grad_mid = grad_ref[...] + grad_in
    out_ref[...] = grad_mid
    masked = mask * grad_mid
    small_ref[OUT_B : OUT_B + 1, :] = jnp.sum(masked, axis=0, keepdims=True)
    low[...] = masked.astype(BF16)

    @pl.loop(0, cols // TILE)
    def _(at):
        grad_att[:, lanes(at, TILE)] = dot_nn(
            low[...], held[1, :, lanes(at + cols // TILE, TILE)]
        ).astype(BF16)

    pump(2)
    pair = 2 * HEAD_DIM
    first = lax.broadcasted_iota(jnp.int32, (rows, pair), 1) < HEAD_DIM
    live = live_ref[...] > 0

    @pl.loop(0, cols // pair)
    def _(at):
        queries = query_ref[:, lanes(at, pair)]
        grads = grad_att[:, lanes(at, pair)]
        keys = kv_ref[:, lanes(at, pair)]
        values = kv_ref[:, lanes(at + cols // pair, pair)]
        found, key_grad, value_grad = [], None, None
        for head in range(2):
            here = first if head == 0 else ~first
            query = jnp.where(here, queries, jnp.zeros_like(queries))
            grad = jnp.where(here, grads, jnp.zeros_like(grads))
            scores = jnp.where(live, dot_nt(query, keys) * HEAD_DIM**-0.5, NEG)
            weights = jnp.exp(scores - log_total_ref[2 * at + head])
            grad_weights = dot_nt(grad, values)
            along = jnp.sum(weights * grad_weights, axis=-1, keepdims=True)
            grad_scores = (weights * (grad_weights - along)).astype(BF16)
            found.append(dot_nn(grad_scores, keys))
            one = dot_tn(grad_scores, query)
            two = dot_tn(weights.astype(BF16), grad)
            key_grad = one if head == 0 else key_grad + one
            value_grad = two if head == 0 else value_grad + two
        grad_qk[:, lanes(at, pair)] = (
            jnp.where(first, found[0], found[1]) * HEAD_DIM**-0.5
        ).astype(BF16)
        grad_kv[:, lanes(at, pair)] = key_grad * HEAD_DIM**-0.5
        grad_kv[:, lanes(at + cols // pair, pair)] = value_grad

    mine, theirs = rows_of(ctx, rows), rows_of(1 - ctx, rows)
    kv_copy = None
    if ctx_size > 1:
        kv_sent[...] = grad_kv[theirs, :].astype(BF16)
        kv_copy = link.push(kv_sent, kv_got, {"ctx": 1 - ctx})
    pump(2)
    small_ref[QV_B : QV_B + 1, :cols] = jnp.sum(
        grad_qk[:, :cols].astype(F32), axis=0, keepdims=True
    )
    turned[...] = jnp.transpose(low[...])
    product(1, cols // TILE, cols // TILE, lambda at: attended_ref[:, lanes(at, TILE)])
    turned[...] = jnp.transpose(normed_a_ref[...])
    product(0, 0, cols // TILE, lambda at: grad_qk[:, lanes(at, TILE)])
    pump(1)
    total_kv = grad_kv[mine, :]
    if kv_copy is not None:
        kv_copy.wait_recv()
        total_kv = total_kv + kv_got[...].astype(F32)
    total_kv = total_kv.astype(BF16)
    grad_qk[:, cols:] = total_kv
    small_ref[QV_B : QV_B + 1, cols:] = jnp.sum(
        grad_qk[:, 2 * cols :].astype(F32), axis=0, keepdims=True
    )

    def in_partial(at):
        here = slice(at * TILE, (at + 1) * TILE)
        return dot_nt(grad_qk[:, : 2 * cols], held[0, here, :]) + dot_nt(
            grad_qk[:, 2 * cols :], held[1, here, :cols]
        )

    copies = send_pieces(link, in_partial, sent.at[1], got.at[1], pieces, across)
    product(0, cols // TILE, cols // TILE, lambda at: grad_qk[:, lanes(at + cols // TILE, TILE)])
    keep(0)
    product(1, 0, cols // TILE, lambda at: grad_qk[:, lanes(at + 2 * cols // TILE, TILE)])
    keep(1)
    pump(2)
    grad_normed = both_halves(copies, sent.at[1], got.at[1])
    grad_in, grad_gain, grad_shift = norm_pull(
        stream_ref[...], vector_ref[GAIN_A : GAIN_A + 1, :], grad_normed
    )
    small_ref[GAIN_A : GAIN_A + 1, :] = grad_gain
    small_ref[SHIFT_A : SHIFT_A + 1, :] = grad_shift
    out_ref[...] = out_ref[...] + grad_in
    pump.rest()
    if with_last:
        finish()
    for copy in stores:
        copy.wait()
    link.drain()


def backward_layer(mesh, grad, mask, live, vectors, kept, whole, last):
    fsdp_size, ctx_size = mesh.shape["fsdp"], mesh.shape["ctx"]
    rows, width = grad.shape
    cols = width // mesh.shape["tp"]
    slots_all = rows * ctx_size
    pieces = width // TILE
    shape = jax.ShapeDtypeStruct
    vmem = pl.BlockSpec(memory_space=pltpu.VMEM)
    any_space = pl.BlockSpec(memory_space=pl.ANY)
    operands = [grad, mask, live, vectors, *kept, whole]
    in_specs = [vmem] * (len(operands) - 1) + [any_space]
    out_shape = [
        shape((rows, width), F32),
        shape(vectors.shape, F32),
        shape(whole.shape, BF16),
    ]
    out_specs = [vmem, vmem, any_space]
    pushes = (ctx_size > 1) + 2 * pieces
    scratch = [
        pltpu.VMEM(whole.shape, BF16),
        pltpu.VMEM(whole.shape, BF16),
        pltpu.VMEM((width, rows), BF16),
        pltpu.VMEM((rows, width), BF16),
        pltpu.VMEM((2, rows, width), BF16),
        pltpu.VMEM((rows, cols), BF16),
        pltpu.VMEM((rows, 3 * cols), BF16),
        pltpu.VMEM((slots_all, 2 * cols), F32),
        pltpu.VMEM((rows, 2 * cols), BF16),
        pltpu.VMEM((rows, 2 * cols), BF16),
        pltpu.VMEM((2, pieces, rows, TILE), BF16),
        pltpu.VMEM((2, pieces, rows, TILE), BF16),
    ]
    with_last = last is not None
    if with_last:
        last_terms, last_small = last
        operands += [last_terms, last_small]
        in_specs += [any_space, vmem]
        out_shape += scatter_shapes(mesh, last_terms, last_small)
        out_specs += [vmem, vmem]
        pushes += scatter_count(mesh)
    scratch += [
        pltpu.SemaphoreType.DMA((pushes,)),
        pltpu.SemaphoreType.DMA((pushes,)),
        pltpu.SemaphoreType.DMA((PARTS,)),
        pltpu.SemaphoreType.DMA((PARTS,)),
    ]
    if with_last:
        scratch += scatter_scratch(mesh, last_terms, last_small)
    return pl.pallas_call(
        functools.partial(backward_kernel, ctx_size, fsdp_size, with_last),
        out_shape=out_shape,
        in_specs=in_specs,
        out_specs=out_specs,
        scratch_shapes=scratch,
        compiler_params=pltpu.CompilerParams(
            collective_id=5 if with_last else 6,
            has_side_effects=True,
            vmem_limit_bytes=62 * 2**20,
        ),
        name="backward_layer",
    )(*operands)
def body(
    mesh,
    tokens,
    lengths,
    cotangent,
    attn_gain,
    attn_shift,
    qkv_weight,
    qv_bias,
    out_weight,
    out_bias,
    mlp_gain,
    mlp_shift,
    up_weight,
    up_bias,
    down_weight,
    down_bias,
):
    images, local_slots, width = tokens.shape
    fsdp_size, ctx_size = mesh.shape["fsdp"], mesh.shape["ctx"]
    everyone = fsdp_size * ctx_size
    rows_here, slots_all = images * local_slots, local_slots * ctx_size
    layers, block, _, cols = qkv_weight.shape
    units = up_weight.shape[2]
    slot_ids = lax.axis_index("ctx") * local_slots + jnp.arange(local_slots, dtype=jnp.int32)
    mask = (slot_ids[None, :] < lengths[:, None]).astype(F32).reshape(rows_here, 1)
    live = (jnp.arange(slots_all, dtype=jnp.int32)[None, :] < lengths[:, None]).astype(F32)
    vectors = jnp.stack((attn_gain, attn_shift, out_bias, mlp_gain, mlp_shift, down_bias), axis=1)
    flat = vectors.reshape(-1)
    small_rows = 16 * -(-flat.size // (16 * 2 * cols))
    small = jnp.pad(flat, (0, small_rows * 2 * cols - flat.size)).reshape(small_rows, 2 * cols)
    out_t = jnp.swapaxes(out_weight, 1, 2)
    down_t = jnp.swapaxes(down_weight, 1, 2)

    def own_parts(at):
        return jnp.stack(
            (
                qkv_weight[at, :, 0:2].reshape(block, 2 * cols),
                jnp.concatenate((qkv_weight[at, :, 2], out_t[at]), axis=1),
                up_weight[at, :, : units // 2],
                up_weight[at, :, units // 2 :],
                down_t[at, :, : units // 2],
                down_t[at, :, units // 2 :],
            )
        )

    whole, small_whole = gather_layer(mesh, own_parts(0), small)
    gathered = small_whole.reshape(everyone, small_rows * 2 * cols)[:, : flat.size]
    gathered = jnp.swapaxes(gathered.reshape(everyone, layers * 6, block), 0, 1)
    vectors = jnp.concatenate(
        (
            gathered.reshape(layers, 6, width),
            qv_bias.reshape(layers, 1, width),
            up_bias.reshape(layers, units // width, width),
        ),
        axis=1,
    ).astype(F32)
    vectors = jnp.pad(vectors, ((0, 0), (0, -vectors.shape[1] % 8), (0, 0)))

    stream = tokens.astype(F32).reshape(rows_here, width) * mask
    kept, weights = [], []
    for at in range(layers):
        weights.append(whole)
        next_own = own_parts(at + 1) if at + 1 < layers else None
        found = forward_layer(mesh, stream, mask, live, vectors[at], whole, next_own)
        kept.append((stream, *found[1:10]))
        stream = found[0]
        whole = found[-1]
    output = stream.astype(BF16).reshape(tokens.shape)
    grad = cotangent.astype(F32).reshape(rows_here, width)
    big, little = [None] * layers, [None] * layers
    last = None
    for at in reversed(range(layers)):
        found = backward_layer(mesh, grad, mask, live, vectors[at], kept[at], weights[at], last)
        grad = found[0]
        if last is not None:
            big[at + 1], little[at + 1] = found[3:]
        last = (found[2], found[1])
    big[0], little[0] = scatter_layer(mesh, *last)
    input_grad = (grad * mask).reshape(tokens.shape)
    big, little = jnp.stack(big), jnp.stack(little)
    here = (lax.axis_index("fsdp") * ctx_size + lax.axis_index("ctx")) * block
    own_vectors = lax.dynamic_slice_in_dim(little[:, :6], here, block, axis=2)
    grad_qkv = jnp.concatenate((big[:, 0], big[:, 1, :, :cols]), axis=2)
    return (
        output,
        input_grad,
        own_vectors[:, 0],
        own_vectors[:, 1],
        grad_qkv.reshape(layers, block, 3, cols),
        little[:, 6].reshape(layers, 2, cols),
        jnp.swapaxes(big[:, 1, :, cols:], 1, 2),
        own_vectors[:, 2],
        own_vectors[:, 3],
        own_vectors[:, 4],
        jnp.concatenate((big[:, 2], big[:, 3]), axis=2),
        little[:, 7 : 7 + units // width].reshape(layers, units),
        jnp.swapaxes(jnp.concatenate((big[:, 4], big[:, 5]), axis=2), 1, 2),
        own_vectors[:, 5],
    )


def solution(mesh):
    place = P(None, ("fsdp", "ctx"))
    rows = P("fsdp", "ctx", None)
    return jax.shard_map(
        functools.partial(body, mesh),
        mesh=mesh,
        in_specs=(
            rows,
            P("fsdp"),
            rows,
            place,
            place,
            P(None, ("fsdp", "ctx"), None, "tp"),
            P(None, None, "tp"),
            P(None, "tp", ("fsdp", "ctx")),
            place,
            place,
            place,
            P(None, ("fsdp", "ctx"), "tp"),
            P(None, "tp"),
            P(None, "tp", ("fsdp", "ctx")),
            place,
        ),
        out_specs=(
            rows,
            rows,
            place,
            place,
            P(None, ("fsdp", "ctx"), None, "tp"),
            P(None, None, "tp"),
            P(None, "tp", ("fsdp", "ctx")),
            place,
            place,
            place,
            P(None, ("fsdp", "ctx"), "tp"),
            P(None, "tp"),
            P(None, "tp", ("fsdp", "ctx")),
            place,
        ),
        check_vma=False,
    )
```

```python
import functools

import jax
import jax.numpy as jnp
from jax import lax
from jax.experimental import pallas as pl
from jax.experimental.pallas import tpu as pltpu
from jax.sharding import PartitionSpec as P

HEAD_DIM = 64
EPS = 1e-05
NEG = -30000.0
MESH = pl.DeviceIdType.MESH
PARTS = 6
BF16 = jnp.bfloat16
F32 = jnp.float32


def flip(index, bit):
    size = 2**bit
    return index + size - 2 * size * ((index // size) % 2)


def flip_all(index, bits):
    for bit in bits:
        index = flip(index, bit)
    return index


def subsets(bits):
    found = [()]
    for bit in bits:
        found = found + [entry + (bit,) for entry in found]
    return found


def orders(fsdp_size):
    top = fsdp_size.bit_length() - 1
    bits = list(range(1, top))
    half = len(bits) // 2
    return bits, bits[half:] + bits[:half]


class Link:
    def __init__(self, send_sem, recv_sem):
        self.send_sem, self.recv_sem, self.used, self.sent = send_sem, recv_sem, 0, []

    def push(self, src, dst, device):
        at = self.used
        self.used += 1
        copy = pltpu.make_async_remote_copy(
            src_ref=src,
            dst_ref=dst,
            send_sem=self.send_sem.at[at],
            recv_sem=self.recv_sem.at[at],
            device_id=device,
            device_id_type=MESH,
        )
        copy.start()
        self.sent.append(copy)
        return copy

    def settle(self, copies):
        for copy in copies:
            copy.wait_send()
            self.sent = [other for other in self.sent if other is not copy]

    def drain(self):
        for copy in self.sent:
            copy.wait_send()
        self.sent = []


def greet(fsdp_size, ctx_size, with_tp):
    me, ctx, tp = lax.axis_index("fsdp"), lax.axis_index("ctx"), lax.axis_index("tp")
    barrier = pltpu.get_barrier_semaphore()
    count = 0
    for bit in range(fsdp_size.bit_length() - 1):
        pl.semaphore_signal(
            barrier, inc=1, device_id={"fsdp": flip(me, bit)}, device_id_type=MESH
        )
        count += 1
    if ctx_size > 1:
        pl.semaphore_signal(barrier, inc=1, device_id={"ctx": 1 - ctx}, device_id_type=MESH)
        count += 1
    if with_tp:
        pl.semaphore_signal(barrier, inc=1, device_id={"tp": 1 - tp}, device_id_type=MESH)
        count += 1
    pl.semaphore_wait(barrier, count)


def rows_of(start, rows):
    return pl.ds(pl.multiple_of(start * rows, rows), rows)


def gather_pushes(fsdp_size, ctx_size):
    steps = fsdp_size.bit_length() - 2
    return (ctx_size - 1) + ctx_size * (2**steps - 1) + 2**steps


class Gather:
    def __init__(self, link, ctx_size, own, whole, block, order, local_sem):
        self.link, self.own, self.whole, self.block, self.order = link, own, whole, block, order
        self.ctx_size = ctx_size
        self.me, self.ctx = lax.axis_index("fsdp"), lax.axis_index("ctx")
        self.waits, self.crossed = {}, False
        self.stay = pltpu.make_async_copy(own, self.rows(self.me, self.ctx), local_sem)

    def rows(self, fsdp, ctx):
        return self.whole.at[rows_of(fsdp * self.ctx_size + ctx, self.block)]

    def spread(self, stream, step):
        ctx = self.ctx if stream == 0 else 1 - self.ctx
        bit = self.order[step]
        to = {"fsdp": flip(self.me, bit)}
        copies = []
        for entry in subsets(self.order[:step]):
            place = self.rows(flip_all(self.me, entry), ctx)
            source = self.own if (stream == 0 and not entry) else place
            copies.append(self.link.push(source, place, to))
        self.waits[stream, step] = copies

    def arrive(self, *key):
        for copy in self.waits.pop(key):
            copy.wait_recv()

    def cross(self):
        if not self.crossed:
            self.crossed = True
            self.waits["ctx",] = [
                self.link.push(self.own, self.rows(self.me, self.ctx), {"ctx": 1 - self.ctx})
            ]

    def start(self):
        self.stay.start()
        self.spread(0, 0)

    def next_step(self, stream, step):
        self.arrive(stream, step - 1)
        self.spread(stream, step)

    def other(self):
        self.cross()
        self.arrive("ctx")
        self.spread(1, 0)

    def core(self):
        last = len(self.order) - 1
        for stream in range(self.ctx_size):
            self.arrive(stream, last)
        self.stay.wait()
        both = self.block * self.ctx_size
        copies = []
        for entry in subsets(self.order):
            place = self.whole.at[rows_of(flip_all(self.me, entry), both)]
            copies.append(self.link.push(place, place, {"fsdp": flip(self.me, 0)}))
        self.waits["core",] = copies

    def finish(self):
        self.arrive("core")

    def events(self):
        found = [self.start]
        for step in range(1, len(self.order)):
            found.append(functools.partial(self.next_step, 0, step))
        if self.ctx_size > 1:
            found.append(self.other)
            for step in range(1, len(self.order)):
                found.append(functools.partial(self.next_step, 1, step))
        return found + [self.core, self.finish]


def in_step(first, second):
    def run(one, two):
        one()
        two()

    return [functools.partial(run, one, two) for one, two in zip(first, second)]


class Total:
    def __init__(self, link, fsdp_size, ctx_size, held, arrived):
        self.link, self.held, self.arrived = link, held, arrived
        me, ctx = lax.axis_index("fsdp"), lax.axis_index("ctx")
        self.partners = [{"fsdp": flip(me, bit)} for bit in range(fsdp_size.bit_length() - 1)]
        if ctx_size > 1:
            self.partners.append({"ctx": 1 - ctx})

    def step(self, at):
        if at > 0:
            self.copy.wait_recv()
            self.held[at] = self.held[at - 1] + self.arrived[at - 1]
        if at < len(self.partners):
            self.copy = self.link.push(self.held.at[at], self.arrived.at[at], self.partners[at])

    def events(self):
        return [functools.partial(self.step, at) for at in range(len(self.partners) + 1)]


def dot_nn(left, right):
    return lax.dot_general(left, right, (((1,), (0,)), ((), ())), preferred_element_type=F32)


def dot_nt(left, right):
    return lax.dot_general(left, right, (((1,), (1,)), ((), ())), preferred_element_type=F32)


def dot_tn(left, right):
    return lax.dot_general(left, right, (((0,), (0,)), ((), ())), preferred_element_type=F32)


TILE = 256
ROOT_HALF = 0.7071067811865476
ROOT_TWO_PI = 2.5066282746310002
VECTORS, BIASES, SMALL_ROWS = 6, 3, 16
PACE, SCATTER_PACE = 2, 2
GAIN_A, SHIFT_A, OUT_B, GAIN_B, SHIFT_B, DOWN_B, QV_B, UP_B = range(8)


def lanes(at, count):
    return pl.ds(pl.multiple_of(at * count, count), count)


def standardized(values):
    centered = values - jnp.mean(values, axis=-1, keepdims=True)
    scale = lax.rsqrt(jnp.mean(centered * centered, axis=-1, keepdims=True) + EPS)
    return centered * scale, scale


def send_pieces(link, partial, sent, got, pieces, partner):
    copies = []
    for at in range(pieces):
        sent[at] = partial(at).astype(BF16)
        copies.append(link.push(sent.at[at], got.at[at], partner))
    return copies


def both_halves(copies, sent, got):
    found = []
    for at, copy in enumerate(copies):
        copy.wait_recv()
        found.append(sent[at].astype(F32) + got[at].astype(F32))
    return jnp.concatenate(found, axis=1)


class Stream:
    def __init__(self):
        self.waiting, self.count, self.done = [], 0, set()

    def release(self, group, events, begin, pace=1):
        for place, event in enumerate(events):
            self.waiting.append((begin + place * pace, self.count, group, event))
            self.count += 1
        self.waiting.sort(key=lambda entry: entry[:2])
        self.last = {entry[2]: entry for entry in self.waiting}

    def __call__(self, count):
        for entry in self.waiting[:count]:
            entry[3]()
            if self.last[entry[2]] is entry:
                self.done.add(entry[2])
        self.waiting = self.waiting[count:]

    def need(self, group):
        while group not in self.done:
            self(1)

    def rest(self):
        self(len(self.waiting))


def forward_kernel(ctx_size, fsdp_size, *refs):
    (
        token_ref,
        mask_ref,
        live_ref,
        small_ref,
        bias_ref,
        own_ref,
        out_ref,
        vector_ref,
        stream_ref,
        query_ref,
        kv_out,
        log_total_ref,
        attended_ref,
        mid_ref,
        pre_ref,
        whole_ref,
        held,
        normed,
        hidden,
        kv,
        sent,
        got,
        small_held,
        small_got,
        send_sem,
        recv_sem,
        local_sem,
        load_sem,
        kv_sem,
    ) = refs
    layers, rows, width = stream_ref.shape
    cols = query_ref.shape[2]
    pieces = width // TILE
    pairs = PARTS // 2
    ctx = lax.axis_index("ctx")
    across = {"tp": 1 - lax.axis_index("tp")}
    greet(fsdp_size, ctx_size, True)
    link = Link(send_sem, recv_sem)
    pump = Stream()
    both = orders(fsdp_size)
    small_held[0] = small_ref[...]
    total = Total(link, fsdp_size, ctx_size, small_held, small_got)
    loads, gathers = {}, {}
    for layer in range(layers):
        for pair in range(pairs):
            found = [
                Gather(
                    link,
                    ctx_size,
                    own_ref.at[layer, part],
                    whole_ref.at[layer, part],
                    own_ref.shape[2],
                    both[part % 2],
                    local_sem.at[layer, part],
                )
                for part in (2 * pair, 2 * pair + 1)
            ]
            gathers[layer, pair] = found

            def bring(layer=layer, pair=pair):
                for part in (2 * pair, 2 * pair + 1):
                    copy = pltpu.make_async_copy(
                        whole_ref.at[layer, part],
                        held.at[layer % 2, part],
                        load_sem.at[layer % 2, part],
                    )
                    copy.start()
                    loads[layer, part] = copy

            events = in_step(*[gather.events() for gather in found]) + [bring]
            pump.release((layer, pair), events, PACE * (layer * pairs + pair))

    def cross(layer):
        if layer < layers and ctx_size > 1:
            for pair in range(pairs):
                for gather in gathers[layer, pair]:
                    gather.cross()

    def need(layer, pair):
        pump.need((layer, pair))
        for part in (2 * pair, 2 * pair + 1):
            loads[layer, part].wait()

    total.step(0)
    cross(0)
    for at in range(1, len(total.partners) + 1):
        pump(1)
        total.step(at)
    vector_ref[...] = small_held[len(total.partners)].astype(F32)
    mask = mask_ref[...]
    stream_ref[0] = mask * token_ref[...].astype(F32)
    mine = rows_of(ctx, rows)
    pair_cols = 2 * HEAD_DIM
    lane = lax.broadcasted_iota(jnp.int32, (rows, pair_cols), 1)
    first = lane < HEAD_DIM
    live = live_ref[...] > 0
    kv_saves = []
    log_total_ref[...] = jnp.zeros_like(log_total_ref)

    for layer in range(layers):
        slot = layer % 2

        def vector(which):
            at = layer * VECTORS + which
            return vector_ref[at : at + 1, :]

        def bias(which, at, slot_layer=layer):
            row = slot_layer * BIASES + which
            return bias_ref[row : row + 1, lanes(at, TILE)]

        normal, _ = standardized(stream_ref[layer])
        normed[...] = (normal * vector(GAIN_A) + vector(SHIFT_A)).astype(BF16)
        need(layer, 0)

        @pl.loop(0, cols // TILE)
        def _(at):
            rows_in = normed[...]
            kv[layer, mine, lanes(at, TILE)] = dot_nn(
                rows_in, held[slot, 0, :, lanes(at + cols // TILE, TILE)]
            ).astype(BF16)
            kv[layer, mine, lanes(at + cols // TILE, TILE)] = (
                dot_nn(rows_in, held[slot, 1, :, lanes(at, TILE)])
                + bias(0, at + cols // TILE)
            ).astype(BF16)

        kv_copy = None
        if ctx_size > 1:
            kv_copy = link.push(kv.at[layer, mine], kv.at[layer, mine], {"ctx": 1 - ctx})

        @pl.loop(0, cols // TILE)
        def _(at):
            query_ref[layer, :, lanes(at, TILE)] = (
                dot_nn(normed[...], held[slot, 0, :, lanes(at, TILE)]) + bias(0, at)
            ).astype(BF16)

        pump(3)
        if kv_copy is not None:
            kv_copy.wait_recv()
        cross(layer + 1)
        save = pltpu.make_async_copy(kv.at[layer], kv_out.at[layer], kv_sem.at[layer])
        save.start()
        kv_saves.append(save)

        for half in range(2):
            per_half = cols // pair_cols // 2

            @pl.loop(half * per_half, (half + 1) * per_half)
            def _(at):
                queries = query_ref[layer, :, lanes(at, pair_cols)]
                keys = kv[layer, :, lanes(at, pair_cols)]
                values = kv[layer, :, lanes(at + cols // pair_cols, pair_cols)]
                found = []
                for head in range(2):
                    chosen = jnp.where(
                        first if head == 0 else ~first, queries, jnp.zeros_like(queries)
                    )
                    scores = jnp.where(live, dot_nt(chosen, keys) * HEAD_DIM**-0.5, NEG)
                    top = jnp.max(scores, axis=-1, keepdims=True)
                    weights = jnp.exp(scores - top)
                    summed = jnp.sum(weights, axis=-1, keepdims=True)
                    log_total_ref[layer] = jnp.where(
                        lane == 2 * at + head, top + jnp.log(summed), log_total_ref[layer]
                    )
                    found.append(dot_nn((weights * (1.0 / summed)).astype(BF16), values))
                attended_ref[layer, :, lanes(at, pair_cols)] = jnp.where(
                    first, found[0], found[1]
                ).astype(BF16)

            pump(2)

        def out_partial(at):
            return dot_nt(attended_ref[layer], held[slot, 1, at * TILE : (at + 1) * TILE, cols:])

        copies = send_pieces(link, out_partial, sent.at[layer, 0], got.at[0], pieces, across)
        pump(2)
        branch = both_halves(copies, sent.at[layer, 0], got.at[0])
        mid = stream_ref[layer] + mask * (branch + vector(OUT_B))
        mid_ref[layer] = mid
        normal, _ = standardized(mid)
        normed[...] = (normal * vector(GAIN_B) + vector(SHIFT_B)).astype(BF16)
        need(layer, 1)
        for part in range(2):

            @pl.loop(0, pieces)
            def _(at):
                pre = dot_nn(normed[...], held[slot, 2 + part, :, lanes(at, TILE)]) + bias(
                    1 + part, at
                )
                pre_ref[layer, part, :, lanes(at, TILE)] = pre
                hidden[part, :, lanes(at, TILE)] = (
                    0.5 * pre * (1.0 + lax.erf(pre * ROOT_HALF))
                ).astype(BF16)

            pump(1)
        need(layer, 2)

        def down_partial(at):
            here = slice(at * TILE, (at + 1) * TILE)
            return dot_nt(hidden[0], held[slot, 4, here, :]) + dot_nt(
                hidden[1], held[slot, 5, here, :]
            )

        copies = send_pieces(link, down_partial, sent.at[layer, 1], got.at[1], pieces, across)
        pump(3)
        branch = both_halves(copies, sent.at[layer, 1], got.at[1])
        after = mid_ref[layer] + mask * (branch + vector(DOWN_B))
        if layer + 1 < layers:
            stream_ref[layer + 1] = after
        else:
            out_ref[...] = after.astype(BF16)
    pump.rest()
    link.drain()
    for save in kv_saves:
        save.wait()


def forward_all(mesh, tokens, mask, live, small, biases, own):
    fsdp_size, ctx_size = mesh.shape["fsdp"], mesh.shape["ctx"]
    rows, width = tokens.shape
    layers, _, block, part_cols = own.shape
    cols = width // mesh.shape["tp"]
    slots_all = rows * ctx_size
    pieces = width // TILE
    steps = fsdp_size.bit_length() - 1 + (ctx_size > 1)
    shape = jax.ShapeDtypeStruct
    whole = (layers, PARTS, width, part_cols)
    out_shape = [
        shape((rows, width), BF16),
        shape(small.shape, F32),
        shape((layers, rows, width), F32),
        shape((layers, rows, cols), BF16),
        shape((layers, slots_all, 2 * cols), BF16),
        shape((layers, rows, 2 * HEAD_DIM), F32),
        shape((layers, rows, cols), BF16),
        shape((layers, rows, width), F32),
        shape((layers, 2, rows, width), F32),
        shape(whole, BF16),
    ]
    vmem = pl.BlockSpec(memory_space=pltpu.VMEM)
    any_space = pl.BlockSpec(memory_space=pl.ANY)
    pushes = (
        layers * ((ctx_size > 1) + 2 * pieces + gather_pushes(fsdp_size, ctx_size) * PARTS) + steps
    )
    return pl.pallas_call(
        functools.partial(forward_kernel, ctx_size, fsdp_size),
        out_shape=out_shape,
        in_specs=[vmem] * 5 + [any_space],
        out_specs=[vmem] * 4 + [any_space] + [vmem] * 4 + [any_space],
        scratch_shapes=[
            pltpu.VMEM((2,) + whole[1:], BF16),
            pltpu.VMEM((rows, width), BF16),
            pltpu.VMEM((2, rows, width), BF16),
            pltpu.VMEM((layers, slots_all, 2 * cols), BF16),
            pltpu.VMEM((layers, 2, pieces, rows, TILE), BF16),
            pltpu.VMEM((2, pieces, rows, TILE), BF16),
            pltpu.VMEM((steps + 1,) + small.shape, BF16),
            pltpu.VMEM((steps,) + small.shape, BF16),
            pltpu.SemaphoreType.DMA((pushes,)),
            pltpu.SemaphoreType.DMA((pushes,)),
            pltpu.SemaphoreType.DMA((layers, PARTS)),
            pltpu.SemaphoreType.DMA((2, PARTS)),
            pltpu.SemaphoreType.DMA((layers,)),
        ],
        compiler_params=pltpu.CompilerParams(
            collective_id=0, has_side_effects=True, vmem_limit_bytes=60 * 2**20
        ),
        name="forward_all",
    )(tokens, mask, live, small, biases, own)


class Scatter:
    def __init__(self, link, ctx_size, terms, arrived, last, order, credits, first, final, write):
        self.link, self.terms, self.arrived, self.last = link, terms, arrived, last
        self.ctx_size, self.order, self.write = ctx_size, order, write
        self.credits, self.first, self.final = credits, first, final
        self.me, self.ctx = lax.axis_index("fsdp"), lax.axis_index("ctx")
        self.slots = 2 ** len(order)
        self.both = terms.shape[0] // (2 * self.slots)
        self.flips = [
            [bit for at, bit in enumerate(order) if (slot >> (len(order) - 1 - at)) % 2 == 1]
            for slot in range(self.slots)
        ]
        self.base, self.sent = 0, []

    def place(self, slot, core=0):
        start = flip(self.me, 0) if core else self.me
        return rows_of(flip_all(start, self.flips[slot]), self.both)

    def send(self, step, pieces, to):
        if not self.first:
            pl.semaphore_wait(self.credits.at[step], 1)
        self.copies = [self.link.push(src, dst, to) for src, dst in pieces]
        self.sent += self.copies

    def read(self, step, to):
        if not self.final:
            pl.semaphore_signal(
                self.credits.at[step], inc=1, device_id=to, device_id_type=MESH
            )

    def start(self):
        self.send(
            0,
            [
                (self.terms.at[self.place(slot, 1)], self.arrived.at[slot])
                for slot in range(self.slots)
            ],
            {"fsdp": flip(self.me, 0)},
        )

    def take(self, step, count, to):
        for copy in self.copies:
            copy.wait_recv()
        for slot in range(count):
            here = self.place(slot)
            self.terms[here, :] = self.terms[here, :] + self.arrived[self.base + slot]
        self.base += count
        self.read(step, to)

    def step(self, at):
        count = self.slots >> at
        self.take(at, count, {"fsdp": flip(self.me, 0 if at == 0 else self.order[at - 1])})
        half = count // 2
        self.send(
            at + 1,
            [
                (self.terms.at[self.place(half + slot)], self.arrived.at[self.base + slot])
                for slot in range(half)
            ],
            {"fsdp": flip(self.me, self.order[at])},
        )

    def across(self):
        steps = len(self.order)
        self.take(steps, 1, {"fsdp": flip(self.me, self.order[-1])})
        if self.ctx_size > 1:
            block = self.both // self.ctx_size
            theirs = rows_of(self.me * self.ctx_size + 1 - self.ctx, block)
            self.send(steps + 1, [(self.terms.at[theirs], self.last)], {"ctx": 1 - self.ctx})

    def finish(self):
        block = self.both // self.ctx_size
        total = self.terms[rows_of(self.me * self.ctx_size + self.ctx, block), :].astype(F32)
        if self.ctx_size > 1:
            for copy in self.copies:
                copy.wait_recv()
            total = total + self.last[...].astype(F32)
            self.read(len(self.order) + 1, {"ctx": 1 - self.ctx})
        self.write(total)
        self.link.settle(self.sent)

    def events(self):
        found = [self.start]
        for at in range(len(self.order)):
            found.append(functools.partial(self.step, at))
        return found + [self.across, self.finish]


def norm_pull(normal, scale, gain, grad):
    grad_gain = jnp.sum(grad * normal, axis=0, keepdims=True)
    grad_shift = jnp.sum(grad, axis=0, keepdims=True)
    inner = grad * gain
    along = jnp.mean(inner * normal, axis=-1, keepdims=True)
    grad_in = scale * (inner - jnp.mean(inner, axis=-1, keepdims=True) - normal * along)
    return grad_in, grad_gain, grad_shift


def backward_kernel(ctx_size, fsdp_size, *refs):
    (
        cotangent_ref,
        mask_ref,
        live_ref,
        vector_ref,
        stream_ref,
        query_ref,
        kv_ref,
        log_total_ref,
        attended_ref,
        mid_ref,
        pre_all,
        whole_ref,
        out_ref,
        summed_ref,
        small_ref,
        pre_ref,
        held,
        terms,
        arrived,
        last,
        turned,
        low,
        low_pre,
        hidden,
        grad_att,
        grad_qk,
        grad_kv,
        kv_sent,
        kv_got,
        sent,
        got,
        small_held,
        small_got,
        send_sem,
        recv_sem,
        load_sem,
        pre_sem,
        credits,
    ) = refs
    layers, rows, width = stream_ref.shape
    cols = query_ref.shape[2]
    pieces = width // TILE
    pairs = PARTS // 2
    ctx = lax.axis_index("ctx")
    across = {"tp": 1 - lax.axis_index("tp")}
    loads = {}

    def bring(layer, parts):
        if layer >= 0:
            for part in parts:
                copy = pltpu.make_async_copy(
                    whole_ref.at[layer, part], held.at[part], load_sem.at[part]
                )
                copy.start()
                loads[layer, part] = copy

    def bring_pre(layer):
        if layer >= 0:
            copy = pltpu.make_async_copy(
                pre_all.at[layer], pre_ref.at[layer % 2], pre_sem.at[layer % 2]
            )
            copy.start()
            loads[layer, "pre"] = copy

    bring_pre(layers - 1)
    bring(layers - 1, (4, 5, 2, 3, 1, 0))
    small_held[...] = jnp.zeros_like(small_held)
    greet(fsdp_size, ctx_size, True)
    link = Link(send_sem, recv_sem)
    pump = Stream()
    both = [order[::-1] for order in orders(fsdp_size)]
    mask = mask_ref[...]
    pair_cols = 2 * HEAD_DIM
    lane = lax.broadcasted_iota(jnp.int32, (rows, pair_cols), 1)
    first = lane < HEAD_DIM
    live = live_ref[...] > 0
    mine, theirs = rows_of(ctx, rows), rows_of(1 - ctx, rows)
    groups = 0
    last_sent = {}

    def scatter(layer, pair):
        nonlocal groups

        def writer(part):
            def write(value):
                summed_ref[layer, part] = value

            return write

        events = in_step(
            *[
                Scatter(
                    link,
                    ctx_size,
                    terms.at[part],
                    arrived.at[part],
                    last.at[part],
                    both[part % 2],
                    credits.at[part],
                    layer == layers - 1,
                    layer == 0,
                    writer(part),
                ).events()
                for part in (2 * pair, 2 * pair + 1)
            ]
        )
        pump.release((layer, pair), events, SCATTER_PACE * groups)
        groups += 1

    def free(layer, pair):
        if layer < layers - 1:
            pump.need((layer + 1, pair))

    def product(part, start, count, right):
        @pl.loop(0, count)
        def _(at):
            terms[part, :, lanes(at + start, TILE)] = dot_nn(turned[...], right(at)).astype(BF16)

    out_ref[...] = cotangent_ref[...].astype(F32)
    for layer in reversed(range(layers)):
        rows_small = small_held.at[layer, 0]

        def vector(which):
            at = layer * VECTORS + which
            return vector_ref[at : at + 1, :]

        def keep_row(which, value):
            rows_small[which : which + 1, :] = value

        bring_pre(layer - 1)
        grad = out_ref[...]
        masked = mask * grad
        keep_row(DOWN_B, jnp.sum(masked, axis=0, keepdims=True))
        low[...] = masked.astype(BF16)
        turned[...] = jnp.transpose(low[...])
        loads[layer, "pre"].wait()
        for part in range(2):
            loads[layer, 4 + part].wait()

            @pl.loop(0, pieces)
            def _(at):
                pre = pre_ref[layer % 2, part, :, lanes(at, TILE)]
                chance = 0.5 * (1.0 + lax.erf(pre * ROOT_HALF))
                hidden[part, :, lanes(at, TILE)] = (pre * chance).astype(BF16)
                slope = chance + pre * (jnp.exp(-0.5 * pre * pre) * (1.0 / ROOT_TWO_PI))
                grad_pre = dot_nn(low[...], held[4 + part, :, lanes(at, TILE)]) * slope
                rows_small[UP_B + part : UP_B + part + 1, lanes(at, TILE)] = jnp.sum(
                    grad_pre, axis=0, keepdims=True
                )
                low_pre[part, :, lanes(at, TILE)] = grad_pre.astype(BF16)

            pump(1)
        bring(layer - 1, (4, 5))
        for part in (2, 3):
            loads[layer, part].wait()

        def up_partial(at):
            here = slice(at * TILE, (at + 1) * TILE)
            return dot_nt(low_pre[0], held[2, here, :]) + dot_nt(low_pre[1], held[3, here, :])

        if layer < layers - 1:
            link.settle(last_sent["up"])
        copies = send_pieces(link, up_partial, sent.at[0], got.at[0], pieces, across)
        last_sent["up"] = copies
        bring(layer - 1, (2, 3))
        free(layer, 2)
        for part in range(2):
            product(4 + part, 0, pieces, lambda at, part=part: hidden[part, :, lanes(at, TILE)])
        scatter(layer, 2)
        pump(1)
        normal, scale = standardized(mid_ref[layer])
        turned[...] = jnp.transpose(
            (normal * vector(GAIN_B) + vector(SHIFT_B)).astype(BF16)
        )
        free(layer, 1)
        for part in range(2):
            product(2 + part, 0, pieces, lambda at, part=part: low_pre[part, :, lanes(at, TILE)])
        scatter(layer, 1)
        pump(1)
        grad_normed = both_halves(copies, sent.at[0], got.at[0])
        normal, scale = standardized(mid_ref[layer])
        grad_in, grad_gain, grad_shift = norm_pull(normal, scale, vector(GAIN_B), grad_normed)
        keep_row(GAIN_B, grad_gain)
        keep_row(SHIFT_B, grad_shift)
        grad_mid = out_ref[...] + grad_in
        out_ref[...] = grad_mid
        masked = mask * grad_mid
        keep_row(OUT_B, jnp.sum(masked, axis=0, keepdims=True))
        low[...] = masked.astype(BF16)
        loads[layer, 1].wait()

        @pl.loop(0, cols // TILE)
        def _(at):
            grad_att[:, lanes(at, TILE)] = dot_nn(
                low[...], held[1, :, lanes(at + cols // TILE, TILE)]
            ).astype(BF16)

        pump(1)
        for half in range(2):
            per_half = cols // pair_cols // 2

            @pl.loop(half * per_half, (half + 1) * per_half)
            def _(at):
                queries = query_ref[layer, :, lanes(at, pair_cols)]
                grads = grad_att[:, lanes(at, pair_cols)]
                keys = kv_ref[layer, :, lanes(at, pair_cols)]
                values = kv_ref[layer, :, lanes(at + cols // pair_cols, pair_cols)]
                found, key_grad, value_grad = [], None, None
                for head in range(2):
                    here = first if head == 0 else ~first
                    query = jnp.where(here, queries, jnp.zeros_like(queries))
                    one_grad = jnp.where(here, grads, jnp.zeros_like(grads))
                    scores = jnp.where(live, dot_nt(query, keys) * HEAD_DIM**-0.5, NEG)
                    log_total = jnp.sum(
                        jnp.where(lane == 2 * at + head, log_total_ref[layer], 0.0),
                        axis=-1,
                        keepdims=True,
                    )
                    weights = jnp.exp(scores - log_total)
                    grad_weights = dot_nt(one_grad, values)
                    along = jnp.sum(weights * grad_weights, axis=-1, keepdims=True)
                    grad_scores = (weights * (grad_weights - along)).astype(BF16)
                    found.append(dot_nn(grad_scores, keys))
                    one = dot_tn(grad_scores, query)
                    two = dot_tn(weights.astype(BF16), one_grad)
                    key_grad = one if head == 0 else key_grad + one
                    value_grad = two if head == 0 else value_grad + two
                grad_qk[:, lanes(at, pair_cols)] = (
                    jnp.where(first, found[0], found[1]) * HEAD_DIM**-0.5
                ).astype(BF16)
                grad_kv[:, lanes(at, pair_cols)] = key_grad * HEAD_DIM**-0.5
                grad_kv[:, lanes(at + cols // pair_cols, pair_cols)] = value_grad

            pump(2)
        kv_copy = None
        if ctx_size > 1:
            if layer < layers - 1:
                link.settle([last_sent["kv"]])
            kv_sent[...] = grad_kv[theirs, :].astype(BF16)
            kv_copy = link.push(kv_sent, kv_got.at[layer], {"ctx": 1 - ctx})
            last_sent["kv"] = kv_copy
        free(layer, 0)
        turned[...] = jnp.transpose(low[...])
        product(1, cols // TILE, cols // TILE, lambda at: attended_ref[layer, :, lanes(at, TILE)])
        normal, scale = standardized(stream_ref[layer])
        turned[...] = jnp.transpose(
            (normal * vector(GAIN_A) + vector(SHIFT_A)).astype(BF16)
        )
        product(0, 0, cols // TILE, lambda at: grad_qk[:, lanes(at, TILE)])
        pump(2)
        total_kv = grad_kv[mine, :]
        if kv_copy is not None:
            kv_copy.wait_recv()
            total_kv = total_kv + kv_got[layer].astype(F32)
        grad_qk[:, cols:] = total_kv.astype(BF16)
        rows_small[QV_B : QV_B + 1, :cols] = jnp.sum(
            grad_qk[:, :cols].astype(F32), axis=0, keepdims=True
        )
        rows_small[QV_B : QV_B + 1, cols:] = jnp.sum(
            grad_qk[:, 2 * cols :].astype(F32), axis=0, keepdims=True
        )
        loads[layer, 0].wait()

        def in_partial(at):
            here = slice(at * TILE, (at + 1) * TILE)
            return dot_nt(grad_qk[:, : 2 * cols], held[0, here, :]) + dot_nt(
                grad_qk[:, 2 * cols :], held[1, here, :cols]
            )

        if layer < layers - 1:
            link.settle(last_sent["in"])
        copies = send_pieces(link, in_partial, sent.at[1], got.at[1], pieces, across)
        last_sent["in"] = copies
        bring(layer - 1, (1, 0))
        product(
            0, cols // TILE, cols // TILE, lambda at: grad_qk[:, lanes(at + cols // TILE, TILE)]
        )
        product(1, 0, cols // TILE, lambda at: grad_qk[:, lanes(at + 2 * cols // TILE, TILE)])
        scatter(layer, 0)
        pump(2)
        grad_normed = both_halves(copies, sent.at[1], got.at[1])
        normal, scale = standardized(stream_ref[layer])
        grad_in, grad_gain, grad_shift = norm_pull(normal, scale, vector(GAIN_A), grad_normed)
        keep_row(GAIN_A, grad_gain)
        keep_row(SHIFT_A, grad_shift)
        grad = out_ref[...] + grad_in
        out_ref[...] = grad if layer > 0 else mask * grad
        total = Total(link, fsdp_size, ctx_size, small_held.at[layer], small_got.at[layer])
        pump.release(("small", layer), total.events(), SCATTER_PACE * (groups - 1))
    pump.rest()
    for layer in range(layers):
        small_ref[layer] = small_held[layer, small_held.shape[1] - 1]
    link.drain()


def backward_all(mesh, cotangent, mask, live, vectors, kept, whole):
    fsdp_size, ctx_size = mesh.shape["fsdp"], mesh.shape["ctx"]
    rows, width = cotangent.shape
    layers, _, _, part_cols = whole.shape
    cols = width // mesh.shape["tp"]
    slots_all = rows * ctx_size
    pieces = width // TILE
    slots = fsdp_size // 2
    both = width // fsdp_size
    block = both // ctx_size
    bits = fsdp_size.bit_length() - 1
    steps = bits + (ctx_size > 1)
    shape = jax.ShapeDtypeStruct
    vmem = pl.BlockSpec(memory_space=pltpu.VMEM)
    any_space = pl.BlockSpec(memory_space=pl.ANY)
    operands = [cotangent, mask, live, vectors, *kept, whole]
    pushes = layers * ((ctx_size > 1) + 2 * pieces + PARTS * (2 * slots) + steps)
    return pl.pallas_call(
        functools.partial(backward_kernel, ctx_size, fsdp_size),
        out_shape=[
            shape((rows, width), F32),
            shape((layers, PARTS, block, part_cols), F32),
            shape((layers, SMALL_ROWS, width), F32),
        ],
        in_specs=[vmem] * (len(operands) - 2) + [any_space] * 2,
        out_specs=[vmem] * 3,
        scratch_shapes=[
            pltpu.VMEM((2, 2, rows, width), F32),
            pltpu.VMEM(whole.shape[1:], BF16),
            pltpu.VMEM(whole.shape[1:], BF16),
            pltpu.VMEM((PARTS, 2 * slots - 1, both, part_cols), BF16),
            pltpu.VMEM((PARTS, block, part_cols), BF16),
            pltpu.VMEM((width, rows), BF16),
            pltpu.VMEM((rows, width), BF16),
            pltpu.VMEM((2, rows, width), BF16),
            pltpu.VMEM((2, rows, width), BF16),
            pltpu.VMEM((rows, cols), BF16),
            pltpu.VMEM((rows, 3 * cols), BF16),
            pltpu.VMEM((slots_all, 2 * cols), F32),
            pltpu.VMEM((rows, 2 * cols), BF16),
            pltpu.VMEM((layers, rows, 2 * cols), BF16),
            pltpu.VMEM((2, pieces, rows, TILE), BF16),
            pltpu.VMEM((2, pieces, rows, TILE), BF16),
            pltpu.VMEM((layers, steps + 1, SMALL_ROWS, width), F32),
            pltpu.VMEM((layers, steps, SMALL_ROWS, width), F32),
            pltpu.SemaphoreType.DMA((pushes,)),
            pltpu.SemaphoreType.DMA((pushes,)),
            pltpu.SemaphoreType.DMA((PARTS,)),
            pltpu.SemaphoreType.DMA((2,)),
            pltpu.SemaphoreType.REGULAR((PARTS, steps + 1)),
        ],
        compiler_params=pltpu.CompilerParams(
            collective_id=1, has_side_effects=True, vmem_limit_bytes=63 * 2**20
        ),
        name="backward_all",
    )(*operands)


def body(
    mesh,
    tokens,
    lengths,
    cotangent,
    attn_gain,
    attn_shift,
    qkv_weight,
    qv_bias,
    out_weight,
    out_bias,
    mlp_gain,
    mlp_shift,
    up_weight,
    up_bias,
    down_weight,
    down_bias,
):
    images, local_slots, width = tokens.shape
    ctx_size = mesh.shape["ctx"]
    rows_here, slots_all = images * local_slots, local_slots * ctx_size
    layers, block, _, cols = qkv_weight.shape
    units = up_weight.shape[2]
    slot_ids = lax.axis_index("ctx") * local_slots + jnp.arange(local_slots, dtype=jnp.int32)
    mask = (slot_ids[None, :] < lengths[:, None]).astype(F32).reshape(rows_here, 1)
    live = (jnp.arange(slots_all, dtype=jnp.int32)[None, :] < lengths[:, None]).astype(F32)
    vectors = jnp.stack((attn_gain, attn_shift, out_bias, mlp_gain, mlp_shift, down_bias), axis=1)
    vectors = vectors.reshape(layers * VECTORS, block)
    here = (lax.axis_index("fsdp") * ctx_size + lax.axis_index("ctx")) * block
    small = lax.dynamic_update_slice(
        jnp.zeros((-(-vectors.shape[0] // 16) * 16, width), BF16), vectors, (0, here)
    )
    biases = jnp.concatenate(
        (qv_bias.reshape(layers, 1, width), up_bias.reshape(layers, units // width, width)), axis=1
    ).reshape(layers * BIASES, width)
    biases = jnp.pad(biases.astype(F32), ((0, -biases.shape[0] % 8), (0, 0)))
    out_t = jnp.swapaxes(out_weight, 1, 2)
    down_t = jnp.swapaxes(down_weight, 1, 2)
    own = jnp.stack(
        (
            qkv_weight[:, :, 0:2].reshape(layers, block, 2 * cols),
            jnp.concatenate((qkv_weight[:, :, 2], out_t), axis=2),
            up_weight[:, :, : units // 2],
            up_weight[:, :, units // 2 :],
            down_t[:, :, : units // 2],
            down_t[:, :, units // 2 :],
        ),
        axis=1,
    )
    found = forward_all(
        mesh, tokens.reshape(rows_here, width), mask, live, small, biases, own
    )
    output, vectors, *kept, whole = found
    output = output.reshape(tokens.shape)
    grad, big, little = backward_all(
        mesh, cotangent.reshape(rows_here, width), mask, live, vectors, kept, whole
    )
    input_grad = grad.reshape(tokens.shape)
    own_vectors = lax.dynamic_slice_in_dim(little[:, :6], here, block, axis=2)
    grad_qkv = jnp.concatenate((big[:, 0], big[:, 1, :, :cols]), axis=2)
    return (
        output,
        input_grad,
        own_vectors[:, 0],
        own_vectors[:, 1],
        grad_qkv.reshape(layers, block, 3, cols),
        little[:, 6].reshape(layers, 2, cols),
        jnp.swapaxes(big[:, 1, :, cols:], 1, 2),
        own_vectors[:, 2],
        own_vectors[:, 3],
        own_vectors[:, 4],
        jnp.concatenate((big[:, 2], big[:, 3]), axis=2),
        little[:, 7 : 7 + units // width].reshape(layers, units),
        jnp.swapaxes(jnp.concatenate((big[:, 4], big[:, 5]), axis=2), 1, 2),
        own_vectors[:, 5],
    )


def solution(mesh):
    place = P(None, ("fsdp", "ctx"))
    rows = P("fsdp", "ctx", None)
    return jax.shard_map(
        functools.partial(body, mesh),
        mesh=mesh,
        in_specs=(
            rows,
            P("fsdp"),
            rows,
            place,
            place,
            P(None, ("fsdp", "ctx"), None, "tp"),
            P(None, None, "tp"),
            P(None, "tp", ("fsdp", "ctx")),
            place,
            place,
            place,
            P(None, ("fsdp", "ctx"), "tp"),
            P(None, "tp"),
            P(None, "tp", ("fsdp", "ctx")),
            place,
        ),
        out_specs=(
            rows,
            rows,
            place,
            place,
            P(None, ("fsdp", "ctx"), None, "tp"),
            P(None, None, "tp"),
            P(None, "tp", ("fsdp", "ctx")),
            place,
            place,
            place,
            P(None, ("fsdp", "ctx"), "tp"),
            P(None, "tp"),
            P(None, "tp", ("fsdp", "ctx")),
            place,
        ),
        check_vma=False,
    )
```

```python
import functools

import jax
import jax.numpy as jnp
from jax import lax
from jax.experimental import pallas as pl
from jax.experimental.pallas import tpu as pltpu
from jax.sharding import PartitionSpec as P

HEAD_DIM = 64
EPS = 1e-05
NEG = -30000.0
MESH = pl.DeviceIdType.MESH
PARTS = 6
BF16 = jnp.bfloat16
F32 = jnp.float32


def flip(index, bit):
    size = 2**bit
    return index + size - 2 * size * ((index // size) % 2)


def flip_all(index, bits):
    for bit in bits:
        index = flip(index, bit)
    return index


def subsets(bits):
    found = [()]
    for bit in bits:
        found = found + [entry + (bit,) for entry in found]
    return found


def orders(fsdp_size):
    top = fsdp_size.bit_length() - 1
    bits = list(range(1, top))
    half = len(bits) // 2
    return bits, bits[half:] + bits[:half]


class Link:
    def __init__(self, send_sem, recv_sem):
        self.send_sem, self.recv_sem, self.used, self.sent = send_sem, recv_sem, 0, []

    def push(self, src, dst, device):
        at = self.used
        self.used += 1
        copy = pltpu.make_async_remote_copy(
            src_ref=src,
            dst_ref=dst,
            send_sem=self.send_sem.at[at],
            recv_sem=self.recv_sem.at[at],
            device_id=device,
            device_id_type=MESH,
        )
        copy.start()
        self.sent.append(copy)
        return copy

    def settle(self, copies):
        for copy in copies:
            copy.wait_send()
            self.sent = [other for other in self.sent if other is not copy]

    def drain(self):
        for copy in self.sent:
            copy.wait_send()
        self.sent = []


def greet(fsdp_size, ctx_size, with_tp):
    me, ctx, tp = lax.axis_index("fsdp"), lax.axis_index("ctx"), lax.axis_index("tp")
    barrier = pltpu.get_barrier_semaphore()
    count = 0
    for bit in range(fsdp_size.bit_length() - 1):
        pl.semaphore_signal(
            barrier, inc=1, device_id={"fsdp": flip(me, bit)}, device_id_type=MESH
        )
        count += 1
    if ctx_size > 1:
        pl.semaphore_signal(barrier, inc=1, device_id={"ctx": 1 - ctx}, device_id_type=MESH)
        count += 1
    if with_tp:
        pl.semaphore_signal(barrier, inc=1, device_id={"tp": 1 - tp}, device_id_type=MESH)
        count += 1
    pl.semaphore_wait(barrier, count)


def rows_of(start, rows):
    return pl.ds(pl.multiple_of(start * rows, rows), rows)


def gather_pushes(fsdp_size, ctx_size):
    steps = fsdp_size.bit_length() - 2
    return (ctx_size - 1) + ctx_size * (2**steps - 1) + 2**steps


class Gather:
    def __init__(self, link, ctx_size, whole, block, order):
        self.link, self.whole, self.block, self.order = link, whole, block, order
        self.ctx_size = ctx_size
        self.me, self.ctx = lax.axis_index("fsdp"), lax.axis_index("ctx")
        self.waits, self.crossed, self.after = {}, False, None

    def rows(self, fsdp, ctx):
        return self.whole.at[rows_of(fsdp * self.ctx_size + ctx, self.block)]

    def spread(self, stream, step):
        ctx = self.ctx if stream == 0 else 1 - self.ctx
        bit = self.order[step]
        to = {"fsdp": flip(self.me, bit)}
        copies = []
        for entry in subsets(self.order[:step]):
            place = self.rows(flip_all(self.me, entry), ctx)
            copies.append(self.link.push(place, place, to))
        self.waits[stream, step] = copies

    def arrive(self, *key):
        for copy in self.waits.pop(key):
            copy.wait_recv()

    def cross(self):
        if not self.crossed:
            self.crossed = True
            own = self.rows(self.me, self.ctx)
            self.waits["ctx",] = [
                self.link.push(own, own, {"ctx": 1 - self.ctx})
            ]

    def start(self):
        self.spread(0, 0)

    def next_step(self, stream, step):
        self.arrive(stream, step - 1)
        self.spread(stream, step)

    def other(self):
        self.cross()
        self.arrive("ctx")
        if self.after is not None:
            self.after.cross()
        self.spread(1, 0)

    def core(self):
        last = len(self.order) - 1
        for stream in range(self.ctx_size):
            self.arrive(stream, last)
        both = self.block * self.ctx_size
        copies = []
        for entry in subsets(self.order):
            place = self.whole.at[rows_of(flip_all(self.me, entry), both)]
            copies.append(self.link.push(place, place, {"fsdp": flip(self.me, 0)}))
        self.waits["core",] = copies

    def finish(self):
        self.arrive("core")

    def events(self):
        found = [self.start]
        for step in range(1, len(self.order)):
            found.append(functools.partial(self.next_step, 0, step))
        if self.ctx_size > 1:
            found.append(self.other)
            for step in range(1, len(self.order)):
                found.append(functools.partial(self.next_step, 1, step))
        return found + [self.core, self.finish]


def in_step(first, second):
    def run(one, two):
        one()
        two()

    return [functools.partial(run, one, two) for one, two in zip(first, second)]


class Total:
    def __init__(self, link, fsdp_size, ctx_size, held, arrived):
        self.link, self.held, self.arrived = link, held, arrived
        me, ctx = lax.axis_index("fsdp"), lax.axis_index("ctx")
        self.partners = [{"fsdp": flip(me, bit)} for bit in range(fsdp_size.bit_length() - 1)]
        if ctx_size > 1:
            self.partners.append({"ctx": 1 - ctx})

    def step(self, at):
        if at > 0:
            self.copy.wait_recv()
            self.held[at] = self.held[at - 1] + self.arrived[at - 1]
        if at < len(self.partners):
            self.copy = self.link.push(self.held.at[at], self.arrived.at[at], self.partners[at])

    def events(self):
        return [functools.partial(self.step, at) for at in range(len(self.partners) + 1)]


def dot_nn(left, right):
    return lax.dot_general(left, right, (((1,), (0,)), ((), ())), preferred_element_type=F32)


def dot_nt(left, right):
    return lax.dot_general(left, right, (((1,), (1,)), ((), ())), preferred_element_type=F32)


def dot_tn(left, right):
    return lax.dot_general(left, right, (((0,), (0,)), ((), ())), preferred_element_type=F32)


TILE = 256
ROOT_HALF = 0.7071067811865476
ROOT_TWO_PI = 2.5066282746310002
VECTORS, BIASES, SMALL_ROWS = 6, 3, 16
PACE, SCATTER_PACE = 1.25, 1
FP = ((3, 2, 2, 2, 1, 1, 3), (3, 2, 2, 2, 1, 1, 3), (3, 2, 2, 2, 1, 1, 3))
BP = ((1, 1, 1, 1, 1, 1, 2, 1, 1, 1), (1, 1, 1, 1, 1, 1, 2, 1, 1, 1), (0, 0, 1, 1, 0, 0, 1, 1, 1, 1))
GAIN_A, SHIFT_A, OUT_B, GAIN_B, SHIFT_B, DOWN_B, QV_B, UP_B = range(8)


def lanes(at, count):
    return pl.ds(pl.multiple_of(at * count, count), count)


def standardized(values):
    centered = values - jnp.mean(values, axis=-1, keepdims=True)
    scale = lax.rsqrt(jnp.mean(centered * centered, axis=-1, keepdims=True) + EPS)
    return centered * scale, scale


def send_pieces(link, partial, sent, got, pieces, partner):
    copies = []
    for at in range(pieces):
        sent[at] = partial(at).astype(BF16)
        copies.append(link.push(sent.at[at], got.at[at], partner))
    return copies


def both_halves(copies, sent, got):
    found = []
    for at, copy in enumerate(copies):
        copy.wait_recv()
        found.append(sent[at].astype(F32) + got[at].astype(F32))
    return jnp.concatenate(found, axis=1)


class Stream:
    def __init__(self):
        self.waiting, self.count, self.done = [], 0, set()

    def release(self, group, events, begin, pace=1):
        for place, event in enumerate(events):
            self.waiting.append((begin + place * pace, self.count, group, event))
            self.count += 1
        self.waiting.sort(key=lambda entry: entry[:2])
        self.last = {entry[2]: entry for entry in self.waiting}

    def __call__(self, count):
        for entry in self.waiting[:count]:
            entry[3]()
            if self.last[entry[2]] is entry:
                self.done.add(entry[2])
        self.waiting = self.waiting[count:]

    def need(self, group):
        while group not in self.done:
            self(1)

    def rest(self):
        self(len(self.waiting))


def forward_kernel(ctx_size, fsdp_size, *refs):
    token_ref, mask_ref, live_ref = refs[:3]
    own_vectors = refs[3 : 3 + VECTORS]
    qv_ref, up_bias_ref, qkv_ref, out_weight_ref, up_ref, down_ref = refs[3 + VECTORS : 9 + VECTORS]
    (
        out_ref,
        vector_ref,
        stream_ref,
        query_ref,
        kv_out,
        log_total_ref,
        attended_ref,
        mid_ref,
        pre_out,
        whole_ref,
        held,
        pre_ref,
        normed,
        hidden,
        kv,
        sent,
        got,
        small_held,
        small_got,
        send_sem,
        recv_sem,
        save_sem,
        kv_sem,
        pre_sem,
    ) = refs[9 + VECTORS :]
    layers, rows, width = stream_ref.shape
    cols = query_ref.shape[2]
    pieces = width // TILE
    pairs = PARTS // 2
    ctx = lax.axis_index("ctx")
    across = {"tp": 1 - lax.axis_index("tp")}
    greet(fsdp_size, ctx_size, True)
    link = Link(send_sem, recv_sem)
    pump = Stream()
    both = orders(fsdp_size)
    block = up_ref.shape[1]
    me = lax.axis_index("fsdp") * ctx_size + ctx
    here = rows_of(me, block)
    for layer in range(layers):
        for at in range(3):
            place = slice(at % 2 * cols, (at % 2 + 1) * cols)
            held[layer, at // 2, here, place] = qkv_ref[layer, at]
        held[layer, 1, here, cols:] = out_weight_ref[layer]
        for half in range(2):
            columns = slice(half * width, (half + 1) * width)
            held[layer, 2 + half, here, :] = up_ref[layer, :, columns]
            held[layer, 4 + half, here, :] = down_ref[layer, :, columns]
    shift = lax.broadcasted_iota(jnp.int32, (block, width), 0) + me * block
    shift = (shift == lax.broadcasted_iota(jnp.int32, (block, width), 1)).astype(BF16)
    placed = [dot_nn(vector[...], shift) for vector in own_vectors]
    unused = small_held.shape[1] - VECTORS * layers
    placed.append(jnp.zeros((unused, width), F32))
    small_held[0] = jnp.concatenate(placed, axis=0).astype(BF16)
    total = Total(link, fsdp_size, ctx_size, small_held, small_got)
    gathers, previous, keeps, saves, pre_saves, groups = (), (), {}, [], {}, 0
    for layer in range(layers):
        for pair in range(pairs):
            found = [
                Gather(
                    link,
                    ctx_size,
                    held.at[layer, part],
                    block,
                    both[part % 2],
                )
                for part in (2 * pair, 2 * pair + 1)
            ]
            for gather, before in zip(found, previous):
                before.after = gather
            previous = found
            if not gathers:
                gathers = found

            def keep(layer=layer, pair=pair):
                for part in (2 * pair, 2 * pair + 1):
                    copy = pltpu.make_async_copy(
                        held.at[layer, part], whole_ref.at[layer, part], save_sem.at[layer, part]
                    )
                    copy.start()
                    saves.append(copy)

            events = in_step(*[gather.events() for gather in found])
            pump.release((layer, pair), events, PACE * groups)
            keeps[layer, pair] = keep
            groups += 1

    def need(layer, pair):
        pump.need((layer, pair))
        keeps[layer, pair]()

    total.step(0)
    for gather in gathers:
        gather.cross()
    for at in range(1, len(total.partners) + 1):
        pump(1)
        total.step(at)
    vector_ref[...] = small_held[len(total.partners)].astype(F32)
    mask = mask_ref[...]
    stream_ref[0] = mask * token_ref[...].astype(F32)
    mine = rows_of(ctx, rows)
    pair_cols = 2 * HEAD_DIM
    lane = lax.broadcasted_iota(jnp.int32, (rows, pair_cols), 1)
    first = lane < HEAD_DIM
    live = live_ref[...] > 0
    log_total_ref[...] = jnp.zeros_like(log_total_ref)

    for layer in range(layers):
        def vector(which):
            at = which * layers + layer
            return vector_ref[at : at + 1, :]

        normal, _ = standardized(stream_ref[layer])
        normed[...] = (normal * vector(GAIN_A) + vector(SHIFT_A)).astype(BF16)
        need(layer, 0)

        @pl.loop(0, cols // TILE)
        def _(at):
            rows_in = normed[...]
            kv[layer, mine, lanes(at, TILE)] = dot_nn(
                rows_in, held[layer, 0, :, lanes(at + cols // TILE, TILE)]
            ).astype(BF16)
            kv[layer, mine, lanes(at + cols // TILE, TILE)] = (
                dot_nn(rows_in, held[layer, 1, :, lanes(at, TILE)])
                + qv_ref[layer, 1:2, lanes(at, TILE)].astype(F32)
            ).astype(BF16)

        kv_copy = None
        if ctx_size > 1:
            kv_copy = link.push(kv.at[layer, mine], kv.at[layer, mine], {"ctx": 1 - ctx})

        @pl.loop(0, cols // TILE)
        def _(at):
            query_ref[layer, :, lanes(at, TILE)] = (
                dot_nn(normed[...], held[layer, 0, :, lanes(at, TILE)]) + qv_ref[layer, 0:1, lanes(at, TILE)].astype(F32)
            ).astype(BF16)

        pump(FP[layer][0])
        if kv_copy is not None:
            kv_copy.wait_recv()
        save = pltpu.make_async_copy(kv.at[layer], kv_out.at[layer], kv_sem.at[layer])
        save.start()
        saves.append(save)

        for half in range(2):
            per_half = cols // pair_cols // 2

            @pl.loop(half * per_half, (half + 1) * per_half)
            def _(at):
                queries = query_ref[layer, :, lanes(at, pair_cols)]
                keys = kv[layer, :, lanes(at, pair_cols)]
                values = kv[layer, :, lanes(at + cols // pair_cols, pair_cols)]
                found = []
                for head in range(2):
                    chosen = jnp.where(
                        first if head == 0 else ~first, queries, jnp.zeros_like(queries)
                    )
                    scores = jnp.where(live, dot_nt(chosen, keys) * HEAD_DIM**-0.5, NEG)
                    top = jnp.max(scores, axis=-1, keepdims=True)
                    weights = jnp.exp(scores - top)
                    summed = jnp.sum(weights, axis=-1, keepdims=True)
                    log_total_ref[layer] = jnp.where(
                        lane == 2 * at + head, top + jnp.log(summed), log_total_ref[layer]
                    )
                    found.append(dot_nn((weights * (1.0 / summed)).astype(BF16), values))
                attended_ref[layer, :, lanes(at, pair_cols)] = jnp.where(
                    first, found[0], found[1]
                ).astype(BF16)

            pump(FP[layer][1 + half])

        def out_partial(at):
            return dot_nt(attended_ref[layer], held[layer, 1, at * TILE : (at + 1) * TILE, cols:])

        copies = send_pieces(link, out_partial, sent.at[layer, 0], got.at[0], pieces, across)
        pump(FP[layer][3])
        branch = both_halves(copies, sent.at[layer, 0], got.at[0])
        mid = stream_ref[layer] + mask * (branch + vector(OUT_B))
        mid_ref[layer] = mid
        normal, _ = standardized(mid)
        normed[...] = (normal * vector(GAIN_B) + vector(SHIFT_B)).astype(BF16)
        need(layer, 1)
        if layer >= 2:
            pre_saves.pop(layer - 2).wait()
        for part in range(2):

            @pl.loop(0, pieces)
            def _(at):
                pre = dot_nn(normed[...], held[layer, 2 + part, :, lanes(at, TILE)]) + up_bias_ref[
                    layer : layer + 1, lanes(at + part * pieces, TILE)
                ].astype(F32)
                pre_ref[layer % 2, part, :, lanes(at, TILE)] = pre
                hidden[part, :, lanes(at, TILE)] = (
                    0.5 * pre * (1.0 + lax.erf(pre * ROOT_HALF))
                ).astype(BF16)

            pump(FP[layer][4 + part])
        pre_saves[layer] = pltpu.make_async_copy(
            pre_ref.at[layer % 2], pre_out.at[layer], pre_sem.at[layer]
        )
        pre_saves[layer].start()
        need(layer, 2)

        def down_partial(at):
            here = slice(at * TILE, (at + 1) * TILE)
            return dot_nt(hidden[0], held[layer, 4, here, :]) + dot_nt(
                hidden[1], held[layer, 5, here, :]
            )

        copies = send_pieces(link, down_partial, sent.at[layer, 1], got.at[1], pieces, across)
        pump(FP[layer][6])
        branch = both_halves(copies, sent.at[layer, 1], got.at[1])
        after = mid_ref[layer] + mask * (branch + vector(DOWN_B))
        if layer + 1 < layers:
            stream_ref[layer + 1] = after
        else:
            out_ref[...] = after.astype(BF16)
    pump.rest()
    link.drain()
    for save in (*saves, *pre_saves.values()):
        save.wait()


def forward_all(mesh, tokens, mask, live, own_vectors, qv_bias, up_bias, qkv, out_t, up, down_t):
    fsdp_size, ctx_size = mesh.shape["fsdp"], mesh.shape["ctx"]
    rows, width = tokens.shape
    layers, _, _, cols = qkv.shape
    part_cols = 2 * cols
    small = (-(-VECTORS * layers // 16) * 16, width)
    slots_all = rows * ctx_size
    pieces = width // TILE
    steps = fsdp_size.bit_length() - 1 + (ctx_size > 1)
    shape = jax.ShapeDtypeStruct
    whole = (layers, PARTS, width, part_cols)
    out_shape = [
        shape((rows, width), BF16),
        shape(small, F32),
        shape((layers, rows, width), F32),
        shape((layers, rows, cols), BF16),
        shape((layers, slots_all, 2 * cols), BF16),
        shape((layers, rows, 2 * HEAD_DIM), F32),
        shape((layers, rows, cols), BF16),
        shape((layers, rows, width), F32),
        shape((layers, 2, rows, width), F32),
        shape(whole, BF16),
    ]
    vmem = pl.BlockSpec(memory_space=pltpu.VMEM)
    any_space = pl.BlockSpec(memory_space=pl.ANY)
    pushes = (
        layers * ((ctx_size > 1) + 2 * pieces + gather_pushes(fsdp_size, ctx_size) * PARTS)
        + steps
    )
    return pl.pallas_call(
        functools.partial(forward_kernel, ctx_size, fsdp_size),
        out_shape=out_shape,
        in_specs=[vmem] * (9 + VECTORS),
        out_specs=[vmem] * 4 + [any_space] + [vmem] * 3 + [any_space] * 2,
        scratch_shapes=[
            pltpu.VMEM(whole, BF16),
            pltpu.VMEM((2, 2, rows, width), F32),
            pltpu.VMEM((rows, width), BF16),
            pltpu.VMEM((2, rows, width), BF16),
            pltpu.VMEM((layers, slots_all, 2 * cols), BF16),
            pltpu.VMEM((layers, 2, pieces, rows, TILE), BF16),
            pltpu.VMEM((2, pieces, rows, TILE), BF16),
            pltpu.VMEM((steps + 1,) + small, BF16),
            pltpu.VMEM((steps,) + small, BF16),
            pltpu.SemaphoreType.DMA((pushes,)),
            pltpu.SemaphoreType.DMA((pushes,)),
            pltpu.SemaphoreType.DMA((layers, PARTS)),
            pltpu.SemaphoreType.DMA((layers,)),
            pltpu.SemaphoreType.DMA((layers,)),
        ],
        compiler_params=pltpu.CompilerParams(
            collective_id=0, has_side_effects=True, vmem_limit_bytes=63 * 2**20
        ),
        name="forward_all",
    )(tokens, mask, live, *own_vectors, qv_bias, up_bias, qkv, out_t, up, down_t)


class Scatter:
    def __init__(self, link, ctx_size, terms, arrived, last, order, credits, first, final, write):
        self.link, self.terms, self.arrived, self.last = link, terms, arrived, last
        self.ctx_size, self.order, self.write = ctx_size, order, write
        self.credits, self.first, self.final = credits, first, final
        self.me, self.ctx = lax.axis_index("fsdp"), lax.axis_index("ctx")
        self.slots = 2 ** len(order)
        self.both = terms.shape[0] // (2 * self.slots)
        self.flips = [
            [bit for at, bit in enumerate(order) if (slot >> (len(order) - 1 - at)) % 2 == 1]
            for slot in range(self.slots)
        ]
        self.base, self.sent = 0, []

    def place(self, slot, core=0):
        start = flip(self.me, 0) if core else self.me
        return rows_of(flip_all(start, self.flips[slot]), self.both)

    def send(self, step, pieces, to):
        if not self.first:
            pl.semaphore_wait(self.credits.at[step], 1)
        self.copies = [self.link.push(src, dst, to) for src, dst in pieces]
        self.sent += self.copies

    def read(self, step, to):
        if not self.final:
            pl.semaphore_signal(
                self.credits.at[step], inc=1, device_id=to, device_id_type=MESH
            )

    def start(self):
        self.send(
            0,
            [
                (self.terms.at[self.place(slot, 1)], self.arrived.at[slot])
                for slot in range(self.slots)
            ],
            {"fsdp": flip(self.me, 0)},
        )

    def take(self, step, count, to):
        for copy in self.copies:
            copy.wait_recv()
        for slot in range(count):
            here = self.place(slot)
            self.terms[here, :] = self.terms[here, :] + self.arrived[self.base + slot]
        self.base += count
        self.read(step, to)

    def step(self, at):
        count = self.slots >> at
        self.take(at, count, {"fsdp": flip(self.me, 0 if at == 0 else self.order[at - 1])})
        half = count // 2
        self.send(
            at + 1,
            [
                (self.terms.at[self.place(half + slot)], self.arrived.at[self.base + slot])
                for slot in range(half)
            ],
            {"fsdp": flip(self.me, self.order[at])},
        )

    def across(self):
        steps = len(self.order)
        self.take(steps, 1, {"fsdp": flip(self.me, self.order[-1])})
        if self.ctx_size > 1:
            block = self.both // self.ctx_size
            theirs = rows_of(self.me * self.ctx_size + 1 - self.ctx, block)
            self.send(steps + 1, [(self.terms.at[theirs], self.last)], {"ctx": 1 - self.ctx})

    def finish(self):
        block = self.both // self.ctx_size
        total = self.terms[rows_of(self.me * self.ctx_size + self.ctx, block), :].astype(F32)
        if self.ctx_size > 1:
            for copy in self.copies:
                copy.wait_recv()
            total = total + self.last[...].astype(F32)
            self.read(len(self.order) + 1, {"ctx": 1 - self.ctx})
        self.write(total)
        self.link.settle(self.sent)

    def events(self):
        found = [self.start]
        for at in range(len(self.order)):
            found.append(functools.partial(self.step, at))
        return found + [self.across, self.finish]


def norm_pull(normal, scale, gain, grad):
    grad_gain = jnp.sum(grad * normal, axis=0, keepdims=True)
    grad_shift = jnp.sum(grad, axis=0, keepdims=True)
    inner = grad * gain
    along = jnp.mean(inner * normal, axis=-1, keepdims=True)
    grad_in = scale * (inner - jnp.mean(inner, axis=-1, keepdims=True) - normal * along)
    return grad_in, grad_gain, grad_shift


def backward_kernel(ctx_size, fsdp_size, *refs):
    (
        cotangent_ref,
        mask_ref,
        live_ref,
        vector_ref,
        stream_ref,
        query_ref,
        kv_ref,
        log_total_ref,
        attended_ref,
        mid_ref,
        pre_all,
        whole_ref,
        out_ref,
        qkv_ref,
        out_weight_ref,
        up_ref,
        down_ref,
        small_ref,
        pre_ref,
        held,
        terms,
        arrived,
        last,
        turned,
        low,
        low_pre,
        hidden,
        grad_att,
        grad_qk,
        grad_kv,
        kv_sent,
        kv_got,
        sent,
        got,
        small_held,
        small_got,
        send_sem,
        recv_sem,
        load_sem,
        pre_sem,
        credits,
    ) = refs
    layers, rows, width = stream_ref.shape
    cols = query_ref.shape[2]
    pieces = width // TILE
    pairs = PARTS // 2
    ctx = lax.axis_index("ctx")
    across = {"tp": 1 - lax.axis_index("tp")}
    loads = {}

    def bring(layer, parts):
        if layer >= 0:
            for part in parts:
                copy = pltpu.make_async_copy(
                    whole_ref.at[layer, part], held.at[part], load_sem.at[part]
                )
                copy.start()
                loads[layer, part] = copy

    def bring_pre(layer):
        if layer >= 0:
            copy = pltpu.make_async_copy(
                pre_all.at[layer], pre_ref.at[layer % 2], pre_sem.at[layer % 2]
            )
            copy.start()
            loads[layer, "pre"] = copy

    bring_pre(layers - 1)
    bring(layers - 1, (4, 5, 2, 3, 1, 0))
    small_held[...] = jnp.zeros_like(small_held)
    greet(fsdp_size, ctx_size, True)
    link = Link(send_sem, recv_sem)
    pump = Stream()
    both = [order[::-1] for order in orders(fsdp_size)]
    mask = mask_ref[...]
    pair_cols = 2 * HEAD_DIM
    lane = lax.broadcasted_iota(jnp.int32, (rows, pair_cols), 1)
    first = lane < HEAD_DIM
    live = live_ref[...] > 0
    mine, theirs = rows_of(ctx, rows), rows_of(1 - ctx, rows)
    groups = 0
    last_sent = {}

    def scatter(layer, pair):
        nonlocal groups

        def writer(part):
            def write(value):
                if part == 0:
                    qkv_ref[layer, 0] = value[:, :cols]
                    qkv_ref[layer, 1] = value[:, cols:]
                elif part == 1:
                    qkv_ref[layer, 2] = value[:, :cols]
                    out_weight_ref[layer] = value[:, cols:]
                else:
                    target = up_ref if part < 4 else down_ref
                    target[layer, :, part % 2 * width : (part % 2 + 1) * width] = value

            return write

        events = in_step(
            *[
                Scatter(
                    link,
                    ctx_size,
                    terms.at[part],
                    arrived.at[part],
                    last.at[part],
                    both[part % 2],
                    credits.at[part],
                    layer == layers - 1,
                    layer == 0,
                    writer(part),
                ).events()
                for part in (2 * pair, 2 * pair + 1)
            ]
        )
        events[0]()
        pump.release((layer, pair), events[1:], SCATTER_PACE * groups)
        groups += 1

    def free(layer, pair):
        if layer < layers - 1:
            pump.need((layer + 1, pair))

    def product(part, start, count, right):
        @pl.loop(0, count)
        def _(at):
            terms[part, :, lanes(at + start, TILE)] = dot_nn(turned[...], right(at)).astype(BF16)

    def up_products(layer, vector):
        normal, _ = standardized(mid_ref[layer])
        turned[...] = jnp.transpose(
            (normal * vector(GAIN_B) + vector(SHIFT_B)).astype(BF16)
        )
        free(layer, 1)
        for part in range(2):
            product(2 + part, 0, pieces, lambda at, part=part: low_pre[part, :, lanes(at, TILE)])
        scatter(layer, 1)

    out_ref[...] = cotangent_ref[...].astype(F32)
    for layer in reversed(range(layers)):
        rows_small = small_held.at[layer, 0]

        def vector(which):
            at = which * layers + layer
            return vector_ref[at : at + 1, :]

        def keep_row(which, value):
            rows_small[which : which + 1, :] = value

        bring_pre(layer - 1)
        grad = out_ref[...]
        masked = mask * grad
        keep_row(DOWN_B, jnp.sum(masked, axis=0, keepdims=True))
        low[...] = masked.astype(BF16)
        turned[...] = jnp.transpose(low[...])
        loads[layer, "pre"].wait()
        for part in range(2):
            loads[layer, 4 + part].wait()

            @pl.loop(0, pieces)
            def _(at):
                pre = pre_ref[layer % 2, part, :, lanes(at, TILE)]
                chance = 0.5 * (1.0 + lax.erf(pre * ROOT_HALF))
                hidden[part, :, lanes(at, TILE)] = (pre * chance).astype(BF16)
                slope = chance + pre * (jnp.exp(-0.5 * pre * pre) * (1.0 / ROOT_TWO_PI))
                grad_pre = dot_nn(low[...], held[4 + part, :, lanes(at, TILE)]) * slope
                rows_small[UP_B + part : UP_B + part + 1, lanes(at, TILE)] = jnp.sum(
                    grad_pre, axis=0, keepdims=True
                )
                low_pre[part, :, lanes(at, TILE)] = grad_pre.astype(BF16)

            pump(BP[layer][part])
        bring(layer - 1, (4, 5))
        for part in (2, 3):
            loads[layer, part].wait()

        def up_partial(at):
            here = slice(at * TILE, (at + 1) * TILE)
            return dot_nt(low_pre[0], held[2, here, :]) + dot_nt(low_pre[1], held[3, here, :])

        if layer < layers - 1:
            link.settle(last_sent["up"])
        copies = send_pieces(link, up_partial, sent.at[0], got.at[0], pieces, across)
        last_sent["up"] = copies
        bring(layer - 1, (2, 3))
        free(layer, 2)
        for part in range(2):
            product(4 + part, 0, pieces, lambda at, part=part: hidden[part, :, lanes(at, TILE)])
        scatter(layer, 2)
        if layer == layers - 1:
            up_products(layer, vector)
        pump(BP[layer][2])
        grad_normed = both_halves(copies, sent.at[0], got.at[0])
        normal, scale = standardized(mid_ref[layer])
        grad_in, grad_gain, grad_shift = norm_pull(normal, scale, vector(GAIN_B), grad_normed)
        keep_row(GAIN_B, grad_gain)
        keep_row(SHIFT_B, grad_shift)
        grad_mid = out_ref[...] + grad_in
        out_ref[...] = grad_mid
        masked = mask * grad_mid
        keep_row(OUT_B, jnp.sum(masked, axis=0, keepdims=True))
        low[...] = masked.astype(BF16)
        loads[layer, 1].wait()

        @pl.loop(0, cols // TILE)
        def _(at):
            grad_att[:, lanes(at, TILE)] = dot_nn(
                low[...], held[1, :, lanes(at + cols // TILE, TILE)]
            ).astype(BF16)

        pump(BP[layer][3])
        for half in range(2):
            per_half = cols // pair_cols // 2

            @pl.loop(half * per_half, (half + 1) * per_half)
            def _(at):
                queries = query_ref[layer, :, lanes(at, pair_cols)]
                grads = grad_att[:, lanes(at, pair_cols)]
                keys = kv_ref[layer, :, lanes(at, pair_cols)]
                values = kv_ref[layer, :, lanes(at + cols // pair_cols, pair_cols)]
                found, key_grad, value_grad = [], None, None
                for head in range(2):
                    here = first if head == 0 else ~first
                    query = jnp.where(here, queries, jnp.zeros_like(queries))
                    one_grad = jnp.where(here, grads, jnp.zeros_like(grads))
                    scores = jnp.where(live, dot_nt(query, keys) * HEAD_DIM**-0.5, NEG)
                    log_total = jnp.sum(
                        jnp.where(lane == 2 * at + head, log_total_ref[layer], 0.0),
                        axis=-1,
                        keepdims=True,
                    )
                    weights = jnp.exp(scores - log_total)
                    grad_weights = dot_nt(one_grad, values)
                    along = jnp.sum(weights * grad_weights, axis=-1, keepdims=True)
                    grad_scores = (weights * (grad_weights - along)).astype(BF16)
                    found.append(dot_nn(grad_scores, keys))
                    one = dot_tn(grad_scores, query)
                    two = dot_tn(weights.astype(BF16), one_grad)
                    key_grad = one if head == 0 else key_grad + one
                    value_grad = two if head == 0 else value_grad + two
                grad_qk[:, lanes(at, pair_cols)] = (
                    jnp.where(first, found[0], found[1]) * HEAD_DIM**-0.5
                ).astype(BF16)
                grad_kv[:, lanes(at, pair_cols)] = key_grad * HEAD_DIM**-0.5
                grad_kv[:, lanes(at + cols // pair_cols, pair_cols)] = value_grad

            pump(BP[layer][4 + half])
        kv_copy = None
        if ctx_size > 1:
            if layer < layers - 1:
                link.settle([last_sent["kv"]])
            kv_sent[...] = grad_kv[theirs, :].astype(BF16)
            kv_copy = link.push(kv_sent, kv_got.at[layer], {"ctx": 1 - ctx})
            last_sent["kv"] = kv_copy
        pump(BP[layer][6])
        if layer < layers - 1:
            up_products(layer, vector)
        pump(BP[layer][7])
        total_kv = grad_kv[mine, :]
        if kv_copy is not None:
            kv_copy.wait_recv()
            total_kv = total_kv + kv_got[layer].astype(F32)
        grad_qk[:, cols:] = total_kv.astype(BF16)
        rows_small[QV_B : QV_B + 1, :cols] = jnp.sum(
            grad_qk[:, :cols].astype(F32), axis=0, keepdims=True
        )
        rows_small[QV_B : QV_B + 1, cols:] = jnp.sum(
            grad_qk[:, 2 * cols :].astype(F32), axis=0, keepdims=True
        )
        loads[layer, 0].wait()

        def in_partial(at):
            here = slice(at * TILE, (at + 1) * TILE)
            return dot_nt(grad_qk[:, : 2 * cols], held[0, here, :]) + dot_nt(
                grad_qk[:, 2 * cols :], held[1, here, :cols]
            )

        if layer < layers - 1:
            link.settle(last_sent["in"])
        copies = send_pieces(link, in_partial, sent.at[1], got.at[1], pieces, across)
        last_sent["in"] = copies
        bring(layer - 1, (1, 0))
        pump(BP[layer][8])
        free(layer, 0)
        turned[...] = jnp.transpose(low[...])
        product(1, cols // TILE, cols // TILE, lambda at: attended_ref[layer, :, lanes(at, TILE)])
        normal, scale = standardized(stream_ref[layer])
        turned[...] = jnp.transpose(
            (normal * vector(GAIN_A) + vector(SHIFT_A)).astype(BF16)
        )
        product(0, 0, 2 * cols // TILE, lambda at: grad_qk[:, lanes(at, TILE)])
        product(1, 0, cols // TILE, lambda at: grad_qk[:, lanes(at + 2 * cols // TILE, TILE)])
        scatter(layer, 0)
        pump(BP[layer][9])
        grad_normed = both_halves(copies, sent.at[1], got.at[1])
        normal, scale = standardized(stream_ref[layer])
        grad_in, grad_gain, grad_shift = norm_pull(normal, scale, vector(GAIN_A), grad_normed)
        keep_row(GAIN_A, grad_gain)
        keep_row(SHIFT_A, grad_shift)
        grad = out_ref[...] + grad_in
        out_ref[...] = grad if layer > 0 else mask * grad
        total = Total(link, fsdp_size, ctx_size, small_held.at[layer], small_got.at[layer])
        pump.release(("small", layer), total.events(), SCATTER_PACE * (groups - 1))
    pump.rest()
    for layer in range(layers):
        for row in range(small_ref.shape[0]):
            small_ref[row, layer : layer + 1, :] = small_held[
                layer, small_held.shape[1] - 1, row : row + 1, :
            ]
    link.drain()


def backward_all(mesh, cotangent, mask, live, vectors, kept, whole):
    fsdp_size, ctx_size = mesh.shape["fsdp"], mesh.shape["ctx"]
    rows, width = cotangent.shape
    layers, _, _, part_cols = whole.shape
    cols = width // mesh.shape["tp"]
    slots_all = rows * ctx_size
    pieces = width // TILE
    slots = fsdp_size // 2
    both = width // fsdp_size
    block = both // ctx_size
    bits = fsdp_size.bit_length() - 1
    steps = bits + (ctx_size > 1)
    shape = jax.ShapeDtypeStruct
    vmem = pl.BlockSpec(memory_space=pltpu.VMEM)
    any_space = pl.BlockSpec(memory_space=pl.ANY)
    operands = [cotangent, mask, live, vectors, *kept, whole]
    pushes = layers * ((ctx_size > 1) + 2 * pieces + PARTS * (2 * slots) + steps)
    return pl.pallas_call(
        functools.partial(backward_kernel, ctx_size, fsdp_size),
        out_shape=[
            shape((rows, width), F32),
            shape((layers, 3, block, cols), F32),
            shape((layers, block, cols), F32),
            shape((layers, block, 2 * width), F32),
            shape((layers, block, 2 * width), F32),
            shape((VECTORS + BIASES, layers, width), F32),
        ],
        in_specs=[vmem] * (len(operands) - 2) + [any_space] * 2,
        out_specs=[vmem] * 6,
        scratch_shapes=[
            pltpu.VMEM((2, 2, rows, width), F32),
            pltpu.VMEM(whole.shape[1:], BF16),
            pltpu.VMEM(whole.shape[1:], BF16),
            pltpu.VMEM((PARTS, 2 * slots - 1, both, part_cols), BF16),
            pltpu.VMEM((PARTS, block, part_cols), BF16),
            pltpu.VMEM((width, rows), BF16),
            pltpu.VMEM((rows, width), BF16),
            pltpu.VMEM((2, rows, width), BF16),
            pltpu.VMEM((2, rows, width), BF16),
            pltpu.VMEM((rows, cols), BF16),
            pltpu.VMEM((rows, 3 * cols), BF16),
            pltpu.VMEM((slots_all, 2 * cols), F32),
            pltpu.VMEM((rows, 2 * cols), BF16),
            pltpu.VMEM((layers, rows, 2 * cols), BF16),
            pltpu.VMEM((2, pieces, rows, TILE), BF16),
            pltpu.VMEM((2, pieces, rows, TILE), BF16),
            pltpu.VMEM((layers, steps + 1, SMALL_ROWS, width), F32),
            pltpu.VMEM((layers, steps, SMALL_ROWS, width), F32),
            pltpu.SemaphoreType.DMA((pushes,)),
            pltpu.SemaphoreType.DMA((pushes,)),
            pltpu.SemaphoreType.DMA((PARTS,)),
            pltpu.SemaphoreType.DMA((2,)),
            pltpu.SemaphoreType.REGULAR((PARTS, steps + 1)),
        ],
        compiler_params=pltpu.CompilerParams(
            collective_id=1, has_side_effects=True, vmem_limit_bytes=63 * 2**20
        ),
        name="backward_all",
    )(*operands)


def body(
    mesh,
    tokens,
    lengths,
    cotangent,
    attn_gain,
    attn_shift,
    qkv_weight,
    qv_bias,
    out_weight,
    out_bias,
    mlp_gain,
    mlp_shift,
    up_weight,
    up_bias,
    down_weight,
    down_bias,
):
    images, local_slots, width = tokens.shape
    ctx_size = mesh.shape["ctx"]
    rows_here, slots_all = images * local_slots, local_slots * ctx_size
    layers, block, _, cols = qkv_weight.shape
    units = up_weight.shape[2]
    slot_ids = lax.axis_index("ctx") * local_slots + jnp.arange(local_slots, dtype=jnp.int32)
    mask = (slot_ids[None, :] < lengths[:, None]).astype(F32).reshape(rows_here, 1)
    live = (jnp.arange(slots_all, dtype=jnp.int32)[None, :] < lengths[:, None]).astype(F32)
    own_vectors = (attn_gain, attn_shift, out_bias, mlp_gain, mlp_shift, down_bias)
    output, vectors, *kept, whole = forward_all(
        mesh,
        tokens.reshape(rows_here, width),
        mask,
        live,
        own_vectors,
        qv_bias,
        up_bias,
        jnp.swapaxes(qkv_weight, 1, 2),
        jnp.swapaxes(out_weight, 1, 2),
        up_weight,
        jnp.swapaxes(down_weight, 1, 2),
    )
    input_grad, grad_qkv, grad_out, grad_up, grad_down, little = backward_all(
        mesh, cotangent.reshape(rows_here, width), mask, live, vectors, kept, whole
    )
    here = (lax.axis_index("fsdp") * ctx_size + lax.axis_index("ctx")) * block
    own = lax.dynamic_slice_in_dim(little[:VECTORS], here, block, axis=2)
    return (
        output.reshape(tokens.shape),
        input_grad.reshape(tokens.shape),
        own[GAIN_A],
        own[SHIFT_A],
        jnp.swapaxes(grad_qkv, 1, 2),
        little[QV_B].reshape(layers, 2, cols),
        jnp.swapaxes(grad_out, 1, 2),
        own[OUT_B],
        own[GAIN_B],
        own[SHIFT_B],
        grad_up,
        jnp.concatenate((little[UP_B], little[UP_B + 1]), axis=1),
        jnp.swapaxes(grad_down, 1, 2),
        own[DOWN_B],
    )


def solution(mesh):
    place = P(None, ("fsdp", "ctx"))
    rows = P("fsdp", "ctx", None)
    return jax.shard_map(
        functools.partial(body, mesh),
        mesh=mesh,
        in_specs=(
            rows,
            P("fsdp"),
            rows,
            place,
            place,
            P(None, ("fsdp", "ctx"), None, "tp"),
            P(None, None, "tp"),
            P(None, "tp", ("fsdp", "ctx")),
            place,
            place,
            place,
            P(None, ("fsdp", "ctx"), "tp"),
            P(None, "tp"),
            P(None, "tp", ("fsdp", "ctx")),
            place,
        ),
        out_specs=(
            rows,
            rows,
            place,
            place,
            P(None, ("fsdp", "ctx"), None, "tp"),
            P(None, None, "tp"),
            P(None, "tp", ("fsdp", "ctx")),
            place,
            place,
            place,
            P(None, ("fsdp", "ctx"), "tp"),
            P(None, "tp"),
            P(None, "tp", ("fsdp", "ctx")),
            place,
        ),
        check_vma=False,
    )
```

```python
import functools

import jax
import jax.numpy as jnp
from jax import lax
from jax.experimental import pallas as pl
from jax.experimental.pallas import tpu as pltpu
from jax.sharding import PartitionSpec as P

HEAD_DIM = 64
EPS = 1e-05
NEG = -30000.0
MESH = pl.DeviceIdType.MESH
PARTS = 6
BF16 = jnp.bfloat16
F32 = jnp.float32


def flip(index, bit):
    size = 2**bit
    return index + size - 2 * size * ((index // size) % 2)


def flip_all(index, bits):
    for bit in bits:
        index = flip(index, bit)
    return index


def subsets(bits):
    found = [()]
    for bit in bits:
        found = found + [entry + (bit,) for entry in found]
    return found


def orders(fsdp_size):
    top = fsdp_size.bit_length() - 1
    bits = list(range(1, top))
    half = len(bits) // 2
    return bits, bits[half:] + bits[:half]


class Link:
    def __init__(self, send_sem, recv_sem):
        self.send_sem, self.recv_sem, self.used, self.sent = send_sem, recv_sem, 0, []

    def push(self, src, dst, device):
        at = self.used
        self.used += 1
        copy = pltpu.make_async_remote_copy(
            src_ref=src,
            dst_ref=dst,
            send_sem=self.send_sem.at[at],
            recv_sem=self.recv_sem.at[at],
            device_id=device,
            device_id_type=MESH,
        )
        copy.start()
        self.sent.append(copy)
        return copy

    def settle(self, copies):
        for copy in copies:
            copy.wait_send()
            self.sent = [other for other in self.sent if other is not copy]

    def drain(self):
        for copy in self.sent:
            copy.wait_send()
        self.sent = []


def greet(fsdp_size, ctx_size, with_tp):
    me, ctx, tp = lax.axis_index("fsdp"), lax.axis_index("ctx"), lax.axis_index("tp")
    barrier = pltpu.get_barrier_semaphore()
    count = 0
    for bit in range(fsdp_size.bit_length() - 1):
        pl.semaphore_signal(
            barrier, inc=1, device_id={"fsdp": flip(me, bit)}, device_id_type=MESH
        )
        count += 1
    if ctx_size > 1:
        pl.semaphore_signal(barrier, inc=1, device_id={"ctx": 1 - ctx}, device_id_type=MESH)
        count += 1
    if with_tp:
        pl.semaphore_signal(barrier, inc=1, device_id={"tp": 1 - tp}, device_id_type=MESH)
        count += 1
    pl.semaphore_wait(barrier, count)


def rows_of(start, rows):
    return pl.ds(pl.multiple_of(start * rows, rows), rows)


def gather_pushes(fsdp_size, ctx_size):
    steps = fsdp_size.bit_length() - 2
    return (ctx_size - 1) + ctx_size * (2**steps - 1) + 2**steps


class Gather:
    def __init__(self, link, ctx_size, whole, block, order):
        self.link, self.whole, self.block, self.order = link, whole, block, order
        self.ctx_size = ctx_size
        self.me, self.ctx = lax.axis_index("fsdp"), lax.axis_index("ctx")
        self.waits, self.crossed, self.after = {}, False, None

    def rows(self, fsdp, ctx):
        return self.whole.at[rows_of(fsdp * self.ctx_size + ctx, self.block)]

    def spread(self, stream, step):
        ctx = self.ctx if stream == 0 else 1 - self.ctx
        bit = self.order[step]
        to = {"fsdp": flip(self.me, bit)}
        copies = []
        for entry in subsets(self.order[:step]):
            place = self.rows(flip_all(self.me, entry), ctx)
            copies.append(self.link.push(place, place, to))
        self.waits[stream, step] = copies

    def arrive(self, *key):
        for copy in self.waits.pop(key):
            copy.wait_recv()

    def cross(self):
        if not self.crossed:
            self.crossed = True
            own = self.rows(self.me, self.ctx)
            self.waits["ctx",] = [
                self.link.push(own, own, {"ctx": 1 - self.ctx})
            ]

    def start(self):
        self.spread(0, 0)

    def next_step(self, stream, step):
        self.arrive(stream, step - 1)
        self.spread(stream, step)

    def other(self):
        self.cross()
        self.arrive("ctx")
        if self.after is not None:
            self.after.cross()
        self.spread(1, 0)

    def core(self):
        last = len(self.order) - 1
        for stream in range(self.ctx_size):
            self.arrive(stream, last)
        both = self.block * self.ctx_size
        copies = []
        for entry in subsets(self.order):
            place = self.whole.at[rows_of(flip_all(self.me, entry), both)]
            copies.append(self.link.push(place, place, {"fsdp": flip(self.me, 0)}))
        self.waits["core",] = copies

    def finish(self):
        self.arrive("core")

    def events(self):
        found = [self.start]
        for step in range(1, len(self.order)):
            found.append(functools.partial(self.next_step, 0, step))
        if self.ctx_size > 1:
            found.append(self.other)
            for step in range(1, len(self.order)):
                found.append(functools.partial(self.next_step, 1, step))
        return found + [self.core, self.finish]


def in_step(first, second):
    def run(one, two):
        one()
        two()

    return [functools.partial(run, one, two) for one, two in zip(first, second)]


class Total:
    def __init__(self, link, fsdp_size, ctx_size, held, arrived):
        self.link, self.held, self.arrived = link, held, arrived
        me, ctx = lax.axis_index("fsdp"), lax.axis_index("ctx")
        self.partners = [{"fsdp": flip(me, bit)} for bit in range(fsdp_size.bit_length() - 1)]
        if ctx_size > 1:
            self.partners.append({"ctx": 1 - ctx})

    def step(self, at):
        if at > 0:
            self.copy.wait_recv()
            self.held[at] = self.held[at - 1] + self.arrived[at - 1]
        if at < len(self.partners):
            self.copy = self.link.push(self.held.at[at], self.arrived.at[at], self.partners[at])

    def events(self):
        return [functools.partial(self.step, at) for at in range(len(self.partners) + 1)]


def dot_nn(left, right):
    return lax.dot_general(left, right, (((1,), (0,)), ((), ())), preferred_element_type=F32)


def dot_nt(left, right):
    return lax.dot_general(left, right, (((1,), (1,)), ((), ())), preferred_element_type=F32)


def dot_tn(left, right):
    return lax.dot_general(left, right, (((0,), (0,)), ((), ())), preferred_element_type=F32)


TILE = 256
ROOT_HALF = 0.7071067811865476
ROOT_TWO_PI = 2.5066282746310002
VECTORS, BIASES, SMALL_ROWS = 6, 3, 16
PACE, SCATTER_PACE = 1.25, 1.25
FP = ((3, 2, 2, 2, 1, 1, 3), (3, 2, 3, 1, 1, 0, 3), (2, 1, 3, 2, 1, 1, 3))
BP = ((0, 1, 1, 1, 1, 1, 2, 2, 0, 0), (2, 1, 1, 1, 1, 2, 2, 1, 1, 2), (0, 0, 1, 0, 0, 0, 0, 1, 1, 1))
GAIN_A, SHIFT_A, OUT_B, GAIN_B, SHIFT_B, DOWN_B, QV_B, UP_B = range(8)


def lanes(at, count):
    return pl.ds(pl.multiple_of(at * count, count), count)


def standardized(values):
    centered = values - jnp.mean(values, axis=-1, keepdims=True)
    scale = lax.rsqrt(jnp.mean(centered * centered, axis=-1, keepdims=True) + EPS)
    return centered * scale, scale


def send_pieces(link, partial, sent, got, pieces, partner):
    copies = []
    for at in range(pieces):
        sent[at] = partial(at).astype(BF16)
        copies.append(link.push(sent.at[at], got.at[at], partner))
    return copies


def both_halves(copies, sent, got):
    found = []
    for at, copy in enumerate(copies):
        copy.wait_recv()
        found.append(sent[at].astype(F32) + got[at].astype(F32))
    return jnp.concatenate(found, axis=1)


class Stream:
    def __init__(self):
        self.waiting, self.count, self.done = [], 0, set()

    def release(self, group, events, begin, pace=1):
        for place, event in enumerate(events):
            self.waiting.append((begin + place * pace, self.count, group, event))
            self.count += 1
        self.waiting.sort(key=lambda entry: entry[:2])
        self.last = {entry[2]: entry for entry in self.waiting}

    def __call__(self, count):
        for entry in self.waiting[:count]:
            entry[3]()
            if self.last[entry[2]] is entry:
                self.done.add(entry[2])
        self.waiting = self.waiting[count:]

    def need(self, group):
        while group not in self.done:
            self(1)

    def rest(self):
        self(len(self.waiting))


def forward_kernel(ctx_size, fsdp_size, *refs):
    token_ref, mask_ref, live_ref = refs[:3]
    own_vectors = refs[3 : 3 + VECTORS]
    qv_ref, up_bias_ref, qkv_ref, out_weight_ref, up_ref, down_ref = refs[3 + VECTORS : 9 + VECTORS]
    (
        out_ref,
        vector_ref,
        stream_ref,
        query_ref,
        kv_out,
        log_total_ref,
        attended_ref,
        mid_ref,
        pre_out,
        whole_ref,
        held,
        pre_ref,
        normed,
        hidden,
        kv,
        sent,
        got,
        small_held,
        small_got,
        send_sem,
        recv_sem,
        save_sem,
        kv_sem,
        pre_sem,
    ) = refs[9 + VECTORS :]
    layers, rows, width = stream_ref.shape
    cols = query_ref.shape[2]
    pieces = width // TILE
    pairs = PARTS // 2
    ctx = lax.axis_index("ctx")
    across = {"tp": 1 - lax.axis_index("tp")}
    greet(fsdp_size, ctx_size, True)
    link = Link(send_sem, recv_sem)
    pump = Stream()
    both = orders(fsdp_size)
    block = up_ref.shape[1]
    me = lax.axis_index("fsdp") * ctx_size + ctx
    here = rows_of(me, block)
    for layer in range(layers):
        for at in range(3):
            place = slice(at % 2 * cols, (at % 2 + 1) * cols)
            held[layer, at // 2, here, place] = qkv_ref[layer, at]
        held[layer, 1, here, cols:] = out_weight_ref[layer]
        for half in range(2):
            columns = slice(half * width, (half + 1) * width)
            held[layer, 2 + half, here, :] = up_ref[layer, :, columns]
            held[layer, 4 + half, here, :] = down_ref[layer, :, columns]
    shift = lax.broadcasted_iota(jnp.int32, (block, width), 0) + me * block
    shift = (shift == lax.broadcasted_iota(jnp.int32, (block, width), 1)).astype(BF16)
    placed = [dot_nn(vector[...], shift) for vector in own_vectors]
    unused = small_held.shape[1] - VECTORS * layers
    placed.append(jnp.zeros((unused, width), F32))
    small_held[0] = jnp.concatenate(placed, axis=0).astype(BF16)
    total = Total(link, fsdp_size, ctx_size, small_held, small_got)
    gathers, previous, keeps, saves, pre_saves, groups = (), (), {}, [], {}, 0
    for layer in range(layers):
        for pair in range(pairs):
            found = [
                Gather(
                    link,
                    ctx_size,
                    held.at[layer, part],
                    block,
                    both[part % 2],
                )
                for part in (2 * pair, 2 * pair + 1)
            ]
            for gather, before in zip(found, previous):
                before.after = gather
            previous = found
            if not gathers:
                gathers = found

            def keep(layer=layer, pair=pair):
                for part in (2 * pair, 2 * pair + 1):
                    copy = pltpu.make_async_copy(
                        held.at[layer, part], whole_ref.at[layer, part], save_sem.at[layer, part]
                    )
                    copy.start()
                    saves.append(copy)

            events = in_step(*[gather.events() for gather in found])
            pump.release((layer, pair), events, PACE * groups)
            keeps[layer, pair] = keep
            groups += 1

    def need(layer, pair):
        pump.need((layer, pair))
        keeps[layer, pair]()

    total.step(0)
    for gather in gathers:
        gather.cross()
    for at in range(1, len(total.partners) + 1):
        pump(1)
        total.step(at)
    vector_ref[...] = small_held[len(total.partners)].astype(F32)
    mask = mask_ref[...]
    stream_ref[0] = mask * token_ref[...].astype(F32)
    mine = rows_of(ctx, rows)
    pair_cols = 2 * HEAD_DIM
    lane = lax.broadcasted_iota(jnp.int32, (rows, pair_cols), 1)
    first = lane < HEAD_DIM
    live = live_ref[...] > 0
    log_total_ref[...] = jnp.zeros_like(log_total_ref)

    for layer in range(layers):
        def vector(which):
            at = which * layers + layer
            return vector_ref[at : at + 1, :]

        normal, _ = standardized(stream_ref[layer])
        normed[...] = (normal * vector(GAIN_A) + vector(SHIFT_A)).astype(BF16)
        need(layer, 0)

        @pl.loop(0, cols // TILE)
        def _(at):
            rows_in = normed[...]
            kv[layer, mine, lanes(at, TILE)] = dot_nn(
                rows_in, held[layer, 0, :, lanes(at + cols // TILE, TILE)]
            ).astype(BF16)
            kv[layer, mine, lanes(at + cols // TILE, TILE)] = (
                dot_nn(rows_in, held[layer, 1, :, lanes(at, TILE)])
                + qv_ref[layer, 1:2, lanes(at, TILE)].astype(F32)
            ).astype(BF16)

        kv_copy = None
        if ctx_size > 1:
            kv_copy = link.push(kv.at[layer, mine], kv.at[layer, mine], {"ctx": 1 - ctx})

        @pl.loop(0, cols // TILE)
        def _(at):
            query_ref[layer, :, lanes(at, TILE)] = (
                dot_nn(normed[...], held[layer, 0, :, lanes(at, TILE)]) + qv_ref[layer, 0:1, lanes(at, TILE)].astype(F32)
            ).astype(BF16)

        pump(FP[layer][0])
        if kv_copy is not None:
            kv_copy.wait_recv()
        save = pltpu.make_async_copy(kv.at[layer], kv_out.at[layer], kv_sem.at[layer])
        save.start()
        saves.append(save)

        for half in range(2):
            per_half = cols // pair_cols // 2

            @pl.loop(half * per_half, (half + 1) * per_half)
            def _(at):
                queries = query_ref[layer, :, lanes(at, pair_cols)]
                keys = kv[layer, :, lanes(at, pair_cols)]
                values = kv[layer, :, lanes(at + cols // pair_cols, pair_cols)]
                found = []
                for head in range(2):
                    chosen = jnp.where(
                        first if head == 0 else ~first, queries, jnp.zeros_like(queries)
                    )
                    scores = jnp.where(live, dot_nt(chosen, keys) * HEAD_DIM**-0.5, NEG)
                    top = jnp.max(scores, axis=-1, keepdims=True)
                    weights = jnp.exp(scores - top)
                    summed = jnp.sum(weights, axis=-1, keepdims=True)
                    log_total_ref[layer] = jnp.where(
                        lane == 2 * at + head, top + jnp.log(summed), log_total_ref[layer]
                    )
                    found.append(dot_nn((weights * (1.0 / summed)).astype(BF16), values))
                attended_ref[layer, :, lanes(at, pair_cols)] = jnp.where(
                    first, found[0], found[1]
                ).astype(BF16)

            pump(FP[layer][1 + half])

        def out_partial(at):
            return dot_nt(attended_ref[layer], held[layer, 1, at * TILE : (at + 1) * TILE, cols:])

        copies = send_pieces(link, out_partial, sent.at[layer, 0], got.at[0], pieces, across)
        pump(FP[layer][3])
        branch = both_halves(copies, sent.at[layer, 0], got.at[0])
        mid = stream_ref[layer] + mask * (branch + vector(OUT_B))
        mid_ref[layer] = mid
        normal, _ = standardized(mid)
        normed[...] = (normal * vector(GAIN_B) + vector(SHIFT_B)).astype(BF16)
        need(layer, 1)
        if layer >= 2:
            pre_saves.pop(layer - 2).wait()
        for part in range(2):

            @pl.loop(0, pieces)
            def _(at):
                pre = dot_nn(normed[...], held[layer, 2 + part, :, lanes(at, TILE)]) + up_bias_ref[
                    layer : layer + 1, lanes(at + part * pieces, TILE)
                ].astype(F32)
                pre_ref[layer % 2, part, :, lanes(at, TILE)] = pre
                hidden[part, :, lanes(at, TILE)] = (
                    0.5 * pre * (1.0 + lax.erf(pre * ROOT_HALF))
                ).astype(BF16)

            pump(FP[layer][4 + part])
        pre_saves[layer] = pltpu.make_async_copy(
            pre_ref.at[layer % 2], pre_out.at[layer], pre_sem.at[layer]
        )
        pre_saves[layer].start()
        need(layer, 2)

        def down_partial(at):
            here = slice(at * TILE, (at + 1) * TILE)
            return dot_nt(hidden[0], held[layer, 4, here, :]) + dot_nt(
                hidden[1], held[layer, 5, here, :]
            )

        copies = send_pieces(link, down_partial, sent.at[layer, 1], got.at[1], pieces, across)
        pump(FP[layer][6])
        branch = both_halves(copies, sent.at[layer, 1], got.at[1])
        after = mid_ref[layer] + mask * (branch + vector(DOWN_B))
        if layer + 1 < layers:
            stream_ref[layer + 1] = after
        else:
            out_ref[...] = after.astype(BF16)
    pump.rest()
    link.drain()
    for save in (*saves, *pre_saves.values()):
        save.wait()


def forward_all(mesh, tokens, mask, live, own_vectors, qv_bias, up_bias, qkv, out_t, up, down_t):
    fsdp_size, ctx_size = mesh.shape["fsdp"], mesh.shape["ctx"]
    rows, width = tokens.shape
    layers, _, _, cols = qkv.shape
    part_cols = 2 * cols
    small = (-(-VECTORS * layers // 16) * 16, width)
    slots_all = rows * ctx_size
    pieces = width // TILE
    steps = fsdp_size.bit_length() - 1 + (ctx_size > 1)
    shape = jax.ShapeDtypeStruct
    whole = (layers, PARTS, width, part_cols)
    out_shape = [
        shape((rows, width), BF16),
        shape(small, F32),
        shape((layers, rows, width), F32),
        shape((layers, rows, cols), BF16),
        shape((layers, slots_all, 2 * cols), BF16),
        shape((layers, rows, 2 * HEAD_DIM), F32),
        shape((layers, rows, cols), BF16),
        shape((layers, rows, width), F32),
        shape((layers, 2, rows, width), F32),
        shape(whole, BF16),
    ]
    vmem = pl.BlockSpec(memory_space=pltpu.VMEM)
    any_space = pl.BlockSpec(memory_space=pl.ANY)
    pushes = (
        layers * ((ctx_size > 1) + 2 * pieces + gather_pushes(fsdp_size, ctx_size) * PARTS)
        + steps
    )
    return pl.pallas_call(
        functools.partial(forward_kernel, ctx_size, fsdp_size),
        out_shape=out_shape,
        in_specs=[vmem] * (9 + VECTORS),
        out_specs=[vmem] * 4 + [any_space] + [vmem] * 3 + [any_space] * 2,
        scratch_shapes=[
            pltpu.VMEM(whole, BF16),
            pltpu.VMEM((2, 2, rows, width), F32),
            pltpu.VMEM((rows, width), BF16),
            pltpu.VMEM((2, rows, width), BF16),
            pltpu.VMEM((layers, slots_all, 2 * cols), BF16),
            pltpu.VMEM((layers, 2, pieces, rows, TILE), BF16),
            pltpu.VMEM((2, pieces, rows, TILE), BF16),
            pltpu.VMEM((steps + 1,) + small, BF16),
            pltpu.VMEM((steps,) + small, BF16),
            pltpu.SemaphoreType.DMA((pushes,)),
            pltpu.SemaphoreType.DMA((pushes,)),
            pltpu.SemaphoreType.DMA((layers, PARTS)),
            pltpu.SemaphoreType.DMA((layers,)),
            pltpu.SemaphoreType.DMA((layers,)),
        ],
        compiler_params=pltpu.CompilerParams(
            collective_id=0, has_side_effects=True, vmem_limit_bytes=63 * 2**20
        ),
        name="forward_all",
    )(tokens, mask, live, *own_vectors, qv_bias, up_bias, qkv, out_t, up, down_t)


class Scatter:
    def __init__(self, link, ctx_size, terms, arrived, last, order, credits, first, final, write):
        self.link, self.terms, self.arrived, self.last = link, terms, arrived, last
        self.ctx_size, self.order, self.write = ctx_size, order, write
        self.credits, self.first, self.final = credits, first, final
        self.me, self.ctx = lax.axis_index("fsdp"), lax.axis_index("ctx")
        self.slots = 2 ** len(order)
        self.both = terms.shape[0] // (2 * self.slots)
        self.flips = [
            [bit for at, bit in enumerate(order) if (slot >> (len(order) - 1 - at)) % 2 == 1]
            for slot in range(self.slots)
        ]
        self.base, self.sent = 0, []

    def place(self, slot, core=0):
        start = flip(self.me, 0) if core else self.me
        return rows_of(flip_all(start, self.flips[slot]), self.both)

    def send(self, step, pieces, to):
        if not self.first:
            pl.semaphore_wait(self.credits.at[step], 1)
        self.copies = [self.link.push(src, dst, to) for src, dst in pieces]
        self.sent += self.copies

    def read(self, step, to):
        if not self.final:
            pl.semaphore_signal(
                self.credits.at[step], inc=1, device_id=to, device_id_type=MESH
            )

    def start(self):
        self.send(
            0,
            [
                (self.terms.at[self.place(slot, 1)], self.arrived.at[slot])
                for slot in range(self.slots)
            ],
            {"fsdp": flip(self.me, 0)},
        )

    def take(self, step, count, to):
        for copy in self.copies:
            copy.wait_recv()
        for slot in range(count):
            here = self.place(slot)
            self.terms[here, :] = self.terms[here, :] + self.arrived[self.base + slot]
        self.base += count
        self.read(step, to)

    def step(self, at):
        count = self.slots >> at
        self.take(at, count, {"fsdp": flip(self.me, 0 if at == 0 else self.order[at - 1])})
        half = count // 2
        self.send(
            at + 1,
            [
                (self.terms.at[self.place(half + slot)], self.arrived.at[self.base + slot])
                for slot in range(half)
            ],
            {"fsdp": flip(self.me, self.order[at])},
        )

    def across(self):
        steps = len(self.order)
        self.take(steps, 1, {"fsdp": flip(self.me, self.order[-1])})
        if self.ctx_size > 1:
            block = self.both // self.ctx_size
            theirs = rows_of(self.me * self.ctx_size + 1 - self.ctx, block)
            self.send(steps + 1, [(self.terms.at[theirs], self.last)], {"ctx": 1 - self.ctx})

    def finish(self):
        block = self.both // self.ctx_size
        total = self.terms[rows_of(self.me * self.ctx_size + self.ctx, block), :].astype(F32)
        if self.ctx_size > 1:
            for copy in self.copies:
                copy.wait_recv()
            total = total + self.last[...].astype(F32)
            self.read(len(self.order) + 1, {"ctx": 1 - self.ctx})
        self.write(total)
        self.link.settle(self.sent)

    def events(self):
        found = [self.start]
        for at in range(len(self.order)):
            found.append(functools.partial(self.step, at))
        return found + [self.across, self.finish]


def norm_pull(normal, scale, gain, grad):
    grad_gain = jnp.sum(grad * normal, axis=0, keepdims=True)
    grad_shift = jnp.sum(grad, axis=0, keepdims=True)
    inner = grad * gain
    along = jnp.mean(inner * normal, axis=-1, keepdims=True)
    grad_in = scale * (inner - jnp.mean(inner, axis=-1, keepdims=True) - normal * along)
    return grad_in, grad_gain, grad_shift


def backward_kernel(ctx_size, fsdp_size, *refs):
    (
        cotangent_ref,
        mask_ref,
        live_ref,
        vector_ref,
        stream_ref,
        query_ref,
        kv_ref,
        log_total_ref,
        attended_ref,
        mid_ref,
        pre_all,
        whole_ref,
        out_ref,
        qkv_ref,
        out_weight_ref,
        up_ref,
        down_ref,
        small_ref,
        pre_ref,
        held,
        terms,
        arrived,
        last,
        turned,
        low,
        low_pre,
        hidden,
        grad_att,
        grad_qk,
        grad_kv,
        kv_sent,
        kv_got,
        sent,
        got,
        small_held,
        small_got,
        send_sem,
        recv_sem,
        load_sem,
        pre_sem,
        credits,
    ) = refs
    layers, rows, width = stream_ref.shape
    cols = query_ref.shape[2]
    pieces = width // TILE
    pairs = PARTS // 2
    ctx = lax.axis_index("ctx")
    across = {"tp": 1 - lax.axis_index("tp")}
    loads = {}

    def bring(layer, parts):
        if layer >= 0:
            for part in parts:
                copy = pltpu.make_async_copy(
                    whole_ref.at[layer, part], held.at[part], load_sem.at[part]
                )
                copy.start()
                loads[layer, part] = copy

    def bring_pre(layer):
        if layer >= 0:
            copy = pltpu.make_async_copy(
                pre_all.at[layer], pre_ref.at[layer % 2], pre_sem.at[layer % 2]
            )
            copy.start()
            loads[layer, "pre"] = copy

    bring_pre(layers - 1)
    bring(layers - 1, (4, 5, 2, 3, 1, 0))
    small_held[...] = jnp.zeros_like(small_held)
    greet(fsdp_size, ctx_size, True)
    link = Link(send_sem, recv_sem)
    pump = Stream()
    both = [order[::-1] for order in orders(fsdp_size)]
    mask = mask_ref[...]
    pair_cols = 2 * HEAD_DIM
    lane = lax.broadcasted_iota(jnp.int32, (rows, pair_cols), 1)
    first = lane < HEAD_DIM
    live = live_ref[...] > 0
    mine, theirs = rows_of(ctx, rows), rows_of(1 - ctx, rows)
    groups = 0
    last_sent = {}

    def scatter(layer, pair):
        nonlocal groups

        def writer(part):
            def write(value):
                if part == 0:
                    qkv_ref[layer, 0] = value[:, :cols]
                    qkv_ref[layer, 1] = value[:, cols:]
                elif part == 1:
                    qkv_ref[layer, 2] = value[:, :cols]
                    out_weight_ref[layer] = value[:, cols:]
                else:
                    target = up_ref if part < 4 else down_ref
                    target[layer, :, part % 2 * width : (part % 2 + 1) * width] = value

            return write

        events = in_step(
            *[
                Scatter(
                    link,
                    ctx_size,
                    terms.at[part],
                    arrived.at[part],
                    last.at[part],
                    both[part % 2],
                    credits.at[part],
                    layer == layers - 1,
                    layer == 0,
                    writer(part),
                ).events()
                for part in (2 * pair, 2 * pair + 1)
            ]
        )
        events[0]()
        pump.release((layer, pair), events[1:], SCATTER_PACE * groups)
        groups += 1

    def free(layer, pair):
        if layer < layers - 1:
            pump.need((layer + 1, pair))

    def product(part, start, count, right):
        @pl.loop(0, count)
        def _(at):
            terms[part, :, lanes(at + start, TILE)] = dot_nn(turned[...], right(at)).astype(BF16)

    def up_products(layer, vector):
        normal, _ = standardized(mid_ref[layer])
        turned[...] = jnp.transpose(
            (normal * vector(GAIN_B) + vector(SHIFT_B)).astype(BF16)
        )
        free(layer, 1)
        for part in range(2):
            product(2 + part, 0, pieces, lambda at, part=part: low_pre[part, :, lanes(at, TILE)])
        scatter(layer, 1)

    out_ref[...] = cotangent_ref[...].astype(F32)
    for layer in reversed(range(layers)):
        rows_small = small_held.at[layer, 0]

        def vector(which):
            at = which * layers + layer
            return vector_ref[at : at + 1, :]

        def keep_row(which, value):
            rows_small[which : which + 1, :] = value

        bring_pre(layer - 1)
        grad = out_ref[...]
        masked = mask * grad
        keep_row(DOWN_B, jnp.sum(masked, axis=0, keepdims=True))
        low[...] = masked.astype(BF16)
        turned[...] = jnp.transpose(low[...])
        loads[layer, "pre"].wait()
        for part in range(2):
            loads[layer, 4 + part].wait()

            @pl.loop(0, pieces)
            def _(at):
                pre = pre_ref[layer % 2, part, :, lanes(at, TILE)]
                chance = 0.5 * (1.0 + lax.erf(pre * ROOT_HALF))
                hidden[part, :, lanes(at, TILE)] = (pre * chance).astype(BF16)
                slope = chance + pre * (jnp.exp(-0.5 * pre * pre) * (1.0 / ROOT_TWO_PI))
                grad_pre = dot_nn(low[...], held[4 + part, :, lanes(at, TILE)]) * slope
                rows_small[UP_B + part : UP_B + part + 1, lanes(at, TILE)] = jnp.sum(
                    grad_pre, axis=0, keepdims=True
                )
                low_pre[part, :, lanes(at, TILE)] = grad_pre.astype(BF16)

            pump(BP[layer][part])
        bring(layer - 1, (4, 5))
        for part in (2, 3):
            loads[layer, part].wait()

        def up_partial(at):
            here = slice(at * TILE, (at + 1) * TILE)
            return dot_nt(low_pre[0], held[2, here, :]) + dot_nt(low_pre[1], held[3, here, :])

        if layer < layers - 1:
            link.settle(last_sent["up"])
        copies = send_pieces(link, up_partial, sent.at[0], got.at[0], pieces, across)
        last_sent["up"] = copies
        bring(layer - 1, (2, 3))
        free(layer, 2)
        for part in range(2):
            product(4 + part, 0, pieces, lambda at, part=part: hidden[part, :, lanes(at, TILE)])
        scatter(layer, 2)
        if layer == layers - 1:
            up_products(layer, vector)
        pump(BP[layer][2])
        grad_normed = both_halves(copies, sent.at[0], got.at[0])
        normal, scale = standardized(mid_ref[layer])
        grad_in, grad_gain, grad_shift = norm_pull(normal, scale, vector(GAIN_B), grad_normed)
        keep_row(GAIN_B, grad_gain)
        keep_row(SHIFT_B, grad_shift)
        grad_mid = out_ref[...] + grad_in
        out_ref[...] = grad_mid
        masked = mask * grad_mid
        keep_row(OUT_B, jnp.sum(masked, axis=0, keepdims=True))
        low[...] = masked.astype(BF16)
        loads[layer, 1].wait()

        @pl.loop(0, cols // TILE)
        def _(at):
            grad_att[:, lanes(at, TILE)] = dot_nn(
                low[...], held[1, :, lanes(at + cols // TILE, TILE)]
            ).astype(BF16)

        pump(BP[layer][3])
        for half in range(2):
            per_half = cols // pair_cols // 2

            @pl.loop(half * per_half, (half + 1) * per_half)
            def _(at):
                queries = query_ref[layer, :, lanes(at, pair_cols)]
                grads = grad_att[:, lanes(at, pair_cols)]
                keys = kv_ref[layer, :, lanes(at, pair_cols)]
                values = kv_ref[layer, :, lanes(at + cols // pair_cols, pair_cols)]
                found, key_grad, value_grad = [], None, None
                for head in range(2):
                    here = first if head == 0 else ~first
                    query = jnp.where(here, queries, jnp.zeros_like(queries))
                    one_grad = jnp.where(here, grads, jnp.zeros_like(grads))
                    scores = jnp.where(live, dot_nt(query, keys) * HEAD_DIM**-0.5, NEG)
                    log_total = jnp.sum(
                        jnp.where(lane == 2 * at + head, log_total_ref[layer], 0.0),
                        axis=-1,
                        keepdims=True,
                    )
                    weights = jnp.exp(scores - log_total)
                    grad_weights = dot_nt(one_grad, values)
                    along = jnp.sum(weights * grad_weights, axis=-1, keepdims=True)
                    grad_scores = (weights * (grad_weights - along)).astype(BF16)
                    found.append(dot_nn(grad_scores, keys))
                    one = dot_tn(grad_scores, query)
                    two = dot_tn(weights.astype(BF16), one_grad)
                    key_grad = one if head == 0 else key_grad + one
                    value_grad = two if head == 0 else value_grad + two
                grad_qk[:, lanes(at, pair_cols)] = (
                    jnp.where(first, found[0], found[1]) * HEAD_DIM**-0.5
                ).astype(BF16)
                grad_kv[:, lanes(at, pair_cols)] = key_grad * HEAD_DIM**-0.5
                grad_kv[:, lanes(at + cols // pair_cols, pair_cols)] = value_grad

            pump(BP[layer][4 + half])
        kv_copy = None
        if ctx_size > 1:
            if layer < layers - 1:
                link.settle([last_sent["kv"]])
            kv_sent[...] = grad_kv[theirs, :].astype(BF16)
            kv_copy = link.push(kv_sent, kv_got.at[layer], {"ctx": 1 - ctx})
            last_sent["kv"] = kv_copy
        pump(BP[layer][6])
        if layer < layers - 1:
            up_products(layer, vector)
        pump(BP[layer][7])
        total_kv = grad_kv[mine, :]
        if kv_copy is not None:
            kv_copy.wait_recv()
            total_kv = total_kv + kv_got[layer].astype(F32)
        grad_qk[:, cols:] = total_kv.astype(BF16)
        rows_small[QV_B : QV_B + 1, :cols] = jnp.sum(
            grad_qk[:, :cols].astype(F32), axis=0, keepdims=True
        )
        rows_small[QV_B : QV_B + 1, cols:] = jnp.sum(
            grad_qk[:, 2 * cols :].astype(F32), axis=0, keepdims=True
        )
        loads[layer, 0].wait()

        def in_partial(at):
            here = slice(at * TILE, (at + 1) * TILE)
            return dot_nt(grad_qk[:, : 2 * cols], held[0, here, :]) + dot_nt(
                grad_qk[:, 2 * cols :], held[1, here, :cols]
            )

        if layer < layers - 1:
            link.settle(last_sent["in"])
        copies = send_pieces(link, in_partial, sent.at[1], got.at[1], pieces, across)
        last_sent["in"] = copies
        bring(layer - 1, (1, 0))
        pump(BP[layer][8])
        free(layer, 0)
        turned[...] = jnp.transpose(low[...])
        product(1, cols // TILE, cols // TILE, lambda at: attended_ref[layer, :, lanes(at, TILE)])
        normal, scale = standardized(stream_ref[layer])
        turned[...] = jnp.transpose(
            (normal * vector(GAIN_A) + vector(SHIFT_A)).astype(BF16)
        )
        product(0, 0, 2 * cols // TILE, lambda at: grad_qk[:, lanes(at, TILE)])
        product(1, 0, cols // TILE, lambda at: grad_qk[:, lanes(at + 2 * cols // TILE, TILE)])
        scatter(layer, 0)
        pump(BP[layer][9])
        grad_normed = both_halves(copies, sent.at[1], got.at[1])
        normal, scale = standardized(stream_ref[layer])
        grad_in, grad_gain, grad_shift = norm_pull(normal, scale, vector(GAIN_A), grad_normed)
        keep_row(GAIN_A, grad_gain)
        keep_row(SHIFT_A, grad_shift)
        grad = out_ref[...] + grad_in
        out_ref[...] = grad if layer > 0 else mask * grad
        total = Total(link, fsdp_size, ctx_size, small_held.at[layer], small_got.at[layer])
        pump.release(("small", layer), total.events(), SCATTER_PACE * (groups - 1))
    pump.rest()
    for layer in range(layers):
        for row in range(small_ref.shape[0]):
            small_ref[row, layer : layer + 1, :] = small_held[
                layer, small_held.shape[1] - 1, row : row + 1, :
            ]
    link.drain()


def backward_all(mesh, cotangent, mask, live, vectors, kept, whole):
    fsdp_size, ctx_size = mesh.shape["fsdp"], mesh.shape["ctx"]
    rows, width = cotangent.shape
    layers, _, _, part_cols = whole.shape
    cols = width // mesh.shape["tp"]
    slots_all = rows * ctx_size
    pieces = width // TILE
    slots = fsdp_size // 2
    both = width // fsdp_size
    block = both // ctx_size
    bits = fsdp_size.bit_length() - 1
    steps = bits + (ctx_size > 1)
    shape = jax.ShapeDtypeStruct
    vmem = pl.BlockSpec(memory_space=pltpu.VMEM)
    any_space = pl.BlockSpec(memory_space=pl.ANY)
    operands = [cotangent, mask, live, vectors, *kept, whole]
    pushes = layers * ((ctx_size > 1) + 2 * pieces + PARTS * (2 * slots) + steps)
    return pl.pallas_call(
        functools.partial(backward_kernel, ctx_size, fsdp_size),
        out_shape=[
            shape((rows, width), F32),
            shape((layers, 3, block, cols), F32),
            shape((layers, block, cols), F32),
            shape((layers, block, 2 * width), F32),
            shape((layers, block, 2 * width), F32),
            shape((VECTORS + BIASES, layers, width), F32),
        ],
        in_specs=[vmem] * (len(operands) - 2) + [any_space] * 2,
        out_specs=[vmem] * 6,
        scratch_shapes=[
            pltpu.VMEM((2, 2, rows, width), F32),
            pltpu.VMEM(whole.shape[1:], BF16),
            pltpu.VMEM(whole.shape[1:], BF16),
            pltpu.VMEM((PARTS, 2 * slots - 1, both, part_cols), BF16),
            pltpu.VMEM((PARTS, block, part_cols), BF16),
            pltpu.VMEM((width, rows), BF16),
            pltpu.VMEM((rows, width), BF16),
            pltpu.VMEM((2, rows, width), BF16),
            pltpu.VMEM((2, rows, width), BF16),
            pltpu.VMEM((rows, cols), BF16),
            pltpu.VMEM((rows, 3 * cols), BF16),
            pltpu.VMEM((slots_all, 2 * cols), F32),
            pltpu.VMEM((rows, 2 * cols), BF16),
            pltpu.VMEM((layers, rows, 2 * cols), BF16),
            pltpu.VMEM((2, pieces, rows, TILE), BF16),
            pltpu.VMEM((2, pieces, rows, TILE), BF16),
            pltpu.VMEM((layers, steps + 1, SMALL_ROWS, width), F32),
            pltpu.VMEM((layers, steps, SMALL_ROWS, width), F32),
            pltpu.SemaphoreType.DMA((pushes,)),
            pltpu.SemaphoreType.DMA((pushes,)),
            pltpu.SemaphoreType.DMA((PARTS,)),
            pltpu.SemaphoreType.DMA((2,)),
            pltpu.SemaphoreType.REGULAR((PARTS, steps + 1)),
        ],
        compiler_params=pltpu.CompilerParams(
            collective_id=1, has_side_effects=True, vmem_limit_bytes=63 * 2**20
        ),
        name="backward_all",
    )(*operands)


def body(
    mesh,
    tokens,
    lengths,
    cotangent,
    attn_gain,
    attn_shift,
    qkv_weight,
    qv_bias,
    out_weight,
    out_bias,
    mlp_gain,
    mlp_shift,
    up_weight,
    up_bias,
    down_weight,
    down_bias,
):
    images, local_slots, width = tokens.shape
    ctx_size = mesh.shape["ctx"]
    rows_here, slots_all = images * local_slots, local_slots * ctx_size
    layers, block, _, cols = qkv_weight.shape
    units = up_weight.shape[2]
    slot_ids = lax.axis_index("ctx") * local_slots + jnp.arange(local_slots, dtype=jnp.int32)
    mask = (slot_ids[None, :] < lengths[:, None]).astype(F32).reshape(rows_here, 1)
    live = (jnp.arange(slots_all, dtype=jnp.int32)[None, :] < lengths[:, None]).astype(F32)
    own_vectors = (attn_gain, attn_shift, out_bias, mlp_gain, mlp_shift, down_bias)
    output, vectors, *kept, whole = forward_all(
        mesh,
        tokens.reshape(rows_here, width),
        mask,
        live,
        own_vectors,
        qv_bias,
        up_bias,
        jnp.swapaxes(qkv_weight, 1, 2),
        jnp.swapaxes(out_weight, 1, 2),
        up_weight,
        jnp.swapaxes(down_weight, 1, 2),
    )
    input_grad, grad_qkv, grad_out, grad_up, grad_down, little = backward_all(
        mesh, cotangent.reshape(rows_here, width), mask, live, vectors, kept, whole
    )
    here = (lax.axis_index("fsdp") * ctx_size + lax.axis_index("ctx")) * block
    own = lax.dynamic_slice_in_dim(little[:VECTORS], here, block, axis=2)
    return (
        output.reshape(tokens.shape),
        input_grad.reshape(tokens.shape),
        own[GAIN_A],
        own[SHIFT_A],
        jnp.swapaxes(grad_qkv, 1, 2),
        little[QV_B].reshape(layers, 2, cols),
        jnp.swapaxes(grad_out, 1, 2),
        own[OUT_B],
        own[GAIN_B],
        own[SHIFT_B],
        grad_up,
        jnp.concatenate((little[UP_B], little[UP_B + 1]), axis=1),
        jnp.swapaxes(grad_down, 1, 2),
        own[DOWN_B],
    )


def solution(mesh):
    place = P(None, ("fsdp", "ctx"))
    rows = P("fsdp", "ctx", None)
    return jax.shard_map(
        functools.partial(body, mesh),
        mesh=mesh,
        in_specs=(
            rows,
            P("fsdp"),
            rows,
            place,
            place,
            P(None, ("fsdp", "ctx"), None, "tp"),
            P(None, None, "tp"),
            P(None, "tp", ("fsdp", "ctx")),
            place,
            place,
            place,
            P(None, ("fsdp", "ctx"), "tp"),
            P(None, "tp"),
            P(None, "tp", ("fsdp", "ctx")),
            place,
        ),
        out_specs=(
            rows,
            rows,
            place,
            place,
            P(None, ("fsdp", "ctx"), None, "tp"),
            P(None, None, "tp"),
            P(None, "tp", ("fsdp", "ctx")),
            place,
            place,
            place,
            P(None, ("fsdp", "ctx"), "tp"),
            P(None, "tp"),
            P(None, "tp", ("fsdp", "ctx")),
            place,
        ),
        check_vma=False,
    )
```

```python
import functools

import jax
import jax.numpy as jnp
from jax import lax
from jax.experimental import pallas as pl
from jax.experimental.pallas import tpu as pltpu
from jax.sharding import PartitionSpec as P

HEAD_DIM = 64
EPS = 1e-05
NEG = -30000.0
MESH = pl.DeviceIdType.MESH
PARTS = 6
BF16 = jnp.bfloat16
F32 = jnp.float32


def flip(index, bit):
    size = 2**bit
    return index + size - 2 * size * ((index // size) % 2)


def flip_all(index, bits):
    for bit in bits:
        index = flip(index, bit)
    return index


def subsets(bits):
    found = [()]
    for bit in bits:
        found = found + [entry + (bit,) for entry in found]
    return found


def orders(fsdp_size):
    top = fsdp_size.bit_length() - 1
    bits = list(range(1, top))
    half = len(bits) // 2
    return bits, bits[half:] + bits[:half]


class Link:
    def __init__(self, send_sem, recv_sem):
        self.send_sem, self.recv_sem, self.used, self.sent = send_sem, recv_sem, 0, []

    def push(self, src, dst, device):
        at = self.used
        self.used += 1
        copy = pltpu.make_async_remote_copy(
            src_ref=src,
            dst_ref=dst,
            send_sem=self.send_sem.at[at],
            recv_sem=self.recv_sem.at[at],
            device_id=device,
            device_id_type=MESH,
        )
        copy.start()
        self.sent.append(copy)
        return copy

    def settle(self, copies):
        for copy in copies:
            copy.wait_send()
            self.sent = [other for other in self.sent if other is not copy]

    def drain(self):
        for copy in self.sent:
            copy.wait_send()
        self.sent = []


def greet(fsdp_size, ctx_size, with_tp):
    me, ctx, tp = lax.axis_index("fsdp"), lax.axis_index("ctx"), lax.axis_index("tp")
    barrier = pltpu.get_barrier_semaphore()
    count = 0
    for bit in range(fsdp_size.bit_length() - 1):
        pl.semaphore_signal(
            barrier, inc=1, device_id={"fsdp": flip(me, bit)}, device_id_type=MESH
        )
        count += 1
    if ctx_size > 1:
        pl.semaphore_signal(barrier, inc=1, device_id={"ctx": 1 - ctx}, device_id_type=MESH)
        count += 1
    if with_tp:
        pl.semaphore_signal(barrier, inc=1, device_id={"tp": 1 - tp}, device_id_type=MESH)
        count += 1
    pl.semaphore_wait(barrier, count)


def rows_of(start, rows):
    return pl.ds(pl.multiple_of(start * rows, rows), rows)


def gather_pushes(fsdp_size, ctx_size):
    steps = fsdp_size.bit_length() - 2
    return (ctx_size - 1) + ctx_size * (2**steps - 1) + 2**steps


class Gather:
    def __init__(self, link, ctx_size, whole, block, order):
        self.link, self.whole, self.block, self.order = link, whole, block, order
        self.ctx_size = ctx_size
        self.me, self.ctx = lax.axis_index("fsdp"), lax.axis_index("ctx")
        self.waits, self.crossed, self.after = {}, False, None

    def rows(self, fsdp, ctx):
        return self.whole.at[rows_of(fsdp * self.ctx_size + ctx, self.block)]

    def spread(self, stream, step):
        ctx = self.ctx if stream == 0 else 1 - self.ctx
        bit = self.order[step]
        to = {"fsdp": flip(self.me, bit)}
        copies = []
        for entry in subsets(self.order[:step]):
            place = self.rows(flip_all(self.me, entry), ctx)
            copies.append(self.link.push(place, place, to))
        self.waits[stream, step] = copies

    def arrive(self, *key):
        for copy in self.waits.pop(key):
            copy.wait_recv()

    def cross(self):
        if not self.crossed:
            self.crossed = True
            own = self.rows(self.me, self.ctx)
            self.waits["ctx",] = [
                self.link.push(own, own, {"ctx": 1 - self.ctx})
            ]

    def start(self):
        self.spread(0, 0)

    def next_step(self, stream, step):
        self.arrive(stream, step - 1)
        self.spread(stream, step)

    def other(self):
        self.cross()
        self.arrive("ctx")
        if self.after is not None:
            self.after.cross()
        self.spread(1, 0)

    def core(self):
        last = len(self.order) - 1
        for stream in range(self.ctx_size):
            self.arrive(stream, last)
        both = self.block * self.ctx_size
        copies = []
        for entry in subsets(self.order):
            place = self.whole.at[rows_of(flip_all(self.me, entry), both)]
            copies.append(self.link.push(place, place, {"fsdp": flip(self.me, 0)}))
        self.waits["core",] = copies

    def finish(self):
        self.arrive("core")

    def events(self):
        found = [self.start]
        for step in range(1, len(self.order)):
            found.append(functools.partial(self.next_step, 0, step))
        if self.ctx_size > 1:
            found.append(self.other)
            for step in range(1, len(self.order)):
                found.append(functools.partial(self.next_step, 1, step))
        return found + [self.core, self.finish]


def in_step(first, second):
    def run(one, two):
        one()
        two()

    return [functools.partial(run, one, two) for one, two in zip(first, second)]


class Total:
    def __init__(self, link, fsdp_size, ctx_size, held, arrived):
        self.link, self.held, self.arrived = link, held, arrived
        me, ctx = lax.axis_index("fsdp"), lax.axis_index("ctx")
        self.partners = [{"fsdp": flip(me, bit)} for bit in range(fsdp_size.bit_length() - 1)]
        if ctx_size > 1:
            self.partners.append({"ctx": 1 - ctx})

    def step(self, at):
        if at > 0:
            self.copy.wait_recv()
            self.held[at] = self.held[at - 1] + self.arrived[at - 1]
        if at < len(self.partners):
            self.copy = self.link.push(self.held.at[at], self.arrived.at[at], self.partners[at])

    def events(self):
        return [functools.partial(self.step, at) for at in range(len(self.partners) + 1)]


def dot_nn(left, right):
    return lax.dot_general(left, right, (((1,), (0,)), ((), ())), preferred_element_type=F32)


def dot_nt(left, right):
    return lax.dot_general(left, right, (((1,), (1,)), ((), ())), preferred_element_type=F32)


def dot_tn(left, right):
    return lax.dot_general(left, right, (((0,), (0,)), ((), ())), preferred_element_type=F32)


TILE = 256
ROOT_HALF = 0.7071067811865476
ROOT_TWO_PI = 2.5066282746310002
VECTORS, BIASES, SMALL_ROWS, RESULTS = 6, 3, 16, 6
PACE, SCATTER_PACE = 1.25, 1.25
FP = ((3, 2, 2, 2, 1, 1, 3), (3, 3, 3, 1, 0, 0, 3), (3, 1, 4, 2, 1, 1, 3))
BP = ((0, 1, 1, 1, 1, 1, 2, 2, 0, 0), (2, 1, 1, 1, 1, 2, 2, 1, 1, 2), (0, 0, 1, 0, 0, 0, 0, 1, 1, 1))
GAIN_A, SHIFT_A, OUT_B, GAIN_B, SHIFT_B, DOWN_B, QV_B, UP_B = range(8)


def lanes(at, count):
    return pl.ds(pl.multiple_of(at * count, count), count)


def standardized(values):
    centered = values - jnp.mean(values, axis=-1, keepdims=True)
    scale = lax.rsqrt(jnp.mean(centered * centered, axis=-1, keepdims=True) + EPS)
    return centered * scale, scale


def send_pieces(link, partial, sent, got, pieces, partner):
    copies = []
    for at in range(pieces):
        sent[at] = partial(at).astype(BF16)
        copies.append(link.push(sent.at[at], got.at[at], partner))
    return copies


def both_halves(copies, sent, got):
    found = []
    for at, copy in enumerate(copies):
        copy.wait_recv()
        found.append(sent[at].astype(F32) + got[at].astype(F32))
    return jnp.concatenate(found, axis=1)


class Stream:
    def __init__(self):
        self.waiting, self.count, self.done = [], 0, set()

    def release(self, group, events, begin, pace=1):
        for place, event in enumerate(events):
            self.waiting.append((begin + place * pace, self.count, group, event))
            self.count += 1
        self.waiting.sort(key=lambda entry: entry[:2])
        self.last = {entry[2]: entry for entry in self.waiting}

    def __call__(self, count):
        for entry in self.waiting[:count]:
            entry[3]()
            if self.last[entry[2]] is entry:
                self.done.add(entry[2])
        self.waiting = self.waiting[count:]

    def need(self, group):
        while group not in self.done:
            self(1)

    def rest(self):
        self(len(self.waiting))


def forward_kernel(ctx_size, fsdp_size, *refs):
    token_ref, mask_ref, live_ref = refs[:3]
    own_vectors = refs[3 : 3 + VECTORS]
    qv_ref, up_bias_ref, qkv_ref, out_weight_ref, up_ref, down_ref = refs[3 + VECTORS : 9 + VECTORS]
    out_ref, vector_ref = refs[9 + VECTORS : 11 + VECTORS]
    kept_out = refs[11 + VECTORS : 16 + VECTORS]
    (
        kv_out,
        pre_out,
        whole_ref,
        stream_ref,
        query_ref,
        log_total_ref,
        attended_ref,
        mid_ref,
        held,
        pre_ref,
        normed,
        hidden,
        kv,
        sent,
        got,
        small_held,
        small_got,
        send_sem,
        recv_sem,
        save_sem,
        kv_sem,
        pre_sem,
        kept_sem,
    ) = refs[16 + VECTORS :]
    kept = (stream_ref, query_ref, log_total_ref, attended_ref, mid_ref)
    layers, rows, width = stream_ref.shape
    cols = query_ref.shape[2]
    pieces = width // TILE
    pairs = PARTS // 2
    ctx = lax.axis_index("ctx")
    across = {"tp": 1 - lax.axis_index("tp")}
    greet(fsdp_size, ctx_size, True)
    link = Link(send_sem, recv_sem)
    pump = Stream()
    both = orders(fsdp_size)
    block = up_ref.shape[1]
    me = lax.axis_index("fsdp") * ctx_size + ctx
    here = rows_of(me, block)
    for layer in range(layers):
        for at in range(3):
            place = slice(at % 2 * cols, (at % 2 + 1) * cols)
            held[layer, at // 2, here, place] = qkv_ref[layer, at]
        held[layer, 1, here, cols:] = out_weight_ref[layer]
        for half in range(2):
            columns = slice(half * width, (half + 1) * width)
            held[layer, 2 + half, here, :] = up_ref[layer, :, columns]
            held[layer, 4 + half, here, :] = down_ref[layer, :, columns]
    shift = lax.broadcasted_iota(jnp.int32, (block, width), 0) + me * block
    shift = (shift == lax.broadcasted_iota(jnp.int32, (block, width), 1)).astype(BF16)
    placed = [dot_nn(vector[...], shift) for vector in own_vectors]
    unused = small_held.shape[1] - VECTORS * layers
    placed.append(jnp.zeros((unused, width), F32))
    small_held[0] = jnp.concatenate(placed, axis=0).astype(BF16)
    total = Total(link, fsdp_size, ctx_size, small_held, small_got)
    gathers, previous, keeps, saves, pre_saves, groups = (), (), {}, [], {}, 0
    for layer in range(layers):
        for pair in range(pairs):
            found = [
                Gather(
                    link,
                    ctx_size,
                    held.at[layer, part],
                    block,
                    both[part % 2],
                )
                for part in (2 * pair, 2 * pair + 1)
            ]
            for gather, before in zip(found, previous):
                before.after = gather
            previous = found
            if not gathers:
                gathers = found

            def keep(layer=layer, pair=pair):
                for part in (2 * pair, 2 * pair + 1):
                    copy = pltpu.make_async_copy(
                        held.at[layer, part], whole_ref.at[layer, part], save_sem.at[layer, part]
                    )
                    copy.start()
                    saves.append(copy)

            events = in_step(*[gather.events() for gather in found])
            pump.release((layer, pair), events, PACE * groups)
            keeps[layer, pair] = keep
            groups += 1

    def need(layer, pair):
        pump.need((layer, pair))
        keeps[layer, pair]()

    total.step(0)
    for gather in gathers:
        gather.cross()
    for at in range(1, len(total.partners) + 1):
        pump(1)
        total.step(at)
    vector_ref[...] = small_held[len(total.partners)].astype(F32)
    mask = mask_ref[...]
    stream_ref[0] = mask * token_ref[...].astype(F32)
    mine = rows_of(ctx, rows)
    pair_cols = 2 * HEAD_DIM
    lane = lax.broadcasted_iota(jnp.int32, (rows, pair_cols), 1)
    first = lane < HEAD_DIM
    live = live_ref[...] > 0
    log_total_ref[...] = jnp.zeros_like(log_total_ref)

    for layer in range(layers):
        def vector(which):
            at = which * layers + layer
            return vector_ref[at : at + 1, :]

        normal, _ = standardized(stream_ref[layer])
        normed[...] = (normal * vector(GAIN_A) + vector(SHIFT_A)).astype(BF16)
        need(layer, 0)

        @pl.loop(0, cols // TILE)
        def _(at):
            rows_in = normed[...]
            kv[layer, mine, lanes(at, TILE)] = dot_nn(
                rows_in, held[layer, 0, :, lanes(at + cols // TILE, TILE)]
            ).astype(BF16)
            kv[layer, mine, lanes(at + cols // TILE, TILE)] = (
                dot_nn(rows_in, held[layer, 1, :, lanes(at, TILE)])
                + qv_ref[layer, 1:2, lanes(at, TILE)].astype(F32)
            ).astype(BF16)

        kv_copy = None
        if ctx_size > 1:
            kv_copy = link.push(kv.at[layer, mine], kv.at[layer, mine], {"ctx": 1 - ctx})

        @pl.loop(0, cols // TILE)
        def _(at):
            query_ref[layer, :, lanes(at, TILE)] = (
                dot_nn(normed[...], held[layer, 0, :, lanes(at, TILE)]) + qv_ref[layer, 0:1, lanes(at, TILE)].astype(F32)
            ).astype(BF16)

        pump(FP[layer][0])
        if kv_copy is not None:
            kv_copy.wait_recv()
        save = pltpu.make_async_copy(kv.at[layer], kv_out.at[layer], kv_sem.at[layer])
        save.start()
        saves.append(save)

        for half in range(2):
            per_half = cols // pair_cols // 2

            @pl.loop(half * per_half, (half + 1) * per_half)
            def _(at):
                queries = query_ref[layer, :, lanes(at, pair_cols)]
                keys = kv[layer, :, lanes(at, pair_cols)]
                values = kv[layer, :, lanes(at + cols // pair_cols, pair_cols)]
                found = []
                for head in range(2):
                    chosen = jnp.where(
                        first if head == 0 else ~first, queries, jnp.zeros_like(queries)
                    )
                    scores = jnp.where(live, dot_nt(chosen, keys) * HEAD_DIM**-0.5, NEG)
                    top = jnp.max(scores, axis=-1, keepdims=True)
                    weights = jnp.exp(scores - top)
                    summed = jnp.sum(weights, axis=-1, keepdims=True)
                    log_total_ref[layer] = jnp.where(
                        lane == 2 * at + head, top + jnp.log(summed), log_total_ref[layer]
                    )
                    found.append(dot_nn((weights * (1.0 / summed)).astype(BF16), values))
                attended_ref[layer, :, lanes(at, pair_cols)] = jnp.where(
                    first, found[0], found[1]
                ).astype(BF16)

            pump(FP[layer][1 + half])

        def out_partial(at):
            return dot_nt(attended_ref[layer], held[layer, 1, at * TILE : (at + 1) * TILE, cols:])

        copies = send_pieces(link, out_partial, sent.at[layer, 0], got.at[0], pieces, across)
        pump(FP[layer][3])
        branch = both_halves(copies, sent.at[layer, 0], got.at[0])
        mid = stream_ref[layer] + mask * (branch + vector(OUT_B))
        mid_ref[layer] = mid
        normal, _ = standardized(mid)
        normed[...] = (normal * vector(GAIN_B) + vector(SHIFT_B)).astype(BF16)
        need(layer, 1)
        if layer >= 2:
            pre_saves.pop(layer - 2).wait()
        for part in range(2):

            @pl.loop(0, pieces)
            def _(at):
                pre = dot_nn(normed[...], held[layer, 2 + part, :, lanes(at, TILE)]) + up_bias_ref[
                    layer : layer + 1, lanes(at + part * pieces, TILE)
                ].astype(F32)
                pre_ref[layer % 2, part, :, lanes(at, TILE)] = pre
                hidden[part, :, lanes(at, TILE)] = (
                    0.5 * pre * (1.0 + lax.erf(pre * ROOT_HALF))
                ).astype(BF16)

            pump(FP[layer][4 + part])
        pre_saves[layer] = pltpu.make_async_copy(
            pre_ref.at[layer % 2], pre_out.at[layer], pre_sem.at[layer]
        )
        pre_saves[layer].start()
        need(layer, 2)

        def down_partial(at):
            here = slice(at * TILE, (at + 1) * TILE)
            return dot_nt(hidden[0], held[layer, 4, here, :]) + dot_nt(
                hidden[1], held[layer, 5, here, :]
            )

        copies = send_pieces(link, down_partial, sent.at[layer, 1], got.at[1], pieces, across)
        pump(FP[layer][6])
        branch = both_halves(copies, sent.at[layer, 1], got.at[1])
        for at, held_here in enumerate(kept):
            save = pltpu.make_async_copy(
                held_here.at[layer], kept_out[at].at[layer], kept_sem.at[layer, at]
            )
            save.start()
            saves.append(save)
        after = mid_ref[layer] + mask * (branch + vector(DOWN_B))
        if layer + 1 < layers:
            stream_ref[layer + 1] = after
        else:
            out_ref[...] = after.astype(BF16)
    pump.rest()
    link.drain()
    for save in (*saves, *pre_saves.values()):
        save.wait()


def forward_all(mesh, tokens, mask, live, own_vectors, qv_bias, up_bias, qkv, out_t, up, down_t):
    fsdp_size, ctx_size = mesh.shape["fsdp"], mesh.shape["ctx"]
    rows, width = tokens.shape
    layers, _, _, cols = qkv.shape
    part_cols = 2 * cols
    small = (-(-VECTORS * layers // 16) * 16, width)
    slots_all = rows * ctx_size
    pieces = width // TILE
    steps = fsdp_size.bit_length() - 1 + (ctx_size > 1)
    shape = jax.ShapeDtypeStruct
    whole = (layers, PARTS, width, part_cols)
    kept = [
        shape((layers, rows, width), F32),
        shape((layers, rows, cols), BF16),
        shape((layers, rows, 2 * HEAD_DIM), F32),
        shape((layers, rows, cols), BF16),
        shape((layers, rows, width), F32),
    ]
    out_shape = [
        shape((rows, width), BF16),
        shape(small, F32),
        *kept,
        shape((layers, slots_all, 2 * cols), BF16),
        shape((layers, 2, rows, width), F32),
        shape(whole, BF16),
    ]
    vmem = pl.BlockSpec(memory_space=pltpu.VMEM)
    any_space = pl.BlockSpec(memory_space=pl.ANY)
    pushes = (
        layers * ((ctx_size > 1) + 2 * pieces + gather_pushes(fsdp_size, ctx_size) * PARTS)
        + steps
    )
    return pl.pallas_call(
        functools.partial(forward_kernel, ctx_size, fsdp_size),
        out_shape=out_shape,
        in_specs=[vmem] * (9 + VECTORS),
        out_specs=[vmem] * 2 + [any_space] * 8,
        scratch_shapes=[pltpu.VMEM(one.shape, one.dtype) for one in kept]
        + [
            pltpu.VMEM(whole, BF16),
            pltpu.VMEM((2, 2, rows, width), F32),
            pltpu.VMEM((rows, width), BF16),
            pltpu.VMEM((2, rows, width), BF16),
            pltpu.VMEM((layers, slots_all, 2 * cols), BF16),
            pltpu.VMEM((layers, 2, pieces, rows, TILE), BF16),
            pltpu.VMEM((2, pieces, rows, TILE), BF16),
            pltpu.VMEM((steps + 1,) + small, BF16),
            pltpu.VMEM((steps,) + small, BF16),
            pltpu.SemaphoreType.DMA((pushes,)),
            pltpu.SemaphoreType.DMA((pushes,)),
            pltpu.SemaphoreType.DMA((layers, PARTS)),
            pltpu.SemaphoreType.DMA((layers,)),
            pltpu.SemaphoreType.DMA((layers,)),
            pltpu.SemaphoreType.DMA((layers, len(kept))),
        ],
        compiler_params=pltpu.CompilerParams(
            collective_id=0, has_side_effects=True, vmem_limit_bytes=63 * 2**20
        ),
        name="forward_all",
    )(tokens, mask, live, *own_vectors, qv_bias, up_bias, qkv, out_t, up, down_t)


class Scatter:
    def __init__(self, link, ctx_size, terms, arrived, last, order, credits, first, final, write):
        self.link, self.terms, self.arrived, self.last = link, terms, arrived, last
        self.ctx_size, self.order, self.write = ctx_size, order, write
        self.credits, self.first, self.final = credits, first, final
        self.me, self.ctx = lax.axis_index("fsdp"), lax.axis_index("ctx")
        self.slots = 2 ** len(order)
        self.both = terms.shape[0] // (2 * self.slots)
        self.flips = [
            [bit for at, bit in enumerate(order) if (slot >> (len(order) - 1 - at)) % 2 == 1]
            for slot in range(self.slots)
        ]
        self.base, self.sent = 0, []

    def place(self, slot, core=0):
        start = flip(self.me, 0) if core else self.me
        return rows_of(flip_all(start, self.flips[slot]), self.both)

    def send(self, step, pieces, to):
        if not self.first:
            pl.semaphore_wait(self.credits.at[step], 1)
        self.copies = [self.link.push(src, dst, to) for src, dst in pieces]
        self.sent += self.copies

    def read(self, step, to):
        if not self.final:
            pl.semaphore_signal(
                self.credits.at[step], inc=1, device_id=to, device_id_type=MESH
            )

    def start(self):
        self.send(
            0,
            [
                (self.terms.at[self.place(slot, 1)], self.arrived.at[slot])
                for slot in range(self.slots)
            ],
            {"fsdp": flip(self.me, 0)},
        )

    def take(self, step, count, to):
        for copy in self.copies:
            copy.wait_recv()
        for slot in range(count):
            here = self.place(slot)
            self.terms[here, :] = self.terms[here, :] + self.arrived[self.base + slot]
        self.base += count
        self.read(step, to)

    def step(self, at):
        count = self.slots >> at
        self.take(at, count, {"fsdp": flip(self.me, 0 if at == 0 else self.order[at - 1])})
        half = count // 2
        self.send(
            at + 1,
            [
                (self.terms.at[self.place(half + slot)], self.arrived.at[self.base + slot])
                for slot in range(half)
            ],
            {"fsdp": flip(self.me, self.order[at])},
        )

    def across(self):
        steps = len(self.order)
        self.take(steps, 1, {"fsdp": flip(self.me, self.order[-1])})
        if self.ctx_size > 1:
            block = self.both // self.ctx_size
            theirs = rows_of(self.me * self.ctx_size + 1 - self.ctx, block)
            self.send(steps + 1, [(self.terms.at[theirs], self.last)], {"ctx": 1 - self.ctx})

    def finish(self):
        block = self.both // self.ctx_size
        total = self.terms[rows_of(self.me * self.ctx_size + self.ctx, block), :].astype(F32)
        if self.ctx_size > 1:
            for copy in self.copies:
                copy.wait_recv()
            total = total + self.last[...].astype(F32)
            self.read(len(self.order) + 1, {"ctx": 1 - self.ctx})
        self.write(total)
        self.link.settle(self.sent)

    def events(self):
        found = [self.start]
        for at in range(len(self.order)):
            found.append(functools.partial(self.step, at))
        return found + [self.across, self.finish]


def norm_pull(normal, scale, gain, grad):
    grad_gain = jnp.sum(grad * normal, axis=0, keepdims=True)
    grad_shift = jnp.sum(grad, axis=0, keepdims=True)
    inner = grad * gain
    along = jnp.mean(inner * normal, axis=-1, keepdims=True)
    grad_in = scale * (inner - jnp.mean(inner, axis=-1, keepdims=True) - normal * along)
    return grad_in, grad_gain, grad_shift


def backward_kernel(ctx_size, fsdp_size, *refs):
    (
        cotangent_ref,
        mask_ref,
        live_ref,
        vector_ref,
        stream_all,
        query_all,
        log_total_all,
        attended_all,
        mid_all,
        kv_all,
        pre_all,
        whole_ref,
        out_ref,
        qkv_ref,
        out_weight_ref,
        up_ref,
        down_ref,
        small_ref,
        stream_ref,
        query_ref,
        log_total_ref,
        attended_ref,
        mid_ref,
        kv_ref,
        pre_ref,
        held,
        terms,
        arrived,
        last,
        turned,
        low,
        low_pre,
        hidden,
        grad_att,
        grad_qk,
        grad_kv,
        kv_sent,
        kv_got,
        sent,
        got,
        small_held,
        small_got,
        send_sem,
        recv_sem,
        load_sem,
        pre_sem,
        kept_sem,
        credits,
    ) = refs
    layers, rows, width = stream_ref.shape
    cols = query_ref.shape[2]
    pieces = width // TILE
    pairs = PARTS // 2
    ctx = lax.axis_index("ctx")
    across = {"tp": 1 - lax.axis_index("tp")}
    loads = {}

    def bring(layer, parts):
        if layer >= 0:
            for part in parts:
                copy = pltpu.make_async_copy(
                    whole_ref.at[layer, part], held.at[part], load_sem.at[part]
                )
                copy.start()
                loads[layer, part] = copy

    def bring_pre(layer):
        if layer >= 0:
            copy = pltpu.make_async_copy(
                pre_all.at[layer], pre_ref.at[layer % 2], pre_sem.at[layer % 2]
            )
            copy.start()
            loads[layer, "pre"] = copy

    kept = {
        "mid": (mid_all, mid_ref),
        "query": (query_all, query_ref),
        "kv": (kv_all, kv_ref),
        "log_total": (log_total_all, log_total_ref),
        "attended": (attended_all, attended_ref),
        "stream": (stream_all, stream_ref),
    }

    def ready(layer, *names):
        for name in names:
            loads[layer, name].wait()

    bring_pre(layers - 1)
    bring(layers - 1, (4, 5, 2, 3, 1, 0))
    for layer in reversed(range(layers)):
        for at, (name, (source, target)) in enumerate(kept.items()):
            copy = pltpu.make_async_copy(
                source.at[layer], target.at[layer], kept_sem.at[layer, at]
            )
            copy.start()
            loads[layer, name] = copy
    small_held[...] = jnp.zeros_like(small_held)
    greet(fsdp_size, ctx_size, True)
    link = Link(send_sem, recv_sem)
    pump = Stream()
    both = [order[::-1] for order in orders(fsdp_size)]
    mask = mask_ref[...]
    pair_cols = 2 * HEAD_DIM
    lane = lax.broadcasted_iota(jnp.int32, (rows, pair_cols), 1)
    first = lane < HEAD_DIM
    live = live_ref[...] > 0
    mine, theirs = rows_of(ctx, rows), rows_of(1 - ctx, rows)
    groups = 0
    last_sent = {}

    def scatter(layer, pair):
        nonlocal groups

        def writer(part):
            def write(value):
                if part == 0:
                    qkv_ref[layer, 0] = value[:, :cols]
                    qkv_ref[layer, 1] = value[:, cols:]
                elif part == 1:
                    qkv_ref[layer, 2] = value[:, :cols]
                    out_weight_ref[layer] = value[:, cols:]
                else:
                    target = up_ref if part < 4 else down_ref
                    target[layer, :, part % 2 * width : (part % 2 + 1) * width] = value

            return write

        events = in_step(
            *[
                Scatter(
                    link,
                    ctx_size,
                    terms.at[part],
                    arrived.at[part],
                    last.at[part],
                    both[part % 2],
                    credits.at[part],
                    layer == layers - 1,
                    layer == 0,
                    writer(part),
                ).events()
                for part in (2 * pair, 2 * pair + 1)
            ]
        )
        events[0]()
        pump.release((layer, pair), events[1:], SCATTER_PACE * groups)
        groups += 1

    def free(layer, pair):
        if layer < layers - 1:
            pump.need((layer + 1, pair))

    def product(part, start, count, right):
        @pl.loop(0, count)
        def _(at):
            terms[part, :, lanes(at + start, TILE)] = dot_nn(turned[...], right(at)).astype(BF16)

    def up_products(layer, vector):
        normal, _ = standardized(mid_ref[layer])
        turned[...] = jnp.transpose(
            (normal * vector(GAIN_B) + vector(SHIFT_B)).astype(BF16)
        )
        free(layer, 1)
        for part in range(2):
            product(2 + part, 0, pieces, lambda at, part=part: low_pre[part, :, lanes(at, TILE)])
        scatter(layer, 1)

    out_ref[...] = cotangent_ref[...].astype(F32)
    for layer in reversed(range(layers)):
        rows_small = small_held.at[layer, 0]

        def vector(which):
            at = which * layers + layer
            return vector_ref[at : at + 1, :]

        def keep_row(which, value):
            rows_small[which : which + 1, :] = value

        bring_pre(layer - 1)
        grad = out_ref[...]
        masked = mask * grad
        keep_row(DOWN_B, jnp.sum(masked, axis=0, keepdims=True))
        low[...] = masked.astype(BF16)
        turned[...] = jnp.transpose(low[...])
        loads[layer, "pre"].wait()
        for part in range(2):
            loads[layer, 4 + part].wait()

            @pl.loop(0, pieces)
            def _(at):
                pre = pre_ref[layer % 2, part, :, lanes(at, TILE)]
                chance = 0.5 * (1.0 + lax.erf(pre * ROOT_HALF))
                hidden[part, :, lanes(at, TILE)] = (pre * chance).astype(BF16)
                slope = chance + pre * (jnp.exp(-0.5 * pre * pre) * (1.0 / ROOT_TWO_PI))
                grad_pre = dot_nn(low[...], held[4 + part, :, lanes(at, TILE)]) * slope
                rows_small[UP_B + part : UP_B + part + 1, lanes(at, TILE)] = jnp.sum(
                    grad_pre, axis=0, keepdims=True
                )
                low_pre[part, :, lanes(at, TILE)] = grad_pre.astype(BF16)

            pump(BP[layer][part])
        bring(layer - 1, (4, 5))
        for part in (2, 3):
            loads[layer, part].wait()

        def up_partial(at):
            here = slice(at * TILE, (at + 1) * TILE)
            return dot_nt(low_pre[0], held[2, here, :]) + dot_nt(low_pre[1], held[3, here, :])

        if layer < layers - 1:
            link.settle(last_sent["up"])
        copies = send_pieces(link, up_partial, sent.at[0], got.at[0], pieces, across)
        last_sent["up"] = copies
        bring(layer - 1, (2, 3))
        free(layer, 2)
        for part in range(2):
            product(4 + part, 0, pieces, lambda at, part=part: hidden[part, :, lanes(at, TILE)])
        scatter(layer, 2)
        ready(layer, "mid")
        if layer == layers - 1:
            up_products(layer, vector)
        pump(BP[layer][2])
        grad_normed = both_halves(copies, sent.at[0], got.at[0])
        normal, scale = standardized(mid_ref[layer])
        grad_in, grad_gain, grad_shift = norm_pull(normal, scale, vector(GAIN_B), grad_normed)
        keep_row(GAIN_B, grad_gain)
        keep_row(SHIFT_B, grad_shift)
        grad_mid = out_ref[...] + grad_in
        out_ref[...] = grad_mid
        masked = mask * grad_mid
        keep_row(OUT_B, jnp.sum(masked, axis=0, keepdims=True))
        low[...] = masked.astype(BF16)
        loads[layer, 1].wait()

        @pl.loop(0, cols // TILE)
        def _(at):
            grad_att[:, lanes(at, TILE)] = dot_nn(
                low[...], held[1, :, lanes(at + cols // TILE, TILE)]
            ).astype(BF16)

        pump(BP[layer][3])
        ready(layer, "query", "kv", "log_total")
        for half in range(2):
            per_half = cols // pair_cols // 2

            @pl.loop(half * per_half, (half + 1) * per_half)
            def _(at):
                queries = query_ref[layer, :, lanes(at, pair_cols)]
                grads = grad_att[:, lanes(at, pair_cols)]
                keys = kv_ref[layer, :, lanes(at, pair_cols)]
                values = kv_ref[layer, :, lanes(at + cols // pair_cols, pair_cols)]
                found, key_grad, value_grad = [], None, None
                for head in range(2):
                    here = first if head == 0 else ~first
                    query = jnp.where(here, queries, jnp.zeros_like(queries))
                    one_grad = jnp.where(here, grads, jnp.zeros_like(grads))
                    scores = jnp.where(live, dot_nt(query, keys) * HEAD_DIM**-0.5, NEG)
                    log_total = jnp.sum(
                        jnp.where(lane == 2 * at + head, log_total_ref[layer], 0.0),
                        axis=-1,
                        keepdims=True,
                    )
                    weights = jnp.exp(scores - log_total)
                    grad_weights = dot_nt(one_grad, values)
                    along = jnp.sum(weights * grad_weights, axis=-1, keepdims=True)
                    grad_scores = (weights * (grad_weights - along)).astype(BF16)
                    found.append(dot_nn(grad_scores, keys))
                    one = dot_tn(grad_scores, query)
                    two = dot_tn(weights.astype(BF16), one_grad)
                    key_grad = one if head == 0 else key_grad + one
                    value_grad = two if head == 0 else value_grad + two
                grad_qk[:, lanes(at, pair_cols)] = (
                    jnp.where(first, found[0], found[1]) * HEAD_DIM**-0.5
                ).astype(BF16)
                grad_kv[:, lanes(at, pair_cols)] = key_grad * HEAD_DIM**-0.5
                grad_kv[:, lanes(at + cols // pair_cols, pair_cols)] = value_grad

            pump(BP[layer][4 + half])
        kv_copy = None
        if ctx_size > 1:
            if layer < layers - 1:
                link.settle([last_sent["kv"]])
            kv_sent[...] = grad_kv[theirs, :].astype(BF16)
            kv_copy = link.push(kv_sent, kv_got.at[layer], {"ctx": 1 - ctx})
            last_sent["kv"] = kv_copy
        pump(BP[layer][6])
        if layer < layers - 1:
            up_products(layer, vector)
        pump(BP[layer][7])
        total_kv = grad_kv[mine, :]
        if kv_copy is not None:
            kv_copy.wait_recv()
            total_kv = total_kv + kv_got[layer].astype(F32)
        grad_qk[:, cols:] = total_kv.astype(BF16)
        rows_small[QV_B : QV_B + 1, :cols] = jnp.sum(
            grad_qk[:, :cols].astype(F32), axis=0, keepdims=True
        )
        rows_small[QV_B : QV_B + 1, cols:] = jnp.sum(
            grad_qk[:, 2 * cols :].astype(F32), axis=0, keepdims=True
        )
        loads[layer, 0].wait()

        def in_partial(at):
            here = slice(at * TILE, (at + 1) * TILE)
            return dot_nt(grad_qk[:, : 2 * cols], held[0, here, :]) + dot_nt(
                grad_qk[:, 2 * cols :], held[1, here, :cols]
            )

        if layer < layers - 1:
            link.settle(last_sent["in"])
        copies = send_pieces(link, in_partial, sent.at[1], got.at[1], pieces, across)
        last_sent["in"] = copies
        bring(layer - 1, (1, 0))
        pump(BP[layer][8])
        ready(layer, "attended", "stream")
        free(layer, 0)
        turned[...] = jnp.transpose(low[...])
        product(1, cols // TILE, cols // TILE, lambda at: attended_ref[layer, :, lanes(at, TILE)])
        normal, scale = standardized(stream_ref[layer])
        turned[...] = jnp.transpose(
            (normal * vector(GAIN_A) + vector(SHIFT_A)).astype(BF16)
        )
        product(0, 0, 2 * cols // TILE, lambda at: grad_qk[:, lanes(at, TILE)])
        product(1, 0, cols // TILE, lambda at: grad_qk[:, lanes(at + 2 * cols // TILE, TILE)])
        scatter(layer, 0)
        pump(BP[layer][9])
        grad_normed = both_halves(copies, sent.at[1], got.at[1])
        normal, scale = standardized(stream_ref[layer])
        grad_in, grad_gain, grad_shift = norm_pull(normal, scale, vector(GAIN_A), grad_normed)
        keep_row(GAIN_A, grad_gain)
        keep_row(SHIFT_A, grad_shift)
        grad = out_ref[...] + grad_in
        out_ref[...] = grad if layer > 0 else mask * grad
        total = Total(link, fsdp_size, ctx_size, small_held.at[layer], small_got.at[layer])
        pump.release(("small", layer), total.events(), SCATTER_PACE * (groups - 1))
    pump.rest()
    for layer in range(layers):
        for row in range(VECTORS + BIASES):
            at = row * layers + layer
            small_ref[at : at + 1, :] = small_held[
                layer, small_held.shape[1] - 1, row : row + 1, :
            ]
    link.drain()


def backward_all(mesh, cotangent, mask, live, vectors, kept, whole):
    fsdp_size, ctx_size = mesh.shape["fsdp"], mesh.shape["ctx"]
    rows, width = cotangent.shape
    layers, _, _, part_cols = whole.shape
    cols = width // mesh.shape["tp"]
    slots_all = rows * ctx_size
    pieces = width // TILE
    slots = fsdp_size // 2
    both = width // fsdp_size
    block = both // ctx_size
    bits = fsdp_size.bit_length() - 1
    steps = bits + (ctx_size > 1)
    shape = jax.ShapeDtypeStruct
    vmem = pl.BlockSpec(memory_space=pltpu.VMEM)
    any_space = pl.BlockSpec(memory_space=pl.ANY)
    operands = [cotangent, mask, live, vectors, *kept, whole]
    pushes = layers * ((ctx_size > 1) + 2 * pieces + PARTS * (2 * slots) + steps)
    return pl.pallas_call(
        functools.partial(backward_kernel, ctx_size, fsdp_size),
        out_shape=[
            shape((rows, width), F32),
            shape((layers, 3, block, cols), F32),
            shape((layers, block, cols), F32),
            shape((layers, block, 2 * width), F32),
            shape((layers, block, 2 * width), F32),
            shape((-(-(VECTORS + BIASES) * layers // 8) * 8, width), F32),
        ],
        in_specs=[vmem] * 4 + [any_space] * (len(operands) - 4),
        out_specs=[vmem] * 6,
        scratch_shapes=[pltpu.VMEM(one.shape, one.dtype) for one in kept[:6]]
        + [
            pltpu.VMEM((2, 2, rows, width), F32),
            pltpu.VMEM(whole.shape[1:], BF16),
            pltpu.VMEM(whole.shape[1:], BF16),
            pltpu.VMEM((PARTS, 2 * slots - 1, both, part_cols), BF16),
            pltpu.VMEM((PARTS, block, part_cols), BF16),
            pltpu.VMEM((width, rows), BF16),
            pltpu.VMEM((rows, width), BF16),
            pltpu.VMEM((2, rows, width), BF16),
            pltpu.VMEM((2, rows, width), BF16),
            pltpu.VMEM((rows, cols), BF16),
            pltpu.VMEM((rows, 3 * cols), BF16),
            pltpu.VMEM((slots_all, 2 * cols), F32),
            pltpu.VMEM((rows, 2 * cols), BF16),
            pltpu.VMEM((layers, rows, 2 * cols), BF16),
            pltpu.VMEM((2, pieces, rows, TILE), BF16),
            pltpu.VMEM((2, pieces, rows, TILE), BF16),
            pltpu.VMEM((layers, steps + 1, SMALL_ROWS, width), F32),
            pltpu.VMEM((layers, steps, SMALL_ROWS, width), F32),
            pltpu.SemaphoreType.DMA((pushes,)),
            pltpu.SemaphoreType.DMA((pushes,)),
            pltpu.SemaphoreType.DMA((PARTS,)),
            pltpu.SemaphoreType.DMA((2,)),
            pltpu.SemaphoreType.DMA((layers, 6)),
            pltpu.SemaphoreType.REGULAR((PARTS, steps + 1)),
        ],
        compiler_params=pltpu.CompilerParams(
            collective_id=1, has_side_effects=True, vmem_limit_bytes=63 * 2**20
        ),
        name="backward_all",
    )(*operands)


def finish_kernel(ctx_size, layers, *refs):
    count = RESULTS
    sources, small_ref = refs[:count], refs[count]
    targets = refs[count + 1 : 2 * count + 1]
    vectors = refs[2 * count + 1 : 2 * count + 1 + VECTORS]
    qv_ref, up_bias_ref = refs[2 * count + 1 + VECTORS : 2 * count + 3 + VECTORS]
    rooms = refs[2 * count + 3 + VECTORS : 3 * count + 3 + VECTORS]
    in_sem, out_sem = refs[3 * count + 3 + VECTORS :]
    brings = [
        pltpu.make_async_copy(source, room, in_sem.at[at])
        for at, (source, room) in enumerate(zip(sources, rooms))
    ]
    for copy in brings:
        copy.start()
    width = small_ref.shape[1]
    block = vectors[0].shape[1]
    here = (lax.axis_index("fsdp") * ctx_size + lax.axis_index("ctx")) * block
    turned = pltpu.roll(small_ref[...], (width - here) % width, 1)
    for at, vector in enumerate(vectors):
        vector[...] = turned[at * layers : (at + 1) * layers, :block]
    cols = qv_ref.shape[2]
    for layer in range(layers):
        row = QV_B * layers + layer
        for half in range(2):
            qv_ref[layer, half : half + 1, :] = small_ref[
                row : row + 1, half * cols : (half + 1) * cols
            ]
    for half in range(up_bias_ref.shape[1] // width):
        row = (UP_B + half) * layers
        up_bias_ref[:, half * width : (half + 1) * width] = small_ref[row : row + layers, :]
    sends = []
    for at, copy in enumerate(brings):
        copy.wait()
        send = pltpu.make_async_copy(rooms[at], targets[at], out_sem.at[at])
        send.start()
        sends.append(send)
    for send in sends:
        send.wait()


def finish(mesh, results, small, layers, block, units):
    width = small.shape[1]
    shape = jax.ShapeDtypeStruct
    vmem = pl.BlockSpec(memory_space=pltpu.VMEM)
    any_space = pl.BlockSpec(memory_space=pl.ANY)
    return pl.pallas_call(
        functools.partial(finish_kernel, mesh.shape["ctx"], layers),
        out_shape=[shape(one.shape, one.dtype) for one in results]
        + [shape((layers, block), F32)] * VECTORS
        + [shape((layers, 2, width // mesh.shape["tp"]), F32), shape((layers, units), F32)],
        in_specs=[any_space] * RESULTS + [vmem],
        out_specs=[any_space] * RESULTS + [vmem] * (VECTORS + 2),
        scratch_shapes=[pltpu.VMEM(one.shape, one.dtype) for one in results]
        + [pltpu.SemaphoreType.DMA((RESULTS,)), pltpu.SemaphoreType.DMA((RESULTS,))],
        compiler_params=pltpu.CompilerParams(vmem_limit_bytes=63 * 2**20),
        name="finish",
    )(*results, small)


def body(
    mesh,
    tokens,
    lengths,
    cotangent,
    attn_gain,
    attn_shift,
    qkv_weight,
    qv_bias,
    out_weight,
    out_bias,
    mlp_gain,
    mlp_shift,
    up_weight,
    up_bias,
    down_weight,
    down_bias,
):
    images, local_slots, width = tokens.shape
    ctx_size = mesh.shape["ctx"]
    rows_here, slots_all = images * local_slots, local_slots * ctx_size
    layers, block, _, cols = qkv_weight.shape
    units = up_weight.shape[2]
    slot_ids = lax.axis_index("ctx") * local_slots + jnp.arange(local_slots, dtype=jnp.int32)
    mask = (slot_ids[None, :] < lengths[:, None]).astype(F32).reshape(rows_here, 1)
    live = (jnp.arange(slots_all, dtype=jnp.int32)[None, :] < lengths[:, None]).astype(F32)
    own_vectors = (attn_gain, attn_shift, out_bias, mlp_gain, mlp_shift, down_bias)
    output, vectors, *kept, whole = forward_all(
        mesh,
        tokens.reshape(rows_here, width),
        mask,
        live,
        own_vectors,
        qv_bias,
        up_bias,
        jnp.swapaxes(qkv_weight, 1, 2),
        jnp.swapaxes(out_weight, 1, 2),
        up_weight,
        jnp.swapaxes(down_weight, 1, 2),
    )
    *results, little = backward_all(
        mesh, cotangent.reshape(rows_here, width), mask, live, vectors, kept, whole
    )
    results = finish(mesh, [output, *results], little, layers, block, units)
    output, input_grad, grad_qkv, grad_out, grad_up, grad_down = results[:RESULTS]
    own = results[RESULTS : RESULTS + VECTORS]
    grad_qv, grad_up_bias = results[RESULTS + VECTORS :]
    return (
        output.reshape(tokens.shape),
        input_grad.reshape(tokens.shape),
        own[GAIN_A],
        own[SHIFT_A],
        jnp.swapaxes(grad_qkv, 1, 2),
        grad_qv,
        jnp.swapaxes(grad_out, 1, 2),
        own[OUT_B],
        own[GAIN_B],
        own[SHIFT_B],
        grad_up,
        grad_up_bias,
        jnp.swapaxes(grad_down, 1, 2),
        own[DOWN_B],
    )


def solution(mesh):
    place = P(None, ("fsdp", "ctx"))
    rows = P("fsdp", "ctx", None)
    return jax.shard_map(
        functools.partial(body, mesh),
        mesh=mesh,
        in_specs=(
            rows,
            P("fsdp"),
            rows,
            place,
            place,
            P(None, ("fsdp", "ctx"), None, "tp"),
            P(None, None, "tp"),
            P(None, "tp", ("fsdp", "ctx")),
            place,
            place,
            place,
            P(None, ("fsdp", "ctx"), "tp"),
            P(None, "tp"),
            P(None, "tp", ("fsdp", "ctx")),
            place,
        ),
        out_specs=(
            rows,
            rows,
            place,
            place,
            P(None, ("fsdp", "ctx"), None, "tp"),
            P(None, None, "tp"),
            P(None, "tp", ("fsdp", "ctx")),
            place,
            place,
            place,
            P(None, ("fsdp", "ctx"), "tp"),
            P(None, "tp"),
            P(None, "tp", ("fsdp", "ctx")),
            place,
        ),
        check_vma=False,
    )
```

```python
import functools

import jax
import jax.numpy as jnp
from jax import lax
from jax.experimental import pallas as pl
from jax.experimental.pallas import tpu as pltpu
from jax.sharding import PartitionSpec as P

HEAD_DIM = 64
EPS = 1e-05
NEG = -30000.0
MESH = pl.DeviceIdType.MESH
PARTS = 6
BF16 = jnp.bfloat16
F32 = jnp.float32


def flip(index, bit):
    size = 2**bit
    return index + size - 2 * size * ((index // size) % 2)


def flip_all(index, bits):
    for bit in bits:
        index = flip(index, bit)
    return index


def subsets(bits):
    found = [()]
    for bit in bits:
        found = found + [entry + (bit,) for entry in found]
    return found


def orders(fsdp_size):
    top = fsdp_size.bit_length() - 1
    bits = list(range(1, top))
    half = len(bits) // 2
    return bits, bits[half:] + bits[:half]


class Link:
    def __init__(self, send_sem, recv_sem):
        self.send_sem, self.recv_sem, self.used, self.sent = send_sem, recv_sem, 0, []

    def push(self, src, dst, device):
        at = self.used
        self.used += 1
        copy = pltpu.make_async_remote_copy(
            src_ref=src,
            dst_ref=dst,
            send_sem=self.send_sem.at[at],
            recv_sem=self.recv_sem.at[at],
            device_id=device,
            device_id_type=MESH,
        )
        copy.start()
        self.sent.append(copy)
        return copy

    def settle(self, copies):
        for copy in copies:
            copy.wait_send()
            self.sent = [other for other in self.sent if other is not copy]

    def drain(self):
        for copy in self.sent:
            copy.wait_send()
        self.sent = []


def greet(fsdp_size, ctx_size, with_tp):
    me, ctx, tp = lax.axis_index("fsdp"), lax.axis_index("ctx"), lax.axis_index("tp")
    barrier = pltpu.get_barrier_semaphore()
    count = 0
    for bit in range(fsdp_size.bit_length() - 1):
        pl.semaphore_signal(
            barrier, inc=1, device_id={"fsdp": flip(me, bit)}, device_id_type=MESH
        )
        count += 1
    if ctx_size > 1:
        pl.semaphore_signal(barrier, inc=1, device_id={"ctx": 1 - ctx}, device_id_type=MESH)
        count += 1
    if with_tp:
        pl.semaphore_signal(barrier, inc=1, device_id={"tp": 1 - tp}, device_id_type=MESH)
        count += 1
    pl.semaphore_wait(barrier, count)


def rows_of(start, rows):
    return pl.ds(pl.multiple_of(start * rows, rows), rows)


def gather_pushes(fsdp_size, ctx_size):
    steps = fsdp_size.bit_length() - 2
    return (ctx_size - 1) + ctx_size * (2**steps - 1) + 2**steps


class Gather:
    def __init__(self, link, ctx_size, whole, block, order):
        self.link, self.whole, self.block, self.order = link, whole, block, order
        self.ctx_size = ctx_size
        self.me, self.ctx = lax.axis_index("fsdp"), lax.axis_index("ctx")
        self.waits, self.crossed, self.after = {}, False, None

    def rows(self, fsdp, ctx):
        return self.whole.at[rows_of(fsdp * self.ctx_size + ctx, self.block)]

    def spread(self, stream, step):
        ctx = self.ctx if stream == 0 else 1 - self.ctx
        bit = self.order[step]
        to = {"fsdp": flip(self.me, bit)}
        copies = []
        for entry in subsets(self.order[:step]):
            place = self.rows(flip_all(self.me, entry), ctx)
            copies.append(self.link.push(place, place, to))
        self.waits[stream, step] = copies

    def arrive(self, *key):
        for copy in self.waits.pop(key):
            copy.wait_recv()

    def cross(self):
        if not self.crossed:
            self.crossed = True
            own = self.rows(self.me, self.ctx)
            self.waits["ctx",] = [
                self.link.push(own, own, {"ctx": 1 - self.ctx})
            ]

    def start(self):
        self.spread(0, 0)

    def next_step(self, stream, step):
        self.arrive(stream, step - 1)
        self.spread(stream, step)

    def other(self):
        self.cross()
        self.arrive("ctx")
        if self.after is not None:
            self.after.cross()
        self.spread(1, 0)

    def core(self):
        last = len(self.order) - 1
        for stream in range(self.ctx_size):
            self.arrive(stream, last)
        both = self.block * self.ctx_size
        copies = []
        for entry in subsets(self.order):
            place = self.whole.at[rows_of(flip_all(self.me, entry), both)]
            copies.append(self.link.push(place, place, {"fsdp": flip(self.me, 0)}))
        self.waits["core",] = copies

    def finish(self):
        self.arrive("core")

    def events(self):
        found = [self.start]
        for step in range(1, len(self.order)):
            found.append(functools.partial(self.next_step, 0, step))
        if self.ctx_size > 1:
            found.append(self.other)
            for step in range(1, len(self.order)):
                found.append(functools.partial(self.next_step, 1, step))
        return found + [self.core, self.finish]


def in_step(first, second):
    def run(one, two):
        one()
        two()

    return [functools.partial(run, one, two) for one, two in zip(first, second)]


class Total:
    def __init__(self, link, fsdp_size, ctx_size, held, arrived):
        self.link, self.held, self.arrived = link, held, arrived
        me, ctx = lax.axis_index("fsdp"), lax.axis_index("ctx")
        self.partners = [{"fsdp": flip(me, bit)} for bit in range(fsdp_size.bit_length() - 1)]
        if ctx_size > 1:
            self.partners.append({"ctx": 1 - ctx})

    def step(self, at):
        if at > 0:
            self.copy.wait_recv()
            self.held[at] = self.held[at - 1] + self.arrived[at - 1]
        if at < len(self.partners):
            self.copy = self.link.push(self.held.at[at], self.arrived.at[at], self.partners[at])

    def events(self):
        return [functools.partial(self.step, at) for at in range(len(self.partners) + 1)]


def dot_nn(left, right):
    return lax.dot_general(left, right, (((1,), (0,)), ((), ())), preferred_element_type=F32)


def dot_nt(left, right):
    return lax.dot_general(left, right, (((1,), (1,)), ((), ())), preferred_element_type=F32)


def dot_tn(left, right):
    return lax.dot_general(left, right, (((0,), (0,)), ((), ())), preferred_element_type=F32)


TILE = 256
ROOT_HALF = 0.7071067811865476
ROOT_TWO_PI = 2.5066282746310002
VECTORS, BIASES, SMALL_ROWS, RESULTS = 6, 3, 16, 6
PACE, SCATTER_PACE = 1.25, 1.25
FP = ((3, 2, 2, 2, 1, 1, 3), (3, 3, 3, 1, 0, 0, 3), (3, 1, 4, 2, 1, 1, 3))
BP = ((0, 1, 1, 1, 1, 1, 2, 2, 0, 0), (2, 1, 1, 1, 1, 2, 2, 1, 1, 2), (0, 0, 1, 0, 0, 0, 0, 1, 1, 1))
GAIN_A, SHIFT_A, OUT_B, GAIN_B, SHIFT_B, DOWN_B, QV_B, UP_B = range(8)


def lanes(at, count):
    return pl.ds(pl.multiple_of(at * count, count), count)


def standardized(values):
    centered = values - jnp.mean(values, axis=-1, keepdims=True)
    scale = lax.rsqrt(jnp.mean(centered * centered, axis=-1, keepdims=True) + EPS)
    return centered * scale, scale


def send_pieces(link, partial, sent, got, pieces, partner):
    copies = []
    for at in range(pieces):
        sent[at] = partial(at).astype(BF16)
        copies.append(link.push(sent.at[at], got.at[at], partner))
    return copies


def both_halves(copies, sent, got):
    found = []
    for at, copy in enumerate(copies):
        copy.wait_recv()
        found.append(sent[at].astype(F32) + got[at].astype(F32))
    return jnp.concatenate(found, axis=1)


class Stream:
    def __init__(self):
        self.waiting, self.count, self.done = [], 0, set()

    def release(self, group, events, begin, pace=1):
        for place, event in enumerate(events):
            self.waiting.append((begin + place * pace, self.count, group, event))
            self.count += 1
        self.waiting.sort(key=lambda entry: entry[:2])
        self.last = {entry[2]: entry for entry in self.waiting}

    def __call__(self, count):
        for entry in self.waiting[:count]:
            entry[3]()
            if self.last[entry[2]] is entry:
                self.done.add(entry[2])
        self.waiting = self.waiting[count:]

    def need(self, group):
        while group not in self.done:
            self(1)

    def rest(self):
        self(len(self.waiting))


def forward_kernel(ctx_size, fsdp_size, *refs):
    token_ref, mask_ref, live_ref = refs[:3]
    own_vectors = refs[3 : 3 + VECTORS]
    qv_ref, up_bias_ref, qkv_ref, out_weight_ref, up_ref, down_ref = refs[3 + VECTORS : 9 + VECTORS]
    out_ref, vector_ref = refs[9 + VECTORS : 11 + VECTORS]
    kept_out = refs[11 + VECTORS : 16 + VECTORS]
    (
        kv_out,
        pre_out,
        whole_ref,
        stream_ref,
        query_ref,
        log_total_ref,
        attended_ref,
        mid_ref,
        held,
        pre_ref,
        normed,
        hidden,
        kv,
        sent,
        got,
        small_held,
        small_got,
        send_sem,
        recv_sem,
        save_sem,
        kv_sem,
        pre_sem,
        kept_sem,
    ) = refs[16 + VECTORS :]
    kept = (stream_ref, query_ref, log_total_ref, attended_ref, mid_ref)
    layers, rows, width = stream_ref.shape
    cols = query_ref.shape[2]
    pieces = width // TILE
    pairs = PARTS // 2
    ctx = lax.axis_index("ctx")
    across = {"tp": 1 - lax.axis_index("tp")}
    greet(fsdp_size, ctx_size, True)
    link = Link(send_sem, recv_sem)
    pump = Stream()
    both = orders(fsdp_size)
    block = up_ref.shape[1]
    me = lax.axis_index("fsdp") * ctx_size + ctx
    here = rows_of(me, block)
    for layer in range(layers):
        for at in range(3):
            place = slice(at % 2 * cols, (at % 2 + 1) * cols)
            held[layer, at // 2, here, place] = qkv_ref[layer, at]
        held[layer, 1, here, cols:] = out_weight_ref[layer]
        for half in range(2):
            columns = slice(half * width, (half + 1) * width)
            held[layer, 2 + half, here, :] = up_ref[layer, :, columns]
            held[layer, 4 + half, here, :] = down_ref[layer, :, columns]
    shift = lax.broadcasted_iota(jnp.int32, (block, width), 0) + me * block
    shift = (shift == lax.broadcasted_iota(jnp.int32, (block, width), 1)).astype(BF16)
    placed = [dot_nn(vector[...], shift) for vector in own_vectors]
    unused = small_held.shape[1] - VECTORS * layers
    placed.append(jnp.zeros((unused, width), F32))
    small_held[0] = jnp.concatenate(placed, axis=0).astype(BF16)
    total = Total(link, fsdp_size, ctx_size, small_held, small_got)
    gathers, previous, keeps, saves, pre_saves, groups = (), (), {}, [], {}, 0
    for layer in range(layers):
        for pair in range(pairs):
            found = [
                Gather(
                    link,
                    ctx_size,
                    held.at[layer, part],
                    block,
                    both[part % 2],
                )
                for part in (2 * pair, 2 * pair + 1)
            ]
            for gather, before in zip(found, previous):
                before.after = gather
            previous = found
            if not gathers:
                gathers = found

            def keep(layer=layer, pair=pair):
                for part in (2 * pair, 2 * pair + 1):
                    copy = pltpu.make_async_copy(
                        held.at[layer, part], whole_ref.at[layer, part], save_sem.at[layer, part]
                    )
                    copy.start()
                    saves.append(copy)

            events = in_step(*[gather.events() for gather in found])
            pump.release((layer, pair), events, PACE * groups)
            keeps[layer, pair] = keep
            groups += 1

    def need(layer, pair):
        pump.need((layer, pair))
        keeps[layer, pair]()

    total.step(0)
    for gather in gathers:
        gather.cross()
    for at in range(1, len(total.partners) + 1):
        pump(1)
        total.step(at)
    vector_ref[...] = small_held[len(total.partners)].astype(F32)
    mask = mask_ref[...]
    stream_ref[0] = mask * token_ref[...].astype(F32)
    mine = rows_of(ctx, rows)
    pair_cols = 2 * HEAD_DIM
    lane = lax.broadcasted_iota(jnp.int32, (rows, pair_cols), 1)
    first = lane < HEAD_DIM
    live = live_ref[...] > 0
    log_total_ref[...] = jnp.zeros_like(log_total_ref)

    for layer in range(layers):
        def vector(which):
            at = which * layers + layer
            return vector_ref[at : at + 1, :]

        normal, _ = standardized(stream_ref[layer])
        normed[...] = (normal * vector(GAIN_A) + vector(SHIFT_A)).astype(BF16)
        need(layer, 0)

        @pl.loop(0, cols // TILE)
        def _(at):
            rows_in = normed[...]
            kv[layer, mine, lanes(at, TILE)] = dot_nn(
                rows_in, held[layer, 0, :, lanes(at + cols // TILE, TILE)]
            ).astype(BF16)
            kv[layer, mine, lanes(at + cols // TILE, TILE)] = (
                dot_nn(rows_in, held[layer, 1, :, lanes(at, TILE)])
                + qv_ref[layer, 1:2, lanes(at, TILE)].astype(F32)
            ).astype(BF16)

        kv_copy = None
        if ctx_size > 1:
            kv_copy = link.push(kv.at[layer, mine], kv.at[layer, mine], {"ctx": 1 - ctx})

        @pl.loop(0, cols // TILE)
        def _(at):
            query_ref[layer, :, lanes(at, TILE)] = (
                dot_nn(normed[...], held[layer, 0, :, lanes(at, TILE)]) + qv_ref[layer, 0:1, lanes(at, TILE)].astype(F32)
            ).astype(BF16)

        pump(FP[layer][0])
        if kv_copy is not None:
            kv_copy.wait_recv()
        save = pltpu.make_async_copy(kv.at[layer], kv_out.at[layer], kv_sem.at[layer])
        save.start()
        saves.append(save)

        for half in range(2):
            per_half = cols // pair_cols // 2

            @pl.loop(half * per_half, (half + 1) * per_half)
            def _(at):
                queries = query_ref[layer, :, lanes(at, pair_cols)]
                keys = kv[layer, :, lanes(at, pair_cols)]
                values = kv[layer, :, lanes(at + cols // pair_cols, pair_cols)]
                found = []
                for head in range(2):
                    chosen = jnp.where(
                        first if head == 0 else ~first, queries, jnp.zeros_like(queries)
                    )
                    scores = jnp.where(live, dot_nt(chosen, keys) * HEAD_DIM**-0.5, NEG)
                    top = jnp.max(scores, axis=-1, keepdims=True)
                    weights = jnp.exp(scores - top)
                    summed = jnp.sum(weights, axis=-1, keepdims=True)
                    log_total_ref[layer] = jnp.where(
                        lane == 2 * at + head, top + jnp.log(summed), log_total_ref[layer]
                    )
                    found.append(dot_nn((weights * (1.0 / summed)).astype(BF16), values))
                attended_ref[layer, :, lanes(at, pair_cols)] = jnp.where(
                    first, found[0], found[1]
                ).astype(BF16)

            pump(FP[layer][1 + half])

        def out_partial(at):
            return dot_nt(attended_ref[layer], held[layer, 1, at * TILE : (at + 1) * TILE, cols:])

        copies = send_pieces(link, out_partial, sent.at[layer, 0], got.at[0], pieces, across)
        pump(FP[layer][3])
        branch = both_halves(copies, sent.at[layer, 0], got.at[0])
        mid = stream_ref[layer] + mask * (branch + vector(OUT_B))
        mid_ref[layer] = mid
        normal, _ = standardized(mid)
        normed[...] = (normal * vector(GAIN_B) + vector(SHIFT_B)).astype(BF16)
        need(layer, 1)
        if layer >= 2:
            pre_saves.pop(layer - 2).wait()
        for part in range(2):

            @pl.loop(0, pieces)
            def _(at):
                pre = dot_nn(normed[...], held[layer, 2 + part, :, lanes(at, TILE)]) + up_bias_ref[
                    layer : layer + 1, lanes(at + part * pieces, TILE)
                ].astype(F32)
                pre_ref[layer % 2, part, :, lanes(at, TILE)] = pre
                hidden[part, :, lanes(at, TILE)] = (
                    0.5 * pre * (1.0 + lax.erf(pre * ROOT_HALF))
                ).astype(BF16)

            pump(FP[layer][4 + part])
        pre_saves[layer] = pltpu.make_async_copy(
            pre_ref.at[layer % 2], pre_out.at[layer], pre_sem.at[layer]
        )
        pre_saves[layer].start()
        need(layer, 2)

        def down_partial(at):
            here = slice(at * TILE, (at + 1) * TILE)
            return dot_nt(hidden[0], held[layer, 4, here, :]) + dot_nt(
                hidden[1], held[layer, 5, here, :]
            )

        copies = send_pieces(link, down_partial, sent.at[layer, 1], got.at[1], pieces, across)
        pump(FP[layer][6])
        branch = both_halves(copies, sent.at[layer, 1], got.at[1])
        for at, held_here in enumerate(kept):
            save = pltpu.make_async_copy(
                held_here.at[layer], kept_out[at].at[layer], kept_sem.at[layer, at]
            )
            save.start()
            saves.append(save)
        after = mid_ref[layer] + mask * (branch + vector(DOWN_B))
        if layer + 1 < layers:
            stream_ref[layer + 1] = after
        else:
            out_ref[...] = after.astype(BF16)
    pump.rest()
    link.drain()
    for save in (*saves, *pre_saves.values()):
        save.wait()


def forward_all(mesh, tokens, mask, live, own_vectors, qv_bias, up_bias, qkv, out_t, up, down_t):
    fsdp_size, ctx_size = mesh.shape["fsdp"], mesh.shape["ctx"]
    rows, width = tokens.shape
    layers, _, _, cols = qkv.shape
    part_cols = 2 * cols
    small = (-(-VECTORS * layers // 16) * 16, width)
    slots_all = rows * ctx_size
    pieces = width // TILE
    steps = fsdp_size.bit_length() - 1 + (ctx_size > 1)
    shape = jax.ShapeDtypeStruct
    whole = (layers, PARTS, width, part_cols)
    kept = [
        shape((layers, rows, width), F32),
        shape((layers, rows, cols), BF16),
        shape((layers, rows, 2 * HEAD_DIM), F32),
        shape((layers, rows, cols), BF16),
        shape((layers, rows, width), F32),
    ]
    out_shape = [
        shape((rows, width), BF16),
        shape(small, F32),
        *kept,
        shape((layers, slots_all, 2 * cols), BF16),
        shape((layers, 2, rows, width), F32),
        shape(whole, BF16),
    ]
    vmem = pl.BlockSpec(memory_space=pltpu.VMEM)
    any_space = pl.BlockSpec(memory_space=pl.ANY)
    pushes = (
        layers * ((ctx_size > 1) + 2 * pieces + gather_pushes(fsdp_size, ctx_size) * PARTS)
        + steps
    )
    return pl.pallas_call(
        functools.partial(forward_kernel, ctx_size, fsdp_size),
        out_shape=out_shape,
        in_specs=[vmem] * (9 + VECTORS),
        out_specs=[vmem] * 2 + [any_space] * 8,
        scratch_shapes=[pltpu.VMEM(one.shape, one.dtype) for one in kept]
        + [
            pltpu.VMEM(whole, BF16),
            pltpu.VMEM((2, 2, rows, width), F32),
            pltpu.VMEM((rows, width), BF16),
            pltpu.VMEM((2, rows, width), BF16),
            pltpu.VMEM((layers, slots_all, 2 * cols), BF16),
            pltpu.VMEM((layers, 2, pieces, rows, TILE), BF16),
            pltpu.VMEM((2, pieces, rows, TILE), BF16),
            pltpu.VMEM((steps + 1,) + small, BF16),
            pltpu.VMEM((steps,) + small, BF16),
            pltpu.SemaphoreType.DMA((pushes,)),
            pltpu.SemaphoreType.DMA((pushes,)),
            pltpu.SemaphoreType.DMA((layers, PARTS)),
            pltpu.SemaphoreType.DMA((layers,)),
            pltpu.SemaphoreType.DMA((layers,)),
            pltpu.SemaphoreType.DMA((layers, len(kept))),
        ],
        compiler_params=pltpu.CompilerParams(
            collective_id=0, has_side_effects=True, vmem_limit_bytes=63 * 2**20
        ),
        name="forward_all",
    )(tokens, mask, live, *own_vectors, qv_bias, up_bias, qkv, out_t, up, down_t)


class Scatter:
    def __init__(self, link, ctx_size, terms, arrived, last, order, credits, first, final, write):
        self.link, self.terms, self.arrived, self.last = link, terms, arrived, last
        self.ctx_size, self.order, self.write = ctx_size, order, write
        self.credits, self.first, self.final = credits, first, final
        self.me, self.ctx = lax.axis_index("fsdp"), lax.axis_index("ctx")
        self.slots = 2 ** len(order)
        self.both = terms.shape[0] // (2 * self.slots)
        self.flips = [
            [bit for at, bit in enumerate(order) if (slot >> (len(order) - 1 - at)) % 2 == 1]
            for slot in range(self.slots)
        ]
        self.base, self.sent = 0, []

    def place(self, slot, core=0):
        start = flip(self.me, 0) if core else self.me
        return rows_of(flip_all(start, self.flips[slot]), self.both)

    def send(self, step, pieces, to):
        if not self.first:
            pl.semaphore_wait(self.credits.at[step], 1)
        self.copies = [self.link.push(src, dst, to) for src, dst in pieces]
        self.sent += self.copies

    def read(self, step, to):
        if not self.final:
            pl.semaphore_signal(
                self.credits.at[step], inc=1, device_id=to, device_id_type=MESH
            )

    def start(self):
        self.send(
            0,
            [
                (self.terms.at[self.place(slot, 1)], self.arrived.at[slot])
                for slot in range(self.slots)
            ],
            {"fsdp": flip(self.me, 0)},
        )

    def take(self, step, count, to):
        for copy in self.copies:
            copy.wait_recv()
        for slot in range(count):
            here = self.place(slot)
            self.terms[here, :] = self.terms[here, :] + self.arrived[self.base + slot]
        self.base += count
        self.read(step, to)

    def step(self, at):
        count = self.slots >> at
        self.take(at, count, {"fsdp": flip(self.me, 0 if at == 0 else self.order[at - 1])})
        half = count // 2
        self.send(
            at + 1,
            [
                (self.terms.at[self.place(half + slot)], self.arrived.at[self.base + slot])
                for slot in range(half)
            ],
            {"fsdp": flip(self.me, self.order[at])},
        )

    def across(self):
        steps = len(self.order)
        self.take(steps, 1, {"fsdp": flip(self.me, self.order[-1])})
        if self.ctx_size > 1:
            block = self.both // self.ctx_size
            theirs = rows_of(self.me * self.ctx_size + 1 - self.ctx, block)
            self.send(steps + 1, [(self.terms.at[theirs], self.last)], {"ctx": 1 - self.ctx})

    def finish(self):
        block = self.both // self.ctx_size
        total = self.terms[rows_of(self.me * self.ctx_size + self.ctx, block), :].astype(F32)
        if self.ctx_size > 1:
            for copy in self.copies:
                copy.wait_recv()
            total = total + self.last[...].astype(F32)
            self.read(len(self.order) + 1, {"ctx": 1 - self.ctx})
        self.write(total)
        self.link.settle(self.sent)

    def events(self):
        found = [self.start]
        for at in range(len(self.order)):
            found.append(functools.partial(self.step, at))
        return found + [self.across, self.finish]


def norm_pull(normal, scale, gain, grad):
    grad_gain = jnp.sum(grad * normal, axis=0, keepdims=True)
    grad_shift = jnp.sum(grad, axis=0, keepdims=True)
    inner = grad * gain
    along = jnp.mean(inner * normal, axis=-1, keepdims=True)
    grad_in = scale * (inner - jnp.mean(inner, axis=-1, keepdims=True) - normal * along)
    return grad_in, grad_gain, grad_shift


def backward_kernel(ctx_size, fsdp_size, *refs):
    (
        cotangent_ref,
        mask_ref,
        live_ref,
        vector_ref,
        stream_all,
        query_all,
        log_total_all,
        attended_all,
        mid_all,
        kv_all,
        pre_all,
        whole_ref,
        out_ref,
        qkv_ref,
        out_weight_ref,
        up_ref,
        down_ref,
        small_ref,
        stream_ref,
        query_ref,
        log_total_ref,
        attended_ref,
        mid_ref,
        kv_ref,
        pre_ref,
        held,
        terms,
        arrived,
        last,
        turned,
        low,
        low_pre,
        hidden,
        grad_att,
        grad_qk,
        grad_kv,
        kv_sent,
        kv_got,
        sent,
        got,
        small_held,
        small_got,
        send_sem,
        recv_sem,
        load_sem,
        pre_sem,
        kept_sem,
        credits,
    ) = refs
    layers, rows, width = stream_ref.shape
    cols = query_ref.shape[2]
    pieces = width // TILE
    pairs = PARTS // 2
    ctx = lax.axis_index("ctx")
    across = {"tp": 1 - lax.axis_index("tp")}
    loads = {}

    def bring(layer, parts):
        if layer >= 0:
            for part in parts:
                copy = pltpu.make_async_copy(
                    whole_ref.at[layer, part], held.at[part], load_sem.at[part]
                )
                copy.start()
                loads[layer, part] = copy

    def bring_pre(layer):
        if layer >= 0:
            copy = pltpu.make_async_copy(
                pre_all.at[layer], pre_ref.at[layer % 2], pre_sem.at[layer % 2]
            )
            copy.start()
            loads[layer, "pre"] = copy

    kept = {
        "mid": (mid_all, mid_ref),
        "query": (query_all, query_ref),
        "kv": (kv_all, kv_ref),
        "log_total": (log_total_all, log_total_ref),
        "attended": (attended_all, attended_ref),
        "stream": (stream_all, stream_ref),
    }

    def ready(layer, *names):
        for name in names:
            loads[layer, name].wait()

    bring_pre(layers - 1)
    bring(layers - 1, (4, 5))

    def bring_kept():
        for layer in reversed(range(layers)):
            for at, (name, (source, target)) in enumerate(kept.items()):
                copy = pltpu.make_async_copy(
                    source.at[layer], target.at[layer], kept_sem.at[layer, at]
                )
                copy.start()
                loads[layer, name] = copy

    small_held[...] = jnp.zeros_like(small_held)
    greet(fsdp_size, ctx_size, True)
    link = Link(send_sem, recv_sem)
    pump = Stream()
    both = [order[::-1] for order in orders(fsdp_size)]
    mask = mask_ref[...]
    pair_cols = 2 * HEAD_DIM
    lane = lax.broadcasted_iota(jnp.int32, (rows, pair_cols), 1)
    first = lane < HEAD_DIM
    live = live_ref[...] > 0
    mine, theirs = rows_of(ctx, rows), rows_of(1 - ctx, rows)
    groups = 0
    last_sent = {}

    def scatter(layer, pair):
        nonlocal groups

        def writer(part):
            def write(value):
                if part == 0:
                    qkv_ref[layer, 0] = value[:, :cols]
                    qkv_ref[layer, 1] = value[:, cols:]
                elif part == 1:
                    qkv_ref[layer, 2] = value[:, :cols]
                    out_weight_ref[layer] = value[:, cols:]
                else:
                    target = up_ref if part < 4 else down_ref
                    target[layer, :, part % 2 * width : (part % 2 + 1) * width] = value

            return write

        events = in_step(
            *[
                Scatter(
                    link,
                    ctx_size,
                    terms.at[part],
                    arrived.at[part],
                    last.at[part],
                    both[part % 2],
                    credits.at[part],
                    layer == layers - 1,
                    layer == 0,
                    writer(part),
                ).events()
                for part in (2 * pair, 2 * pair + 1)
            ]
        )
        events[0]()
        pump.release((layer, pair), events[1:], SCATTER_PACE * groups)
        groups += 1

    def free(layer, pair):
        if layer < layers - 1:
            pump.need((layer + 1, pair))

    def product(part, start, count, right):
        @pl.loop(0, count)
        def _(at):
            terms[part, :, lanes(at + start, TILE)] = dot_nn(turned[...], right(at)).astype(BF16)

    def up_products(layer, vector):
        normal, _ = standardized(mid_ref[layer])
        turned[...] = jnp.transpose(
            (normal * vector(GAIN_B) + vector(SHIFT_B)).astype(BF16)
        )
        free(layer, 1)
        for part in range(2):
            product(2 + part, 0, pieces, lambda at, part=part: low_pre[part, :, lanes(at, TILE)])
        scatter(layer, 1)

    out_ref[...] = cotangent_ref[...].astype(F32)
    for layer in reversed(range(layers)):
        rows_small = small_held.at[layer, 0]

        def vector(which):
            at = which * layers + layer
            return vector_ref[at : at + 1, :]

        def keep_row(which, value):
            rows_small[which : which + 1, :] = value

        bring_pre(layer - 1)
        grad = out_ref[...]
        masked = mask * grad
        keep_row(DOWN_B, jnp.sum(masked, axis=0, keepdims=True))
        low[...] = masked.astype(BF16)
        turned[...] = jnp.transpose(low[...])
        loads[layer, "pre"].wait()
        for part in range(2):
            loads[layer, 4 + part].wait()

            @pl.loop(0, pieces)
            def _(at):
                pre = pre_ref[layer % 2, part, :, lanes(at, TILE)]
                chance = 0.5 * (1.0 + lax.erf(pre * ROOT_HALF))
                hidden[part, :, lanes(at, TILE)] = (pre * chance).astype(BF16)
                slope = chance + pre * (jnp.exp(-0.5 * pre * pre) * (1.0 / ROOT_TWO_PI))
                grad_pre = dot_nn(low[...], held[4 + part, :, lanes(at, TILE)]) * slope
                rows_small[UP_B + part : UP_B + part + 1, lanes(at, TILE)] = jnp.sum(
                    grad_pre, axis=0, keepdims=True
                )
                low_pre[part, :, lanes(at, TILE)] = grad_pre.astype(BF16)

            if layer == layers - 1:
                if part == 0:
                    bring(layer, (2, 3))
                else:
                    bring(layer, (1, 0))
                    bring_kept()
            pump(BP[layer][part])
        bring(layer - 1, (4, 5))
        for part in (2, 3):
            loads[layer, part].wait()

        def up_partial(at):
            here = slice(at * TILE, (at + 1) * TILE)
            return dot_nt(low_pre[0], held[2, here, :]) + dot_nt(low_pre[1], held[3, here, :])

        if layer < layers - 1:
            link.settle(last_sent["up"])
        copies = send_pieces(link, up_partial, sent.at[0], got.at[0], pieces, across)
        last_sent["up"] = copies
        bring(layer - 1, (2, 3))
        free(layer, 2)
        for part in range(2):
            product(4 + part, 0, pieces, lambda at, part=part: hidden[part, :, lanes(at, TILE)])
        scatter(layer, 2)
        ready(layer, "mid")
        if layer == layers - 1:
            up_products(layer, vector)
        pump(BP[layer][2])
        grad_normed = both_halves(copies, sent.at[0], got.at[0])
        normal, scale = standardized(mid_ref[layer])
        grad_in, grad_gain, grad_shift = norm_pull(normal, scale, vector(GAIN_B), grad_normed)
        keep_row(GAIN_B, grad_gain)
        keep_row(SHIFT_B, grad_shift)
        grad_mid = out_ref[...] + grad_in
        out_ref[...] = grad_mid
        masked = mask * grad_mid
        keep_row(OUT_B, jnp.sum(masked, axis=0, keepdims=True))
        low[...] = masked.astype(BF16)
        loads[layer, 1].wait()

        @pl.loop(0, cols // TILE)
        def _(at):
            grad_att[:, lanes(at, TILE)] = dot_nn(
                low[...], held[1, :, lanes(at + cols // TILE, TILE)]
            ).astype(BF16)

        pump(BP[layer][3])
        ready(layer, "query", "kv", "log_total")
        for half in range(2):
            per_half = cols // pair_cols // 2

            @pl.loop(half * per_half, (half + 1) * per_half)
            def _(at):
                queries = query_ref[layer, :, lanes(at, pair_cols)]
                grads = grad_att[:, lanes(at, pair_cols)]
                keys = kv_ref[layer, :, lanes(at, pair_cols)]
                values = kv_ref[layer, :, lanes(at + cols // pair_cols, pair_cols)]
                found, key_grad, value_grad = [], None, None
                for head in range(2):
                    here = first if head == 0 else ~first
                    query = jnp.where(here, queries, jnp.zeros_like(queries))
                    one_grad = jnp.where(here, grads, jnp.zeros_like(grads))
                    scores = jnp.where(live, dot_nt(query, keys) * HEAD_DIM**-0.5, NEG)
                    log_total = jnp.sum(
                        jnp.where(lane == 2 * at + head, log_total_ref[layer], 0.0),
                        axis=-1,
                        keepdims=True,
                    )
                    weights = jnp.exp(scores - log_total)
                    grad_weights = dot_nt(one_grad, values)
                    along = jnp.sum(weights * grad_weights, axis=-1, keepdims=True)
                    grad_scores = (weights * (grad_weights - along)).astype(BF16)
                    found.append(dot_nn(grad_scores, keys))
                    one = dot_tn(grad_scores, query)
                    two = dot_tn(weights.astype(BF16), one_grad)
                    key_grad = one if head == 0 else key_grad + one
                    value_grad = two if head == 0 else value_grad + two
                grad_qk[:, lanes(at, pair_cols)] = (
                    jnp.where(first, found[0], found[1]) * HEAD_DIM**-0.5
                ).astype(BF16)
                grad_kv[:, lanes(at, pair_cols)] = key_grad * HEAD_DIM**-0.5
                grad_kv[:, lanes(at + cols // pair_cols, pair_cols)] = value_grad

            pump(BP[layer][4 + half])
        kv_copy = None
        if ctx_size > 1:
            if layer < layers - 1:
                link.settle([last_sent["kv"]])
            kv_sent[...] = grad_kv[theirs, :].astype(BF16)
            kv_copy = link.push(kv_sent, kv_got.at[layer], {"ctx": 1 - ctx})
            last_sent["kv"] = kv_copy
        pump(BP[layer][6])
        if layer < layers - 1:
            up_products(layer, vector)
        pump(BP[layer][7])
        total_kv = grad_kv[mine, :]
        if kv_copy is not None:
            kv_copy.wait_recv()
            total_kv = total_kv + kv_got[layer].astype(F32)
        grad_qk[:, cols:] = total_kv.astype(BF16)
        rows_small[QV_B : QV_B + 1, :cols] = jnp.sum(
            grad_qk[:, :cols].astype(F32), axis=0, keepdims=True
        )
        rows_small[QV_B : QV_B + 1, cols:] = jnp.sum(
            grad_qk[:, 2 * cols :].astype(F32), axis=0, keepdims=True
        )
        loads[layer, 0].wait()

        def in_partial(at):
            here = slice(at * TILE, (at + 1) * TILE)
            return dot_nt(grad_qk[:, : 2 * cols], held[0, here, :]) + dot_nt(
                grad_qk[:, 2 * cols :], held[1, here, :cols]
            )

        if layer < layers - 1:
            link.settle(last_sent["in"])
        copies = send_pieces(link, in_partial, sent.at[1], got.at[1], pieces, across)
        last_sent["in"] = copies
        bring(layer - 1, (1, 0))
        pump(BP[layer][8])
        ready(layer, "attended", "stream")
        free(layer, 0)
        turned[...] = jnp.transpose(low[...])
        product(1, cols // TILE, cols // TILE, lambda at: attended_ref[layer, :, lanes(at, TILE)])
        normal, scale = standardized(stream_ref[layer])
        turned[...] = jnp.transpose(
            (normal * vector(GAIN_A) + vector(SHIFT_A)).astype(BF16)
        )
        product(0, 0, 2 * cols // TILE, lambda at: grad_qk[:, lanes(at, TILE)])
        product(1, 0, cols // TILE, lambda at: grad_qk[:, lanes(at + 2 * cols // TILE, TILE)])
        scatter(layer, 0)
        pump(BP[layer][9])
        grad_normed = both_halves(copies, sent.at[1], got.at[1])
        normal, scale = standardized(stream_ref[layer])
        grad_in, grad_gain, grad_shift = norm_pull(normal, scale, vector(GAIN_A), grad_normed)
        keep_row(GAIN_A, grad_gain)
        keep_row(SHIFT_A, grad_shift)
        grad = out_ref[...] + grad_in
        out_ref[...] = grad if layer > 0 else mask * grad
        total = Total(link, fsdp_size, ctx_size, small_held.at[layer], small_got.at[layer])
        pump.release(("small", layer), total.events(), SCATTER_PACE * (groups - 1))
    pump.rest()
    for layer in range(layers):
        for row in range(VECTORS + BIASES):
            at = row * layers + layer
            small_ref[at : at + 1, :] = small_held[
                layer, small_held.shape[1] - 1, row : row + 1, :
            ]
    link.drain()


def backward_all(mesh, cotangent, mask, live, vectors, kept, whole):
    fsdp_size, ctx_size = mesh.shape["fsdp"], mesh.shape["ctx"]
    rows, width = cotangent.shape
    layers, _, _, part_cols = whole.shape
    cols = width // mesh.shape["tp"]
    slots_all = rows * ctx_size
    pieces = width // TILE
    slots = fsdp_size // 2
    both = width // fsdp_size
    block = both // ctx_size
    bits = fsdp_size.bit_length() - 1
    steps = bits + (ctx_size > 1)
    shape = jax.ShapeDtypeStruct
    vmem = pl.BlockSpec(memory_space=pltpu.VMEM)
    any_space = pl.BlockSpec(memory_space=pl.ANY)
    operands = [cotangent, mask, live, vectors, *kept, whole]
    pushes = layers * ((ctx_size > 1) + 2 * pieces + PARTS * (2 * slots) + steps)
    return pl.pallas_call(
        functools.partial(backward_kernel, ctx_size, fsdp_size),
        out_shape=[
            shape((rows, width), F32),
            shape((layers, 3, block, cols), F32),
            shape((layers, block, cols), F32),
            shape((layers, block, 2 * width), F32),
            shape((layers, block, 2 * width), F32),
            shape((-(-(VECTORS + BIASES) * layers // 8) * 8, width), F32),
        ],
        in_specs=[vmem] * 4 + [any_space] * (len(operands) - 4),
        out_specs=[vmem] * 6,
        scratch_shapes=[pltpu.VMEM(one.shape, one.dtype) for one in kept[:6]]
        + [
            pltpu.VMEM((2, 2, rows, width), F32),
            pltpu.VMEM(whole.shape[1:], BF16),
            pltpu.VMEM(whole.shape[1:], BF16),
            pltpu.VMEM((PARTS, 2 * slots - 1, both, part_cols), BF16),
            pltpu.VMEM((PARTS, block, part_cols), BF16),
            pltpu.VMEM((width, rows), BF16),
            pltpu.VMEM((rows, width), BF16),
            pltpu.VMEM((2, rows, width), BF16),
            pltpu.VMEM((2, rows, width), BF16),
            pltpu.VMEM((rows, cols), BF16),
            pltpu.VMEM((rows, 3 * cols), BF16),
            pltpu.VMEM((slots_all, 2 * cols), F32),
            pltpu.VMEM((rows, 2 * cols), BF16),
            pltpu.VMEM((layers, rows, 2 * cols), BF16),
            pltpu.VMEM((2, pieces, rows, TILE), BF16),
            pltpu.VMEM((2, pieces, rows, TILE), BF16),
            pltpu.VMEM((layers, steps + 1, SMALL_ROWS, width), F32),
            pltpu.VMEM((layers, steps, SMALL_ROWS, width), F32),
            pltpu.SemaphoreType.DMA((pushes,)),
            pltpu.SemaphoreType.DMA((pushes,)),
            pltpu.SemaphoreType.DMA((PARTS,)),
            pltpu.SemaphoreType.DMA((2,)),
            pltpu.SemaphoreType.DMA((layers, 6)),
            pltpu.SemaphoreType.REGULAR((PARTS, steps + 1)),
        ],
        compiler_params=pltpu.CompilerParams(
            collective_id=1, has_side_effects=True, vmem_limit_bytes=63 * 2**20
        ),
        name="backward_all",
    )(*operands)


def finish_kernel(ctx_size, layers, *refs):
    count = RESULTS
    sources, small_ref = refs[:count], refs[count]
    targets = refs[count + 1 : 2 * count + 1]
    vectors = refs[2 * count + 1 : 2 * count + 1 + VECTORS]
    qv_ref, up_bias_ref = refs[2 * count + 1 + VECTORS : 2 * count + 3 + VECTORS]
    rooms = refs[2 * count + 3 + VECTORS : 3 * count + 3 + VECTORS]
    in_sem, out_sem = refs[3 * count + 3 + VECTORS :]
    brings = [
        pltpu.make_async_copy(source, room, in_sem.at[at])
        for at, (source, room) in enumerate(zip(sources, rooms))
    ]
    for copy in brings:
        copy.start()
    width = small_ref.shape[1]
    block = vectors[0].shape[1]
    here = (lax.axis_index("fsdp") * ctx_size + lax.axis_index("ctx")) * block
    turned = pltpu.roll(small_ref[...], (width - here) % width, 1)
    for at, vector in enumerate(vectors):
        vector[...] = turned[at * layers : (at + 1) * layers, :block]
    cols = qv_ref.shape[2]
    for layer in range(layers):
        row = QV_B * layers + layer
        for half in range(2):
            qv_ref[layer, half : half + 1, :] = small_ref[
                row : row + 1, half * cols : (half + 1) * cols
            ]
    for half in range(up_bias_ref.shape[1] // width):
        row = (UP_B + half) * layers
        up_bias_ref[:, half * width : (half + 1) * width] = small_ref[row : row + layers, :]
    sends = []
    for at, copy in enumerate(brings):
        copy.wait()
        send = pltpu.make_async_copy(rooms[at], targets[at], out_sem.at[at])
        send.start()
        sends.append(send)
    for send in sends:
        send.wait()


def finish(mesh, results, small, layers, block, units):
    width = small.shape[1]
    shape = jax.ShapeDtypeStruct
    vmem = pl.BlockSpec(memory_space=pltpu.VMEM)
    any_space = pl.BlockSpec(memory_space=pl.ANY)
    return pl.pallas_call(
        functools.partial(finish_kernel, mesh.shape["ctx"], layers),
        out_shape=[shape(one.shape, one.dtype) for one in results]
        + [shape((layers, block), F32)] * VECTORS
        + [shape((layers, 2, width // mesh.shape["tp"]), F32), shape((layers, units), F32)],
        in_specs=[any_space] * RESULTS + [vmem],
        out_specs=[any_space] * RESULTS + [vmem] * (VECTORS + 2),
        scratch_shapes=[pltpu.VMEM(one.shape, one.dtype) for one in results]
        + [pltpu.SemaphoreType.DMA((RESULTS,)), pltpu.SemaphoreType.DMA((RESULTS,))],
        compiler_params=pltpu.CompilerParams(vmem_limit_bytes=63 * 2**20),
        name="finish",
    )(*results, small)


def body(
    mesh,
    tokens,
    lengths,
    cotangent,
    attn_gain,
    attn_shift,
    qkv_weight,
    qv_bias,
    out_weight,
    out_bias,
    mlp_gain,
    mlp_shift,
    up_weight,
    up_bias,
    down_weight,
    down_bias,
):
    images, local_slots, width = tokens.shape
    ctx_size = mesh.shape["ctx"]
    rows_here, slots_all = images * local_slots, local_slots * ctx_size
    layers, block, _, cols = qkv_weight.shape
    units = up_weight.shape[2]
    slot_ids = lax.axis_index("ctx") * local_slots + jnp.arange(local_slots, dtype=jnp.int32)
    mask = (slot_ids[None, :] < lengths[:, None]).astype(F32).reshape(rows_here, 1)
    live = (jnp.arange(slots_all, dtype=jnp.int32)[None, :] < lengths[:, None]).astype(F32)
    own_vectors = (attn_gain, attn_shift, out_bias, mlp_gain, mlp_shift, down_bias)
    output, vectors, *kept, whole = forward_all(
        mesh,
        tokens.reshape(rows_here, width),
        mask,
        live,
        own_vectors,
        qv_bias,
        up_bias,
        jnp.swapaxes(qkv_weight, 1, 2),
        jnp.swapaxes(out_weight, 1, 2),
        up_weight,
        jnp.swapaxes(down_weight, 1, 2),
    )
    *results, little = backward_all(
        mesh, cotangent.reshape(rows_here, width), mask, live, vectors, kept, whole
    )
    results = finish(mesh, [output, *results], little, layers, block, units)
    output, input_grad, grad_qkv, grad_out, grad_up, grad_down = results[:RESULTS]
    own = results[RESULTS : RESULTS + VECTORS]
    grad_qv, grad_up_bias = results[RESULTS + VECTORS :]
    return (
        output.reshape(tokens.shape),
        input_grad.reshape(tokens.shape),
        own[GAIN_A],
        own[SHIFT_A],
        jnp.swapaxes(grad_qkv, 1, 2),
        grad_qv,
        jnp.swapaxes(grad_out, 1, 2),
        own[OUT_B],
        own[GAIN_B],
        own[SHIFT_B],
        grad_up,
        grad_up_bias,
        jnp.swapaxes(grad_down, 1, 2),
        own[DOWN_B],
    )


def solution(mesh):
    place = P(None, ("fsdp", "ctx"))
    rows = P("fsdp", "ctx", None)
    return jax.shard_map(
        functools.partial(body, mesh),
        mesh=mesh,
        in_specs=(
            rows,
            P("fsdp"),
            rows,
            place,
            place,
            P(None, ("fsdp", "ctx"), None, "tp"),
            P(None, None, "tp"),
            P(None, "tp", ("fsdp", "ctx")),
            place,
            place,
            place,
            P(None, ("fsdp", "ctx"), "tp"),
            P(None, "tp"),
            P(None, "tp", ("fsdp", "ctx")),
            place,
        ),
        out_specs=(
            rows,
            rows,
            place,
            place,
            P(None, ("fsdp", "ctx"), None, "tp"),
            P(None, None, "tp"),
            P(None, "tp", ("fsdp", "ctx")),
            place,
            place,
            place,
            P(None, ("fsdp", "ctx"), "tp"),
            P(None, "tp"),
            P(None, "tp", ("fsdp", "ctx")),
            place,
        ),
        check_vma=False,
    )
```
